32 devices in a mesh: ta: 2 (over y), gz: 4 (over x, core), xy: 4 (over z).
Axes of the slice: x: 2, y: 2, z: 4, core: 2. Of those that a mesh axis runs over, the one named last changes fastest.
Arguments:
- right_side: float32 [2, 4, 4, 2, 32, 128], P('ta', 'gz', 'xy'), may hold values from -40 to 40
- stencil: float32 [2, 4, 4, 2, 9, 128, 128], P('ta', 'gz', 'xy'), may hold values from -0.5 to 1.5, as said below
- restrict: float32 [2, 4, 4, 2, 32, 128], P('ta', 'gz', 'xy'), may hold values from -0.5 to 0.5
- aggregate: int32 [2, 4, 4, 2], P('ta', 'gz', 'xy'), may hold values from 0 to 3, as said below
- coarsest_inverse: float32 [128, 128], P('xy'), may hold values from -0.5 to 0.5
Outputs:
- solution: float32 [2, 4, 4, 2, 32, 128], P('ta', 'gz', 'xy')
- residual: float32 [2, 4, 4, 2, 32, 128], P('ta', 'gz', 'xy')
The draws below stay inside these ranges and needn't reach their ends.
Inputs may be any that keep to these rules, and one draw needn't show every extreme that they name: `aggregate`: sites are grouped into 2 x 2 x 2 x 2 blocks aligned at even coordinates; each block forms one coarsest site, and the coarsest sites are numbered in an order drawn from the seed. `stencil`: each self block is close to the identity; the other blocks are small and full.
All inputs are finite; a program needn't handle non-finite values.
Results may differ from the reference program's by a relative error of at most 0.0001.
Values sent between devices are 32-bit elements; how exact they have to be, the bound alone decides.
A program may use at most 64 MiB of HBM per device.

```python
import jax
import jax.numpy as jnp
from jax import lax

C = 128
K3 = 32
NRHS = 32
X_LOC = 2
NT = 2
NZ = 4
NY = 4
NS = 64
NA = 4
NC3 = 128


def draw_stencil(key, part):
    noise_key = jax.random.fold_in(key, 11)
    shape = (NT, NZ, NY, X_LOC, 9, C, C)
    noise = jnp.clip(jax.random.normal(noise_key, shape, jnp.float32), -4.0, 4.0)
    noise = noise * (0.3 / C ** 0.5)
    rows = lax.broadcasted_iota(jnp.int32, shape, 5)
    cols = lax.broadcasted_iota(jnp.int32, shape, 6)
    blocks = lax.broadcasted_iota(jnp.int32, shape, 4)
    ident = jnp.where((rows == cols) & (blocks == 0), 1.0, 0.0).astype(jnp.float32)
    return (ident + noise).astype(jnp.float32)


def draw_right_side(key, part):
    base_key = jax.random.fold_in(key, 21)
    scale_key = jax.random.fold_in(key, 22)
    shape = (NT, NZ, NY, X_LOC, NRHS, C)
    values = jnp.clip(jax.random.normal(base_key, shape, jnp.float32), -4.0, 4.0)
    small = (NT, NZ, NY, X_LOC, NRHS, 1)
    tpos = lax.broadcasted_iota(jnp.int32, small, 0)
    zpos = lax.broadcasted_iota(jnp.int32, small, 1)
    ypos = lax.broadcasted_iota(jnp.int32, small, 2)
    xpos = lax.broadcasted_iota(jnp.int32, small, 3)
    flat = ((tpos * NZ + zpos) * NY + ypos) * X_LOC + xpos
    rising = jnp.exp(jnp.log(3.0) * flat.astype(jnp.float32) / (NS - 1))
    spread = jax.random.uniform(scale_key, small, jnp.float32, -0.5, 0.5)
    return (values * rising * jnp.exp(jnp.log(10.0) * spread)).astype(jnp.float32)


def draw_aggregate(key, part):
    perm_key = jax.random.fold_in(key, 31)
    labels = jax.random.permutation(perm_key, NA).astype(jnp.int32)
    shape = (NT, NZ, NY, X_LOC)
    tpos = lax.broadcasted_iota(jnp.int32, shape, 0) // 2
    zpos = lax.broadcasted_iota(jnp.int32, shape, 1) // 2
    ypos = lax.broadcasted_iota(jnp.int32, shape, 2) // 2
    xpos = lax.broadcasted_iota(jnp.int32, shape, 3) // 2
    block = ((tpos * (NZ // 2) + zpos) * (NY // 2) + ypos) * (X_LOC // 2) + xpos
    return labels[block].astype(jnp.int32)


def shard_levels(key, shape, pieces, least, high):
    level, own = 1.0, jax.random.fold_in(key, 6)
    for dim, shards_of in pieces:
        heights = jnp.exp(jax.random.uniform(jax.random.fold_in(own, dim), (shards_of,), jnp.float32, least / len(pieces), high / len(pieces)))
        level = level * jnp.repeat(heights, shape[dim] // shards_of).reshape([-1 if axis == dim else 1 for axis in range(len(shape))])
    return level


def gaussian(key, shape, scale, bound, cuts=(), kind=jnp.bfloat16):
    drawn = scale * jax.random.normal(key, shape, jnp.float32)
    if cuts:
        drawn = drawn * shard_levels(key, shape, cuts, -0.22, 0.18)
    return jnp.clip(drawn, -bound, bound).astype(kind)


def setup_inputs(seed: int = 0) -> dict:
    key_list = jax.random.split(jax.random.key(seed), 6)
    right_side = draw_right_side(jax.random.fold_in(key_list[5], 71), 0)
    stencil = draw_stencil(jax.random.fold_in(key_list[5], 71), 0)
    restrict = gaussian(key_list[2], (NT, NZ, NY, X_LOC, K3, C), C ** -0.5, 0.5, ((0, 2), (1, 4), (2, 4)), jnp.float32)
    aggregate = draw_aggregate(jax.random.fold_in(key_list[5], 71), 0)
    coarsest_inverse = gaussian(key_list[4], (NC3, NC3), NC3 ** -0.5, 0.5, ((0, 4),), jnp.float32)
    return {"right_side": right_side, "stencil": stencil, "restrict": restrict, "aggregate": aggregate, "coarsest_inverse": coarsest_inverse}


def apply_operator(field, stencil):
    shifted = [field,
               jnp.roll(field, -1, 0), jnp.roll(field, 1, 0),
               jnp.roll(field, -1, 1), jnp.roll(field, 1, 1),
               jnp.roll(field, -1, 2), jnp.roll(field, 1, 2),
               jnp.roll(field, -1, 3), jnp.roll(field, 1, 3)]
    result = jnp.zeros(field.shape, jnp.float32)
    for offset in range(9):
        result = result + jnp.einsum("tzyxij,tzyxrj->tzyxri", stencil[:, :, :, :, offset], shifted[offset],
                                     precision=lax.Precision.HIGHEST)
    return result


def inner_sum(one_side, other_side):
    return jnp.sum(one_side * other_side, axis=(0, 1, 2, 3, 5))


def reference(right_side, stencil, restrict, aggregate, coarsest_inverse):
    image_first = apply_operator(right_side, stencil)
    step_first = inner_sum(image_first, right_side) / inner_sum(image_first, image_first)
    resid_mid = right_side - step_first[:, None] * image_first
    image_raw = apply_operator(resid_mid, stencil)
    beta = inner_sum(image_first, image_raw) / inner_sum(image_first, image_first)
    image_second = image_raw - beta[:, None] * image_first
    direction = resid_mid - beta[:, None] * right_side
    step_second = inner_sum(image_second, resid_mid) / inner_sum(image_second, image_second)
    solution_gcr = step_first[:, None] * right_side + step_second[:, None] * direction
    residual = resid_mid - step_second[:, None] * image_second
    restricted = jnp.einsum("tzyxkc,tzyxrc->tzyxrk", restrict, residual, precision=lax.Precision.HIGHEST)
    sites_all = NS
    restricted = restricted.reshape(sites_all, NRHS, K3)
    onehot = (aggregate.reshape(sites_all)[:, None] == jnp.arange(NA, dtype=jnp.int32)[None, :]).astype(jnp.float32)
    coarse_rhs = jnp.einsum("sa,srk->akr", onehot, restricted, precision=lax.Precision.HIGHEST).reshape(NC3, NRHS)
    correction = jnp.dot(coarsest_inverse, coarse_rhs, precision=lax.Precision.HIGHEST,
                         preferred_element_type=jnp.float32).reshape(NA, K3, NRHS)
    per_site = jnp.einsum("sa,akr->skr", onehot, correction, precision=lax.Precision.HIGHEST)
    vectors = restrict.reshape(sites_all, K3, C)
    lifted = jnp.einsum("skc,skr->src", vectors, per_site, precision=lax.Precision.HIGHEST)
    solution = solution_gcr + lifted.reshape(solution_gcr.shape)
    return solution, residual
```

```python
import functools
import itertools

import jax
import jax.numpy as jnp
from jax import lax
from jax.experimental import pallas as pl
from jax.experimental.pallas import tpu as pltpu
from jax.sharding import PartitionSpec as P

AXES = ("ta", "gz", "xy")
F32 = jnp.float32
BF16 = jnp.bfloat16
MESH = pl.DeviceIdType.MESH


def split(x):
    high = x.astype(BF16)
    return high, (x - high.astype(F32)).astype(BF16)


def dot_nt(a, b):
    return lax.dot_general(a, b, (((1,), (1,)), ((), ())), preferred_element_type=F32)


def dot_nn(a, b):
    return lax.dot_general(a, b, (((1,), (0,)), ((), ())), preferred_element_type=F32)


def stack_split(x):
    return jnp.concatenate(split(x), axis=0)


def fold(o):
    r, n = o.shape[0] // 2, o.shape[1] // 2
    return o[:r, :n] + (o[:r, n:] + o[r:, :n])


def loop(n, step, init, most=8):
    if n <= most:
        for i in range(n):
            init = step(i, init)
        return init
    return lax.fori_loop(0, n, step, init)


def kernel(
    sizes, agg_ref, b_ref, sten_ref, res_ref, inv_ref, sol_ref, resid_ref,
    sten, sw, rp, halo1, halo2, w1, w2, inv, lab, wr, near, far,
    sten_sem, h1s, h1r, h2s, h2r, ivs, ivr, lbs, lbr, nrs, nrr, frs, frr,
):
    xs, nrhs, comps = b_ref.shape
    k3 = res_ref.shape[1]
    na, _, nc3 = inv.shape
    per = inv_ref.shape[0]
    groups = far.shape[0]
    me = tuple(lax.axis_index(a) for a in AXES)

    def at(offset):
        return {a: lax.rem(i + o, n) for a, i, o, n in zip(AXES, me, offset, sizes)}

    def across(bits):
        return {a: (i + 1 - 2 * lax.rem(i, 2)) if f else i for a, i, f in zip(AXES, me, bits)}

    def line(axis, o):
        return tuple(o if a == axis else 0 for a in range(3))

    halo_sends = []
    for a in range(3):
        halo_sends.append((2 * a, line(a, sizes[a] - 1)))
        if sizes[a] > 2:
            halo_sends.append((2 * a + 1, line(a, 1)))
    near_sends = [bits for bits in itertools.product((0, 1), repeat=3) if any(bits)]
    far_sends = [
        tuple(2 * o for o in offs)
        for offs in itertools.product(*(range(n // 2) for n in sizes))
        if any(offs)
    ]
    inv_sends = [line(2, o) for o in range(1, sizes[2])]

    copies = [
        pltpu.make_async_copy(sten_ref.at[x], sten.at[x], sten_sem.at[x]) for x in range(xs)
    ]
    for c in copies:
        c.start()

    barrier = pltpu.get_barrier_semaphore()
    offsets = sorted({o for _, o in halo_sends} | set(far_sends) | set(inv_sends))
    diagonals = [bits for bits in near_sends if sum(bits) > 1]
    for device in [at(o) for o in offsets] + [across(f) for f in diagonals]:
        pl.semaphore_signal(barrier, inc=1, device_id=device, device_id_type=MESH)

    lab[0] = jnp.full(lab.shape[1:], agg_ref[0].astype(F32), F32)
    inv[pl.ds(me[2] * per, per)] = inv_ref[...]
    rp[...] = jnp.zeros_like(rp)
    for x in range(xs):
        high, low = split(res_ref[x])
        for f in range(3):
            cols = pl.ds((f * xs + x) * comps, comps)
            rp[pl.ds(f * k3, k3), cols] = high
            rp[pl.ds(comps + f * k3, k3), cols] = low

    pl.semaphore_wait(barrier, len(offsets) + len(diagonals))

    def remote(src, dst, send, recv, device):
        return pltpu.make_async_remote_copy(
            src_ref=src, dst_ref=dst, send_sem=send, recv_sem=recv,
            device_id=device, device_id_type=MESH,
        )

    def start_halo(src, halo, send, recv):
        out = [remote(src, halo.at[s], send.at[s], recv.at[s], at(o)) for s, o in halo_sends]
        for c in out:
            c.start()
        return out

    first = start_halo(b_ref, halo1, h1s, h1r)
    early = [
        remote(inv_ref, inv.at[pl.ds(me[2] * per, per)], ivs.at[i], ivr.at[i], at(o))
        for i, o in enumerate(inv_sends)
    ] + [
        remote(lab.at[0], lab.at[i + 1], lbs.at[i], lbr.at[i], at(o))
        for i, o in enumerate(far_sends)
    ]
    for c in early:
        c.start()

    for x in range(xs):
        copies[x].wait()
        for k in range(9):
            high, low = split(sten[x, k])
            cols = pl.ds(k * comps, comps)
            sw[x, pl.ds(0, comps), cols] = high
            sw[x, pl.ds(comps, comps), cols] = low

    def local_part(field):
        out = []
        for x in range(xs):
            ahead = jnp.concatenate([field[(x + 1) % xs], field[(x + xs - 1) % xs]], axis=1)
            out.append(
                fold(dot_nt(stack_split(field[x]), sw[x, :, pl.ds(0, comps)]))
                + fold(dot_nt(stack_split(ahead), sw[x, :, pl.ds(7 * comps, 2 * comps)]))
            )
        return out

    def halo_part(halo, base):
        out = []
        for x in range(xs):
            sides = []
            for a in range(3):
                sides.append(halo[2 * a, x])
                sides.append(halo[2 * a + (1 if sizes[a] > 2 else 0), x])
            lhs = stack_split(jnp.concatenate(sides, axis=1))
            out.append(base[x] + fold(dot_nt(lhs, sw[x, :, pl.ds(comps, 6 * comps)])))
        return out

    def restricted(field, f):
        lhs = jnp.concatenate(field, axis=1)
        cols = pl.ds(f * xs * comps, xs * comps)
        return fold(dot_nt(stack_split(lhs), rp[:, cols]))

    lane = lax.broadcasted_iota(jnp.int32, (nrhs, comps), 1)

    def product(u, v, i):
        total = sum(u[x] * v[x] for x in range(xs))
        total = jnp.sum(total, axis=1, keepdims=True)
        return jnp.where(lane == 3 * k3 + i, total, 0.0)

    bs = [b_ref[x] for x in range(xs)]
    base = local_part(bs)
    message = restricted(bs, 0)
    for c in first:
        c.wait_recv()
    w1s = halo_part(halo1, base)
    for x in range(xs):
        w1[x] = w1s[x]
    second = start_halo(w1, halo2, h2s, h2r)

    base = local_part(w1s)
    message = message + restricted(w1s, 1) + product(w1s, w1s, 0) + product(w1s, bs, 1)
    for c in early:
        c.wait_recv()

    own = inv[agg_ref[0]]
    own_high, own_low = split(own)
    rows = lax.broadcasted_iota(jnp.int32, (comps, nc3), 0)
    cols = lax.broadcasted_iota(jnp.int32, (comps, nc3), 1)
    same = (lax.rem(rows, k3) == lax.rem(cols, k3)) & (rows < 3 * k3)
    block = (cols // k3).astype(F32)
    vec_high, vec_low = split(jnp.concatenate([res_ref[x] for x in range(xs)], axis=1))

    def prepare(g, carry):
        label = lab[g][0:1, 0:1]
        pick = jnp.where(same & (block == label), 1.0, 0.0).astype(BF16)
        weights = dot_nt(pick, own_high) + dot_nt(pick, own_low)
        high, low = split(weights)
        lift = dot_nn(high, vec_high) + (dot_nn(high, vec_low) + dot_nn(low, vec_high))
        high, low = split(lift)
        width = xs * comps
        wr[g, :, pl.ds(0, width)] = high
        wr[g, :, pl.ds(width, width)] = low
        return carry

    loop(groups, prepare, 0)

    for c in second:
        c.wait_recv()
    w2s = halo_part(halo2, base)
    message = message + (
        restricted(w2s, 2)
        + (product(w1s, w2s, 2) + product(w2s, w2s, 3) + product(w2s, bs, 4))
    )
    near[0] = message
    third = [
        remote(near.at[0], near.at[i + 1], nrs.at[i], nrr.at[i], across(f))
        for i, f in enumerate(near_sends)
    ]
    for c in third:
        c.start()
    for x in range(xs):
        w2[x] = w2s[x]
    for c in third:
        c.wait_recv()
    total = message
    for i in range(len(near_sends)):
        total = total + near[i + 1]
    far[0] = total
    fourth = [
        remote(far.at[0], far.at[i + 1], frs.at[i], frr.at[i], at(o))
        for i, o in enumerate(far_sends)
    ]
    for c in fourth:
        c.start()
    for c in first + early + second + third:
        c.wait_send()
    for c in fourth:
        c.wait_recv()

    sums = loop(groups, lambda g, acc: acc + far[g], jnp.zeros((nrhs, comps), F32))
    square, cross, corr, square2, cross2 = (
        sums[:, 3 * k3 + i : 3 * k3 + i + 1] for i in range(5)
    )
    step = cross / square
    ratio = corr / square
    turn = (step * corr - cross2) / (square2 - ratio * corr)
    push = step + turn * ratio
    weight = jnp.where(
        lane < k3, 1.0, jnp.where(lane < 2 * k3, -push, jnp.where(lane < 3 * k3, turn, 0.0))
    )
    width = xs * comps

    def lift_step(g, acc):
        return acc + dot_nn(stack_split(far[g] * weight), wr[g])

    lifted = fold(loop(groups, lift_step, jnp.zeros((2 * nrhs, 2 * width), F32)))
    for x in range(xs):
        bx, ux, vx = b_ref[x], w1[x], w2[x]
        resid_ref[x] = bx - push * ux + turn * vx
        sol_ref[x] = (push * bx - turn * ux) + lifted[:, x * comps : (x + 1) * comps]
    for c in fourth:
        c.wait_send()


def body(sizes, right_side, stencil, restrict, aggregate, coarsest_inverse):
    shape = right_side.shape
    xs, nrhs, comps = shape[3:]
    k3 = restrict.shape[4]
    nc3 = coarsest_inverse.shape[1]
    na = nc3 // k3
    groups = (sizes[0] // 2) * (sizes[1] // 2) * (sizes[2] // 2)
    per = coarsest_inverse.shape[0] // k3
    vmem = pl.BlockSpec(memory_space=pltpu.VMEM)
    dma = pltpu.SemaphoreType.DMA
    field = jax.ShapeDtypeStruct((xs, nrhs, comps), F32)
    sol, resid = pl.pallas_call(
        functools.partial(kernel, sizes),
        out_shape=(field, field),
        in_specs=[
            pl.BlockSpec(memory_space=pltpu.SMEM),
            vmem,
            pl.BlockSpec(memory_space=pl.ANY),
            vmem,
            vmem,
        ],
        out_specs=(vmem, vmem),
        scratch_shapes=[
            pltpu.VMEM((xs, 9, comps, comps), F32),
            pltpu.VMEM((xs, 2 * comps, 9 * comps), BF16),
            pltpu.VMEM((2 * comps, 3 * xs * comps), BF16),
            pltpu.VMEM((6, xs, nrhs, comps), F32),
            pltpu.VMEM((6, xs, nrhs, comps), F32),
            pltpu.VMEM((xs, nrhs, comps), F32),
            pltpu.VMEM((xs, nrhs, comps), F32),
            pltpu.VMEM((na, k3, nc3), F32),
            pltpu.VMEM((groups, 8, comps), F32),
            pltpu.VMEM((groups, comps, 2 * xs * comps), BF16),
            pltpu.VMEM((8, nrhs, comps), F32),
            pltpu.VMEM((groups, nrhs, comps), F32),
            dma((xs,)),
            dma((6,)), dma((6,)), dma((6,)), dma((6,)),
            dma((sizes[2],)), dma((sizes[2],)),
            dma((groups,)), dma((groups,)),
            dma((7,)), dma((7,)),
            dma((groups,)), dma((groups,)),
        ],
        compiler_params=pltpu.CompilerParams(
            collective_id=0,
            has_side_effects=True,
            vmem_limit_bytes=(16 if groups <= 8 else 48) * 2**20,
        ),
    )(
        aggregate.reshape(xs),
        right_side.reshape(xs, nrhs, comps),
        stencil.reshape(xs, 9, comps, comps),
        restrict.reshape(xs, k3, comps),
        coarsest_inverse.reshape(per, k3, nc3),
    )
    return sol.reshape(shape), resid.reshape(shape)


def solution(mesh):
    sizes = tuple(mesh.shape[a] for a in AXES)
    return jax.shard_map(
        functools.partial(body, sizes),
        mesh=mesh,
        in_specs=(
            P("ta", "gz", "xy", None, None, None),
            P("ta", "gz", "xy", None, None, None, None),
            P("ta", "gz", "xy", None, None, None),
            P("ta", "gz", "xy", None),
            P("xy", None),
        ),
        out_specs=(P("ta", "gz", "xy", None, None, None), P("ta", "gz", "xy", None, None, None)),
        check_vma=False,
    )
```

```python
import functools
import itertools

import jax
import jax.numpy as jnp
from jax import lax
from jax.experimental import pallas as pl
from jax.experimental.pallas import tpu as pltpu
from jax.sharding import PartitionSpec as P

AXES = ("ta", "gz", "xy")
F32 = jnp.float32
BF16 = jnp.bfloat16
MESH = pl.DeviceIdType.MESH


def split(x):
    high = x.astype(BF16)
    return high, (x - high.astype(F32)).astype(BF16)


def dot_nt(a, b):
    return lax.dot_general(a, b, (((1,), (1,)), ((), ())), preferred_element_type=F32)


def dot_nn(a, b):
    return lax.dot_general(a, b, (((1,), (0,)), ((), ())), preferred_element_type=F32)


def stack_split(x):
    return jnp.concatenate(split(x), axis=0)


def fold(o):
    r, n = o.shape[0] // 2, o.shape[1] // 2
    return o[:r, :n] + (o[:r, n:] + o[r:, :n])


def loop(n, step, init, most=8):
    if n <= most:
        for i in range(n):
            init = step(i, init)
        return init
    return lax.fori_loop(0, n, step, init)


def kernel(
    sizes, agg_in, b_in, sten_in, res_in, inv_in, sol_ref, resid_ref,
    agg_ref, b_ref, res_ref, in_sem, sten, sw, rp, halo1, halo2, w1, w2, inv, lab, wr, near, far,
    sten_sem, h1s, h1r, h2s, h2r, ivs, ivr, lbs, lbr, nrs, nrr, frs, frr,
):
    xs, nrhs, comps = b_ref.shape
    k3 = res_ref.shape[1]
    na, _, nc3 = inv.shape
    per = inv_in.shape[0]
    groups = far.shape[0]
    me = tuple(lax.axis_index(a) for a in AXES)

    def at(offset):
        return {a: lax.rem(i + o, n) for a, i, o, n in zip(AXES, me, offset, sizes)}

    def across(bits):
        return {a: (i + 1 - 2 * lax.rem(i, 2)) if f else i for a, i, f in zip(AXES, me, bits)}

    def line(axis, o):
        return tuple(o if a == axis else 0 for a in range(3))

    halo_sends = []
    for a in range(3):
        halo_sends.append((2 * a, line(a, sizes[a] - 1)))
        if sizes[a] > 2:
            halo_sends.append((2 * a + 1, line(a, 1)))
    near_sends = [bits for bits in itertools.product((0, 1), repeat=3) if any(bits)]
    far_sends = [
        tuple(2 * o for o in offs)
        for offs in itertools.product(*(range(n // 2) for n in sizes))
        if any(offs)
    ]
    inv_sends = [line(2, o) for o in range(1, sizes[2])]

    mine = inv.at[pl.ds(me[2] * per, per)]
    loads = [
        pltpu.make_async_copy(src, dst, in_sem.at[i])
        for i, (src, dst) in enumerate(
            ((b_in, b_ref), (agg_in, agg_ref), (res_in, res_ref), (inv_in, mine))
        )
    ]
    copies = [
        pltpu.make_async_copy(sten_in.at[x], sten.at[x], sten_sem.at[x]) for x in range(xs)
    ]
    for c in loads + copies:
        c.start()

    barrier = pltpu.get_barrier_semaphore()
    offsets = sorted({o for _, o in halo_sends} | set(far_sends) | set(inv_sends))
    diagonals = [bits for bits in near_sends if sum(bits) > 1]
    for device in [at(o) for o in offsets] + [across(f) for f in diagonals]:
        pl.semaphore_signal(barrier, inc=1, device_id=device, device_id_type=MESH)

    rp[...] = jnp.zeros_like(rp)
    for c in loads:
        c.wait()
    lab[0] = jnp.full(lab.shape[1:], agg_ref[0].astype(F32), F32)
    for x in range(xs):
        high, low = split(res_ref[x])
        for f in range(3):
            cols = pl.ds((f * xs + x) * comps, comps)
            rp[pl.ds(f * k3, k3), cols] = high
            rp[pl.ds(comps + f * k3, k3), cols] = low

    pl.semaphore_wait(barrier, len(offsets) + len(diagonals))

    def remote(src, dst, send, recv, device):
        return pltpu.make_async_remote_copy(
            src_ref=src, dst_ref=dst, send_sem=send, recv_sem=recv,
            device_id=device, device_id_type=MESH,
        )

    def start_halo(src, halo, send, recv):
        out = [remote(src, halo.at[s], send.at[s], recv.at[s], at(o)) for s, o in halo_sends]
        for c in out:
            c.start()
        return out

    first = start_halo(b_ref, halo1, h1s, h1r)
    early = [
        remote(mine, mine, ivs.at[i], ivr.at[i], at(o))
        for i, o in enumerate(inv_sends)
    ] + [
        remote(lab.at[0], lab.at[i + 1], lbs.at[i], lbr.at[i], at(o))
        for i, o in enumerate(far_sends)
    ]
    for c in early:
        c.start()

    for x in range(xs):
        copies[x].wait()
        for k in range(9):
            high, low = split(sten[x, k])
            cols = pl.ds(k * comps, comps)
            sw[x, pl.ds(0, comps), cols] = high
            sw[x, pl.ds(comps, comps), cols] = low

    def local_part(field):
        out = []
        for x in range(xs):
            ahead = jnp.concatenate([field[(x + 1) % xs], field[(x + xs - 1) % xs]], axis=1)
            out.append(
                fold(dot_nt(stack_split(field[x]), sw[x, :, pl.ds(0, comps)]))
                + fold(dot_nt(stack_split(ahead), sw[x, :, pl.ds(7 * comps, 2 * comps)]))
            )
        return out

    def halo_part(halo, base):
        out = []
        for x in range(xs):
            sides = []
            for a in range(3):
                sides.append(halo[2 * a, x])
                sides.append(halo[2 * a + (1 if sizes[a] > 2 else 0), x])
            lhs = stack_split(jnp.concatenate(sides, axis=1))
            out.append(base[x] + fold(dot_nt(lhs, sw[x, :, pl.ds(comps, 6 * comps)])))
        return out

    def restricted(field, f):
        lhs = jnp.concatenate(field, axis=1)
        cols = pl.ds(f * xs * comps, xs * comps)
        return fold(dot_nt(stack_split(lhs), rp[:, cols]))

    lane = lax.broadcasted_iota(jnp.int32, (nrhs, comps), 1)

    def product(u, v, i):
        total = sum(u[x] * v[x] for x in range(xs))
        total = jnp.sum(total, axis=1, keepdims=True)
        return jnp.where(lane == 3 * k3 + i, total, 0.0)

    bs = [b_ref[x] for x in range(xs)]
    base = local_part(bs)
    message = restricted(bs, 0)
    for c in first:
        c.wait_recv()
    w1s = halo_part(halo1, base)
    for x in range(xs):
        w1[x] = w1s[x]
    second = start_halo(w1, halo2, h2s, h2r)

    base = local_part(w1s)
    message = message + restricted(w1s, 1) + product(w1s, w1s, 0) + product(w1s, bs, 1)
    for c in early:
        c.wait_recv()

    own = inv[agg_ref[0]]
    own_high, own_low = split(own)
    rows = lax.broadcasted_iota(jnp.int32, (comps, nc3), 0)
    cols = lax.broadcasted_iota(jnp.int32, (comps, nc3), 1)
    same = (lax.rem(rows, k3) == lax.rem(cols, k3)) & (rows < 3 * k3)
    block = (cols // k3).astype(F32)
    vec_high, vec_low = split(jnp.concatenate([res_ref[x] for x in range(xs)], axis=1))

    def prepare(g, carry):
        label = lab[g][0:1, 0:1]
        pick = jnp.where(same & (block == label), 1.0, 0.0).astype(BF16)
        weights = dot_nt(pick, own_high) + dot_nt(pick, own_low)
        high, low = split(weights)
        lift = dot_nn(high, vec_high) + (dot_nn(high, vec_low) + dot_nn(low, vec_high))
        high, low = split(lift)
        width = xs * comps
        wr[g, :, pl.ds(0, width)] = high
        wr[g, :, pl.ds(width, width)] = low
        return carry

    loop(groups, prepare, 0)

    for c in second:
        c.wait_recv()
    w2s = halo_part(halo2, base)
    message = message + (
        restricted(w2s, 2)
        + (product(w1s, w2s, 2) + product(w2s, w2s, 3) + product(w2s, bs, 4))
    )
    near[0] = message
    third = [
        remote(near.at[0], near.at[i + 1], nrs.at[i], nrr.at[i], across(f))
        for i, f in enumerate(near_sends)
    ]
    for c in third:
        c.start()
    for x in range(xs):
        w2[x] = w2s[x]
    for c in third:
        c.wait_recv()
    total = message
    for i in range(len(near_sends)):
        total = total + near[i + 1]
    far[0] = total
    fourth = [
        remote(far.at[0], far.at[i + 1], frs.at[i], frr.at[i], at(o))
        for i, o in enumerate(far_sends)
    ]
    for c in fourth:
        c.start()
    for c in first + early + second + third:
        c.wait_send()
    for c in fourth:
        c.wait_recv()

    sums = loop(groups, lambda g, acc: acc + far[g], jnp.zeros((nrhs, comps), F32))
    square, cross, corr, square2, cross2 = (
        sums[:, 3 * k3 + i : 3 * k3 + i + 1] for i in range(5)
    )
    step = cross / square
    ratio = corr / square
    turn = (step * corr - cross2) / (square2 - ratio * corr)
    push = step + turn * ratio
    weight = jnp.where(
        lane < k3, 1.0, jnp.where(lane < 2 * k3, -push, jnp.where(lane < 3 * k3, turn, 0.0))
    )
    width = xs * comps

    def lift_step(g, acc):
        return acc + dot_nn(stack_split(far[g] * weight), wr[g])

    lifted = fold(loop(groups, lift_step, jnp.zeros((2 * nrhs, 2 * width), F32)))
    for x in range(xs):
        bx, ux, vx = b_ref[x], w1[x], w2[x]
        resid_ref[x] = bx - push * ux + turn * vx
        sol_ref[x] = (push * bx - turn * ux) + lifted[:, x * comps : (x + 1) * comps]
    for c in fourth:
        c.wait_send()


def body(sizes, right_side, stencil, restrict, aggregate, coarsest_inverse):
    shape = right_side.shape
    xs, nrhs, comps = shape[3:]
    k3 = restrict.shape[4]
    nc3 = coarsest_inverse.shape[1]
    na = nc3 // k3
    groups = (sizes[0] // 2) * (sizes[1] // 2) * (sizes[2] // 2)
    per = coarsest_inverse.shape[0] // k3
    vmem = pl.BlockSpec(memory_space=pltpu.VMEM)
    dma = pltpu.SemaphoreType.DMA
    field = jax.ShapeDtypeStruct((xs, nrhs, comps), F32)
    sol, resid = pl.pallas_call(
        functools.partial(kernel, sizes),
        out_shape=(field, field),
        in_specs=[pl.BlockSpec(memory_space=pltpu.HBM)] * 5,
        out_specs=(vmem, vmem),
        scratch_shapes=[
            pltpu.SMEM((xs,), jnp.int32),
            pltpu.VMEM((xs, nrhs, comps), F32),
            pltpu.VMEM((xs, k3, comps), F32),
            dma((4,)),
            pltpu.VMEM((xs, 9, comps, comps), F32),
            pltpu.VMEM((xs, 2 * comps, 9 * comps), BF16),
            pltpu.VMEM((2 * comps, 3 * xs * comps), BF16),
            pltpu.VMEM((6, xs, nrhs, comps), F32),
            pltpu.VMEM((6, xs, nrhs, comps), F32),
            pltpu.VMEM((xs, nrhs, comps), F32),
            pltpu.VMEM((xs, nrhs, comps), F32),
            pltpu.VMEM((na, k3, nc3), F32),
            pltpu.VMEM((groups, 8, comps), F32),
            pltpu.VMEM((groups, comps, 2 * xs * comps), BF16),
            pltpu.VMEM((8, nrhs, comps), F32),
            pltpu.VMEM((groups, nrhs, comps), F32),
            dma((xs,)),
            dma((6,)), dma((6,)), dma((6,)), dma((6,)),
            dma((sizes[2],)), dma((sizes[2],)),
            dma((groups,)), dma((groups,)),
            dma((7,)), dma((7,)),
            dma((groups,)), dma((groups,)),
        ],
        compiler_params=pltpu.CompilerParams(
            collective_id=0,
            has_side_effects=True,
            vmem_limit_bytes=60 * 2**20,
        ),
    )(
        aggregate.reshape(xs),
        right_side.reshape(xs, nrhs, comps),
        stencil.reshape(xs, 9, comps, comps),
        restrict.reshape(xs, k3, comps),
        coarsest_inverse.reshape(per, k3, nc3),
    )
    return sol.reshape(shape), resid.reshape(shape)


def solution(mesh):
    sizes = tuple(mesh.shape[a] for a in AXES)
    return jax.shard_map(
        functools.partial(body, sizes),
        mesh=mesh,
        in_specs=(
            P("ta", "gz", "xy", None, None, None),
            P("ta", "gz", "xy", None, None, None, None),
            P("ta", "gz", "xy", None, None, None),
            P("ta", "gz", "xy", None),
            P("xy", None),
        ),
        out_specs=(P("ta", "gz", "xy", None, None, None), P("ta", "gz", "xy", None, None, None)),
        check_vma=False,
    )
```

```python
import functools
import itertools

import jax
import jax.numpy as jnp
from jax import lax
from jax.experimental import pallas as pl
from jax.experimental.pallas import tpu as pltpu
from jax.sharding import PartitionSpec as P

AXES = ("ta", "gz", "xy")
F32 = jnp.float32
BF16 = jnp.bfloat16
MESH = pl.DeviceIdType.MESH


def split(x):
    high = x.astype(BF16)
    return high, (x - high.astype(F32)).astype(BF16)


def dot_nt(a, b):
    return lax.dot_general(a, b, (((1,), (1,)), ((), ())), preferred_element_type=F32)


def dot_nn(a, b):
    return lax.dot_general(a, b, (((1,), (0,)), ((), ())), preferred_element_type=F32)


def stack_split(x):
    return jnp.concatenate(split(x), axis=0)


def fold(o):
    r, n = o.shape[0] // 2, o.shape[1] // 2
    return o[:r, :n] + (o[:r, n:] + o[r:, :n])


def loop(n, step, init, most=8):
    if n <= most:
        for i in range(n):
            init = step(i, init)
        return init
    return lax.fori_loop(0, n, step, init)


def kernel(
    sizes, agg_in, b_in, sten_in, res_in, inv_in, sol_ref, resid_ref,
    agg_ref, b_ref, res_ref, in_sem, sten, sw, rp, halo1, halo2, w1, w2, inv, lab, wr, near_e, far_e, near_l, far_l,
    sten_sem, h1s, h1r, h2s, h2r, ivs, ivr, lbs, lbr, nes, ner, fes, fer, nls, nlr, fls, flr,
):
    xs, nrhs, comps = b_ref.shape
    k3 = res_ref.shape[1]
    na, _, nc3 = inv.shape
    per = inv_in.shape[0]
    groups = far_e.shape[0]
    packs = comps // k3
    part = nrhs // packs
    width = xs * comps
    me = tuple(lax.axis_index(a) for a in AXES)

    def at(offset):
        return {a: lax.rem(i + o, n) for a, i, o, n in zip(AXES, me, offset, sizes)}

    def across(bits):
        return {a: (i + 1 - 2 * lax.rem(i, 2)) if f else i for a, i, f in zip(AXES, me, bits)}

    def line(axis, o):
        return tuple(o if a == axis else 0 for a in range(3))

    halo_sends = []
    for a in range(3):
        halo_sends.append((2 * a, line(a, sizes[a] - 1)))
        if sizes[a] > 2:
            halo_sends.append((2 * a + 1, line(a, 1)))
    near_sends = [bits for bits in itertools.product((0, 1), repeat=3) if any(bits)]
    far_sends = [
        tuple(2 * o for o in offs)
        for offs in itertools.product(*(range(n // 2) for n in sizes))
        if any(offs)
    ]
    inv_sends = [line(2, o) for o in range(1, sizes[2])]

    mine = inv.at[pl.ds(me[2] * per, per)]
    loads = [
        pltpu.make_async_copy(src, dst, in_sem.at[i])
        for i, (src, dst) in enumerate(
            ((b_in, b_ref), (agg_in, agg_ref), (res_in, res_ref), (inv_in, mine))
        )
    ]
    copies = [
        pltpu.make_async_copy(sten_in.at[x], sten.at[x], sten_sem.at[x]) for x in range(xs)
    ]
    for c in loads + copies:
        c.start()

    barrier = pltpu.get_barrier_semaphore()
    offsets = sorted({o for _, o in halo_sends} | set(far_sends) | set(inv_sends))
    diagonals = [bits for bits in near_sends if sum(bits) > 1]
    for device in [at(o) for o in offsets] + [across(f) for f in diagonals]:
        pl.semaphore_signal(barrier, inc=1, device_id=device, device_id_type=MESH)

    for c in loads:
        c.wait()
    lab[0] = jnp.full(lab.shape[1:], agg_ref[0].astype(F32), F32)
    for x in range(xs):
        high, low = split(jnp.concatenate([res_ref[x]] * packs, axis=0))
        rp[pl.ds(0, comps), pl.ds(x * comps, comps)] = high
        rp[pl.ds(comps, comps), pl.ds(x * comps, comps)] = low

    pl.semaphore_wait(barrier, len(offsets) + len(diagonals))

    def remote(src, dst, send, recv, device):
        return pltpu.make_async_remote_copy(
            src_ref=src, dst_ref=dst, send_sem=send, recv_sem=recv,
            device_id=device, device_id_type=MESH,
        )

    def start_halo(src, halo, send, recv):
        out = [remote(src, halo.at[s], send.at[s], recv.at[s], at(o)) for s, o in halo_sends]
        for c in out:
            c.start()
        return out

    first = start_halo(b_ref, halo1, h1s, h1r)
    early = [
        remote(mine, mine, ivs.at[i], ivr.at[i], at(o))
        for i, o in enumerate(inv_sends)
    ] + [
        remote(lab.at[0], lab.at[i + 1], lbs.at[i], lbr.at[i], at(o))
        for i, o in enumerate(far_sends)
    ]
    for c in early:
        c.start()

    for x in range(xs):
        copies[x].wait()
        for k in range(9):
            high, low = split(sten[x, k])
            cols = pl.ds(k * comps, comps)
            sw[x, pl.ds(0, comps), cols] = high
            sw[x, pl.ds(comps, comps), cols] = low

    def local_part(field):
        out = []
        for x in range(xs):
            ahead = jnp.concatenate([field[(x + 1) % xs], field[(x + xs - 1) % xs]], axis=1)
            out.append(
                fold(dot_nt(stack_split(field[x]), sw[x, :, pl.ds(0, comps)]))
                + fold(dot_nt(stack_split(ahead), sw[x, :, pl.ds(7 * comps, 2 * comps)]))
            )
        return out

    def halo_part(halo, base):
        out = []
        for x in range(xs):
            sides = []
            for a in range(3):
                sides.append(halo[2 * a, x])
                sides.append(halo[2 * a + (1 if sizes[a] > 2 else 0), x])
            lhs = stack_split(jnp.concatenate(sides, axis=1))
            out.append(base[x] + fold(dot_nt(lhs, sw[x, :, pl.ds(comps, 6 * comps)])))
        return out

    lane = lax.broadcasted_iota(jnp.int32, (part, comps), 1)
    slot = lane // k3
    place = lax.rem(lane, k3)

    def pack(full):
        out = full[:part]
        for q in range(1, packs):
            out = jnp.where(slot == q, full[q * part : (q + 1) * part], out)
        return out

    def restricted(field):
        return pack(fold(dot_nt(stack_split(jnp.concatenate(field, axis=1)), rp[...])))

    def product(u, v, i):
        total = sum(u[x] * v[x] for x in range(xs))
        total = jnp.sum(total, axis=1, keepdims=True)
        return jnp.where(place == i, pack(jnp.broadcast_to(total, (nrhs, comps))), 0.0)

    def to_near(near, send, recv):
        out = [
            remote(near.at[0], near.at[i + 1], send.at[i], recv.at[i], across(f))
            for i, f in enumerate(near_sends)
        ]
        for c in out:
            c.start()
        return out

    def to_far(near, far, send, recv):
        total = near[0]
        for i in range(len(near_sends)):
            total = total + near[i + 1]
        far[0] = total
        out = [
            remote(far.at[0], far.at[i + 1], send.at[i], recv.at[i], at(o))
            for i, o in enumerate(far_sends)
        ]
        for c in out:
            c.start()
        return out

    bs = [b_ref[x] for x in range(xs)]
    base = local_part(bs)
    near_e[0, pl.ds(0, part)] = restricted(bs)
    for c in first:
        c.wait_recv()
    w1s = halo_part(halo1, base)
    for x in range(xs):
        w1[x] = w1s[x]
    second = start_halo(w1, halo2, h2s, h2r)

    near_e[0, pl.ds(part, part)] = restricted(w1s)
    near_e[0, pl.ds(2 * part, part)] = product(w1s, w1s, 0) + product(w1s, bs, 1)
    third_e = to_near(near_e, nes, ner)
    base = local_part(w1s)
    for c in early:
        c.wait_recv()

    own = inv[agg_ref[0]]
    own_high, own_low = split(own)
    rows = lax.broadcasted_iota(jnp.int32, (comps, nc3), 0)
    cols = lax.broadcasted_iota(jnp.int32, (comps, nc3), 1)
    same = lax.rem(rows, k3) == lax.rem(cols, k3)
    block = (cols // k3).astype(F32)
    vec_high, vec_low = split(jnp.concatenate([res_ref[x] for x in range(xs)], axis=1))

    def prepare(g, carry):
        label = lab[g][0:1, 0:1]
        pick = jnp.where(same & (block == label), 1.0, 0.0).astype(BF16)
        weights = dot_nt(pick, own_high) + dot_nt(pick, own_low)
        high, low = split(weights)
        lift = dot_nn(high, vec_high) + (dot_nn(high, vec_low) + dot_nn(low, vec_high))
        high, low = split(lift)
        first_row = g * comps if isinstance(g, int) else pl.multiple_of(g * comps, comps)
        wr[pl.ds(first_row, comps), pl.ds(0, width)] = high
        wr[pl.ds(first_row, comps), pl.ds(width, width)] = low
        return carry

    loop(groups, prepare, 0)

    for c in second:
        c.wait_recv()
    w2s = halo_part(halo2, base)
    near_l[0, pl.ds(0, part)] = restricted(w2s)
    near_l[0, pl.ds(part, part)] = (
        product(w1s, w2s, 2) + product(w2s, w2s, 3) + product(w2s, bs, 4)
    )
    third_l = to_near(near_l, nls, nlr)
    for x in range(xs):
        w2[x] = w2s[x]
    for c in third_e:
        c.wait_recv()
    fourth_e = to_far(near_e, far_e, fes, fer)
    for c in third_l:
        c.wait_recv()
    fourth_l = to_far(near_l, far_l, fls, flr)
    for c in first + early + second + third_e + third_l:
        c.wait_send()
    for c in fourth_e + fourth_l:
        c.wait_recv()

    def add(g, acc):
        return acc + (far_e[g, pl.ds(2 * part, part)] + far_l[g, pl.ds(part, part)])

    square = loop(groups, add, jnp.zeros((part, comps), F32))
    cross, corr, square2, cross2 = (pltpu.roll(square, comps - i, 1) for i in range(1, 5))
    step = cross / square
    ratio = corr / square
    turn = (step * corr - cross2) / (square2 - ratio * corr)
    push = step + turn * ratio

    def spread(coef):
        return jnp.concatenate(
            [
                jnp.broadcast_to(coef[:, q * k3 : q * k3 + 1], (part, comps))
                for q in range(packs)
            ],
            axis=0,
        )

    push, turn = spread(push), spread(turn)
    push_packed, turn_packed = pack(push), pack(turn)

    def coarse(g):
        mixed = (
            far_e[g, pl.ds(0, part)]
            - push_packed * far_e[g, pl.ds(part, part)]
            + turn_packed * far_l[g, pl.ds(0, part)]
        )
        return jnp.concatenate([jnp.where(slot == q, mixed, 0.0) for q in range(packs)], axis=0)

    pair = 2 if groups % 2 == 0 else 1

    def lift_step(h, acc):
        lhs = jnp.concatenate([coarse(h * pair + j) for j in range(pair)], axis=1)
        rows = pair * comps
        first_row = h * rows if isinstance(h, int) else pl.multiple_of(h * rows, rows)
        return acc + dot_nn(stack_split(lhs), wr[pl.ds(first_row, rows), :])

    lifted = fold(loop(groups // pair, lift_step, jnp.zeros((2 * nrhs, 2 * width), F32)))
    for x in range(xs):
        bx, ux, vx = b_ref[x], w1[x], w2[x]
        resid_ref[x] = bx - push * ux + turn * vx
        sol_ref[x] = (push * bx - turn * ux) + lifted[:, x * comps : (x + 1) * comps]
    for c in fourth_e + fourth_l:
        c.wait_send()


def body(sizes, right_side, stencil, restrict, aggregate, coarsest_inverse):
    shape = right_side.shape
    xs, nrhs, comps = shape[3:]
    k3 = restrict.shape[4]
    nc3 = coarsest_inverse.shape[1]
    na = nc3 // k3
    groups = (sizes[0] // 2) * (sizes[1] // 2) * (sizes[2] // 2)
    per = coarsest_inverse.shape[0] // k3
    part = nrhs * k3 // comps
    vmem = pl.BlockSpec(memory_space=pltpu.VMEM)
    dma = pltpu.SemaphoreType.DMA
    field = jax.ShapeDtypeStruct((xs, nrhs, comps), F32)
    sol, resid = pl.pallas_call(
        functools.partial(kernel, sizes),
        out_shape=(field, field),
        in_specs=[pl.BlockSpec(memory_space=pltpu.HBM)] * 5,
        out_specs=(vmem, vmem),
        scratch_shapes=[
            pltpu.SMEM((xs,), jnp.int32),
            pltpu.VMEM((xs, nrhs, comps), F32),
            pltpu.VMEM((xs, k3, comps), F32),
            dma((4,)),
            pltpu.VMEM((xs, 9, comps, comps), F32),
            pltpu.VMEM((xs, 2 * comps, 9 * comps), BF16),
            pltpu.VMEM((2 * comps, xs * comps), BF16),
            pltpu.VMEM((6, xs, nrhs, comps), F32),
            pltpu.VMEM((6, xs, nrhs, comps), F32),
            pltpu.VMEM((xs, nrhs, comps), F32),
            pltpu.VMEM((xs, nrhs, comps), F32),
            pltpu.VMEM((na, k3, nc3), F32),
            pltpu.VMEM((groups, 8, comps), F32),
            pltpu.VMEM((groups * comps, 2 * xs * comps), BF16),
            pltpu.VMEM((8, 3 * part, comps), F32),
            pltpu.VMEM((groups, 3 * part, comps), F32),
            pltpu.VMEM((8, 2 * part, comps), F32),
            pltpu.VMEM((groups, 2 * part, comps), F32),
            dma((xs,)),
            dma((6,)), dma((6,)), dma((6,)), dma((6,)),
            dma((sizes[2],)), dma((sizes[2],)),
            dma((groups,)), dma((groups,)),
            dma((7,)), dma((7,)), dma((groups,)), dma((groups,)),
            dma((7,)), dma((7,)), dma((groups,)), dma((groups,)),
        ],
        compiler_params=pltpu.CompilerParams(
            collective_id=0,
            has_side_effects=True,
            vmem_limit_bytes=(16 if groups <= 8 else 48) * 2**20,
        ),
    )(
        *(
            pltpu.with_memory_space_constraint(a, pltpu.HBM)
            for a in (
                aggregate.reshape(xs),
                right_side.reshape(xs, nrhs, comps),
                stencil.reshape(xs, 9, comps, comps),
                restrict.reshape(xs, k3, comps),
                coarsest_inverse.reshape(per, k3, nc3),
            )
        )
    )
    return sol.reshape(shape), resid.reshape(shape)


def solution(mesh):
    sizes = tuple(mesh.shape[a] for a in AXES)
    return jax.shard_map(
        functools.partial(body, sizes),
        mesh=mesh,
        in_specs=(
            P("ta", "gz", "xy", None, None, None),
            P("ta", "gz", "xy", None, None, None, None),
            P("ta", "gz", "xy", None, None, None),
            P("ta", "gz", "xy", None),
            P("xy", None),
        ),
        out_specs=(P("ta", "gz", "xy", None, None, None), P("ta", "gz", "xy", None, None, None)),
        check_vma=False,
    )
```

```python
import functools
import itertools

import jax
import jax.numpy as jnp
from jax import lax
from jax.experimental import pallas as pl
from jax.experimental.pallas import tpu as pltpu
from jax.sharding import PartitionSpec as P

AXES = ("ta", "gz", "xy")
F32 = jnp.float32
BF16 = jnp.bfloat16
MESH = pl.DeviceIdType.MESH


def split(x):
    high = x.astype(BF16)
    return high, (x - high.astype(F32)).astype(BF16)


def dot_nt(a, b):
    return lax.dot_general(a, b, (((1,), (1,)), ((), ())), preferred_element_type=F32)


def dot_nn(a, b):
    return lax.dot_general(a, b, (((1,), (0,)), ((), ())), preferred_element_type=F32)


def stack_split(x):
    return jnp.concatenate(split(x), axis=0)


def fold(o):
    r, n = o.shape[0] // 2, o.shape[1] // 2
    return o[:r, :n] + (o[:r, n:] + o[r:, :n])


def loop(n, step, init, most=8):
    if n <= most:
        for i in range(n):
            init = step(i, init)
        return init
    return lax.fori_loop(0, n, step, init)


def kernel(
    sizes, agg_in, b_in, sten_in, res_in, inv_in, sol_ref, resid_ref,
    agg_ref, b_ref, res_ref, in_sem, sten, sw, rp, halo1, halo2, w1, w2, inv, lab, wr, near_e, far_e, near_l, far_l,
    sten_sem, h1s, h1r, h2s, h2r, ivs, ivr, lbs, lbr, nes, ner, fes, fer, nls, nlr, fls, flr,
):
    xs, nrhs, comps = b_ref.shape
    k3 = res_ref.shape[1]
    na, _, nc3 = inv.shape
    per = inv_in.shape[0]
    groups = far_e.shape[0]
    packs = comps // k3
    part = nrhs // packs
    width = xs * comps
    me = tuple(lax.axis_index(a) for a in AXES)

    def at(offset):
        return {a: lax.rem(i + o, n) for a, i, o, n in zip(AXES, me, offset, sizes)}

    def across(bits):
        return {a: (i + 1 - 2 * lax.rem(i, 2)) if f else i for a, i, f in zip(AXES, me, bits)}

    def line(axis, o):
        return tuple(o if a == axis else 0 for a in range(3))

    halo_sends = []
    for a in (2, 1, 0):
        halo_sends.append((2 * a, line(a, sizes[a] - 1)))
        if sizes[a] > 2:
            halo_sends.append((2 * a + 1, line(a, 1)))
    near_sends = [bits for bits in itertools.product((0, 1), repeat=3) if any(bits)]
    far_sends = [
        tuple(2 * o for o in offs)
        for offs in itertools.product(*(range(n // 2) for n in sizes))
        if any(offs)
    ]
    inv_sends = [line(2, o) for o in range(1, sizes[2])]

    barrier = pltpu.get_barrier_semaphore()
    offsets = sorted({o for _, o in halo_sends} | set(far_sends) | set(inv_sends))
    diagonals = [bits for bits in near_sends if sum(bits) > 1]
    for device in [at(o) for o in offsets] + [across(f) for f in diagonals]:
        pl.semaphore_signal(barrier, inc=1, device_id=device, device_id_type=MESH)

    mine = inv.at[pl.ds(me[2] * per, per)]
    loads = [
        pltpu.make_async_copy(src, dst, in_sem.at[i])
        for i, (src, dst) in enumerate(
            ((b_in, b_ref), (agg_in, agg_ref), (res_in, res_ref), (inv_in, mine))
        )
    ]
    copies = [
        pltpu.make_async_copy(sten_in.at[x], sten.at[x], sten_sem.at[x]) for x in range(xs)
    ]
    for c in loads + copies:
        c.start()

    pl.semaphore_wait(barrier, len(offsets) + len(diagonals))

    def remote(src, dst, send, recv, device):
        return pltpu.make_async_remote_copy(
            src_ref=src, dst_ref=dst, send_sem=send, recv_sem=recv,
            device_id=device, device_id_type=MESH,
        )

    def start_halo(src, halo, send, recv):
        out = [remote(src, halo.at[s], send.at[s], recv.at[s], at(o)) for s, o in halo_sends]
        for c in out:
            c.start()
        return out

    first = start_halo(b_in, halo1, h1s, h1r)

    for c in loads:
        c.wait()
    lab[0] = jnp.full(lab.shape[1:], agg_ref[0].astype(F32), F32)
    for x in range(xs):
        high, low = split(jnp.concatenate([res_ref[x]] * packs, axis=0))
        rp[pl.ds(0, comps), pl.ds(x * comps, comps)] = high
        rp[pl.ds(comps, comps), pl.ds(x * comps, comps)] = low
    early = [
        remote(mine, mine, ivs.at[i], ivr.at[i], at(o))
        for i, o in enumerate(inv_sends)
    ] + [
        remote(lab.at[0], lab.at[i + 1], lbs.at[i], lbr.at[i], at(o))
        for i, o in enumerate(far_sends)
    ]
    for c in early:
        c.start()

    inside = ((0,), (7, 8)) if xs == 2 else ((0,), (7,), (8,))
    sides, slots = [(), ()], [(), ()]
    for a in range(3):
        pair = ((1 + 2 * a,), (2 + 2 * a,))
        sides[a // 2] += pair if sizes[a] > 2 else (pair[0] + pair[1],)
        slots[a // 2] += (2 * a, 2 * a + 1) if sizes[a] > 2 else (2 * a,)

    for x in range(xs):
        copies[x].wait()
        for i, ks in enumerate(inside + sides[0] + sides[1]):
            high, low = split(sum(sten[x, k] for k in ks))
            cols = pl.ds(i * comps, comps)
            sw[x, pl.ds(0, comps), cols] = high
            sw[x, pl.ds(comps, comps), cols] = low

    def multiply(x, fields, begin):
        lhs = stack_split(jnp.concatenate(fields, axis=1))
        return dot_nt(lhs, sw[x, :, pl.ds(begin * comps, len(fields) * comps)])

    def local_part(field):
        out = []
        for x in range(xs):
            fields = [field[x], field[(x + 1) % xs]]
            if xs > 2:
                fields.append(field[(x + xs - 1) % xs])
            out.append(multiply(x, fields, 0))
        return out

    def halo_part(halo, base, sends):
        for group in range(2):
            for (slot, _), c in zip(halo_sends, sends):
                if slot in slots[group]:
                    c.wait_recv()
            begin = len(inside) + (len(sides[0]) if group else 0)
            base = [
                base[x] + multiply(x, [halo[i, x] for i in slots[group]], begin)
                for x in range(xs)
            ]
        return [fold(o) for o in base]

    lane = lax.broadcasted_iota(jnp.int32, (part, comps), 1)
    slot = lane // k3
    place = lax.rem(lane, k3)

    def pack(full):
        out = full[:part]
        for q in range(1, packs):
            out = jnp.where(slot == q, full[q * part : (q + 1) * part], out)
        return out

    def restricted(field):
        return pack(fold(dot_nt(stack_split(jnp.concatenate(field, axis=1)), rp[...])))

    def product(u, v, i):
        total = sum(u[x] * v[x] for x in range(xs))
        total = jnp.sum(total, axis=1, keepdims=True)
        return jnp.where(place == i, pack(jnp.broadcast_to(total, (nrhs, comps))), 0.0)

    def to_near(near, send, recv):
        out = [
            remote(near.at[0], near.at[i + 1], send.at[i], recv.at[i], across(f))
            for i, f in enumerate(near_sends)
        ]
        for c in out:
            c.start()
        return out

    def to_far(near, far, send, recv):
        total = near[0]
        for i in range(len(near_sends)):
            total = total + near[i + 1]
        far[0] = total
        out = [
            remote(far.at[0], far.at[i + 1], send.at[i], recv.at[i], at(o))
            for i, o in enumerate(far_sends)
        ]
        for c in out:
            c.start()
        return out

    bs = [b_ref[x] for x in range(xs)]
    base = local_part(bs)
    near_e[0, pl.ds(0, part)] = restricted(bs)
    w1s = halo_part(halo1, base, first)
    for x in range(xs):
        w1[x] = w1s[x]
    second = start_halo(w1, halo2, h2s, h2r)

    near_e[0, pl.ds(part, part)] = restricted(w1s)
    near_e[0, pl.ds(2 * part, part)] = product(w1s, w1s, 0) + product(w1s, bs, 1)
    third_e = to_near(near_e, nes, ner)
    base = local_part(w1s)
    for c in early:
        c.wait_recv()

    own = inv[agg_ref[0]]
    own_high, own_low = split(own)
    rows = lax.broadcasted_iota(jnp.int32, (comps, nc3), 0)
    cols = lax.broadcasted_iota(jnp.int32, (comps, nc3), 1)
    same = lax.rem(rows, k3) == lax.rem(cols, k3)
    block = (cols // k3).astype(F32)
    vec_high, vec_low = split(jnp.concatenate([res_ref[x] for x in range(xs)], axis=1))

    def prepare(g, carry):
        label = lab[g][0:1, 0:1]
        pick = jnp.where(same & (block == label), 1.0, 0.0).astype(BF16)
        weights = dot_nt(pick, own_high) + dot_nt(pick, own_low)
        high, low = split(weights)
        lift = dot_nn(high, vec_high) + (dot_nn(high, vec_low) + dot_nn(low, vec_high))
        high, low = split(lift)
        first_row = g * comps if isinstance(g, int) else pl.multiple_of(g * comps, comps)
        wr[pl.ds(first_row, comps), pl.ds(0, width)] = high
        wr[pl.ds(first_row, comps), pl.ds(width, width)] = low
        return carry

    loop(groups, prepare, 0)

    w2s = halo_part(halo2, base, second)
    near_l[0, pl.ds(0, part)] = restricted(w2s)
    near_l[0, pl.ds(part, part)] = (
        product(w1s, w2s, 2) + product(w2s, w2s, 3) + product(w2s, bs, 4)
    )
    third_l = to_near(near_l, nls, nlr)
    for x in range(xs):
        w2[x] = w2s[x]
    for c in third_e:
        c.wait_recv()
    fourth_e = to_far(near_e, far_e, fes, fer)
    for c in third_l:
        c.wait_recv()
    fourth_l = to_far(near_l, far_l, fls, flr)
    for c in first + early + second + third_e + third_l:
        c.wait_send()
    for c in fourth_e + fourth_l:
        c.wait_recv()

    def add(g, acc):
        return acc + (far_e[g, pl.ds(2 * part, part)] + far_l[g, pl.ds(part, part)])

    square = loop(groups, add, jnp.zeros((part, comps), F32))
    cross, corr, square2, cross2 = (pltpu.roll(square, comps - i, 1) for i in range(1, 5))
    step = cross / square
    ratio = corr / square
    turn = (step * corr - cross2) / (square2 - ratio * corr)
    push = step + turn * ratio

    def spread(coef):
        return jnp.concatenate(
            [
                jnp.broadcast_to(coef[:, q * k3 : q * k3 + 1], (part, comps))
                for q in range(packs)
            ],
            axis=0,
        )

    push, turn = spread(push), spread(turn)
    push_packed, turn_packed = pack(push), pack(turn)

    def coarse(g):
        mixed = (
            far_e[g, pl.ds(0, part)]
            - push_packed * far_e[g, pl.ds(part, part)]
            + turn_packed * far_l[g, pl.ds(0, part)]
        )
        return jnp.concatenate([jnp.where(slot == q, mixed, 0.0) for q in range(packs)], axis=0)

    pair = 2 if groups % 2 == 0 else 1

    def lift_step(h, acc):
        lhs = jnp.concatenate([coarse(h * pair + j) for j in range(pair)], axis=1)
        rows = pair * comps
        first_row = h * rows if isinstance(h, int) else pl.multiple_of(h * rows, rows)
        return acc + dot_nn(stack_split(lhs), wr[pl.ds(first_row, rows), :])

    lifted = fold(loop(groups // pair, lift_step, jnp.zeros((2 * nrhs, 2 * width), F32)))
    for x in range(xs):
        bx, ux, vx = b_ref[x], w1[x], w2[x]
        resid_ref[x] = bx - push * ux + turn * vx
        sol_ref[x] = (push * bx - turn * ux) + lifted[:, x * comps : (x + 1) * comps]
    for c in fourth_e + fourth_l:
        c.wait_send()


def finish(sol_ref, resid_ref, sol_out, resid_out, sem):
    out = [
        pltpu.make_async_copy(src, dst, sem.at[i])
        for i, (src, dst) in enumerate(((sol_ref, sol_out), (resid_ref, resid_out)))
    ]
    for c in out:
        c.start()
    for c in out:
        c.wait()


def body(sizes, right_side, stencil, restrict, aggregate, coarsest_inverse):
    shape = right_side.shape
    xs, nrhs, comps = shape[3:]
    k3 = restrict.shape[4]
    nc3 = coarsest_inverse.shape[1]
    na = nc3 // k3
    groups = (sizes[0] // 2) * (sizes[1] // 2) * (sizes[2] // 2)
    per = coarsest_inverse.shape[0] // k3
    part = nrhs * k3 // comps
    blocks = 9 - (xs == 2) - sum(n == 2 for n in sizes)
    vmem = pl.BlockSpec(memory_space=pltpu.VMEM)
    dma = pltpu.SemaphoreType.DMA
    field = jax.ShapeDtypeStruct((xs, nrhs, comps), F32)
    sol, resid = pl.pallas_call(
        functools.partial(kernel, sizes),
        out_shape=(field, field),
        in_specs=[pl.BlockSpec(memory_space=pltpu.HBM)] * 5,
        out_specs=(vmem, vmem),
        scratch_shapes=[
            pltpu.SMEM((xs,), jnp.int32),
            pltpu.VMEM((xs, nrhs, comps), F32),
            pltpu.VMEM((xs, k3, comps), F32),
            dma((4,)),
            pltpu.VMEM((xs, 9, comps, comps), F32),
            pltpu.VMEM((xs, 2 * comps, blocks * comps), BF16),
            pltpu.VMEM((2 * comps, xs * comps), BF16),
            pltpu.VMEM((6, xs, nrhs, comps), F32),
            pltpu.VMEM((6, xs, nrhs, comps), F32),
            pltpu.VMEM((xs, nrhs, comps), F32),
            pltpu.VMEM((xs, nrhs, comps), F32),
            pltpu.VMEM((na, k3, nc3), F32),
            pltpu.VMEM((groups, 8, comps), F32),
            pltpu.VMEM((groups * comps, 2 * xs * comps), BF16),
            pltpu.VMEM((8, 3 * part, comps), F32),
            pltpu.VMEM((groups, 3 * part, comps), F32),
            pltpu.VMEM((8, 2 * part, comps), F32),
            pltpu.VMEM((groups, 2 * part, comps), F32),
            dma((xs,)),
            dma((6,)), dma((6,)), dma((6,)), dma((6,)),
            dma((sizes[2],)), dma((sizes[2],)),
            dma((groups,)), dma((groups,)),
            dma((7,)), dma((7,)), dma((groups,)), dma((groups,)),
            dma((7,)), dma((7,)), dma((groups,)), dma((groups,)),
        ],
        compiler_params=pltpu.CompilerParams(
            collective_id=0,
            has_side_effects=True,
            vmem_limit_bytes=(16 if groups <= 8 else 48) * 2**20,
        ),
    )(
        *(
            pltpu.with_memory_space_constraint(a, pltpu.HBM)
            for a in (
                aggregate.reshape(xs),
                right_side.reshape(xs, nrhs, comps),
                stencil.reshape(xs, 9, comps, comps),
                restrict.reshape(xs, k3, comps),
                coarsest_inverse.reshape(per, k3, nc3),
            )
        )
    )
    sol, resid = pl.pallas_call(
        finish,
        out_shape=(field, field),
        in_specs=[vmem, vmem],
        out_specs=[pl.BlockSpec(memory_space=pl.ANY)] * 2,
        scratch_shapes=[dma((2,))],
        compiler_params=pltpu.CompilerParams(vmem_limit_bytes=2**20),
    )(sol, resid)
    return sol.reshape(shape), resid.reshape(shape)


def solution(mesh):
    sizes = tuple(mesh.shape[a] for a in AXES)
    return jax.shard_map(
        functools.partial(body, sizes),
        mesh=mesh,
        in_specs=(
            P("ta", "gz", "xy", None, None, None),
            P("ta", "gz", "xy", None, None, None, None),
            P("ta", "gz", "xy", None, None, None),
            P("ta", "gz", "xy", None),
            P("xy", None),
        ),
        out_specs=(P("ta", "gz", "xy", None, None, None), P("ta", "gz", "xy", None, None, None)),
        check_vma=False,
    )
```

```python
import functools
import itertools

import jax
import jax.numpy as jnp
from jax import lax
from jax.experimental import pallas as pl
from jax.experimental.pallas import tpu as pltpu
from jax.sharding import PartitionSpec as P

AXES = ("ta", "gz", "xy")
F32 = jnp.float32
BF16 = jnp.bfloat16
MESH = pl.DeviceIdType.MESH


def split(x):
    high = x.astype(BF16)
    return high, (x - high.astype(F32)).astype(BF16)


def dot_nt(a, b):
    return lax.dot_general(a, b, (((1,), (1,)), ((), ())), preferred_element_type=F32)


def dot_nn(a, b):
    return lax.dot_general(a, b, (((1,), (0,)), ((), ())), preferred_element_type=F32)


def stack_split(x):
    return jnp.concatenate(split(x), axis=0)


def fold(o):
    r, n = o.shape[0] // 2, o.shape[1] // 2
    return o[:r, :n] + (o[:r, n:] + o[r:, :n])


def loop(n, step, init, most=8):
    if n <= most:
        for i in range(n):
            init = step(i, init)
        return init
    return lax.fori_loop(0, n, step, init)


def kernel(
    sizes, agg_in, b_in, sten_in, res_in, inv_in, sol_ref, resid_ref,
    agg_ref, b_ref, res_ref, in_sem, sten, sw, rp, halo1, halo2, w1, w2, inv, lab, wr, near_e, far_e, near_l, far_l,
    sten_sem, h1s, h1r, h2s, h2r, ivs, ivr, lbs, lbr, nes, ner, fes, fer, nls, nlr, fls, flr,
):
    xs, nrhs, comps = b_ref.shape
    k3 = res_ref.shape[1]
    na, _, nc3 = inv.shape
    per = inv_in.shape[0]
    groups = far_e.shape[0]
    packs = comps // k3
    part = nrhs // packs
    width = xs * comps
    me = tuple(lax.axis_index(a) for a in AXES)

    def at(offset):
        return {a: lax.rem(i + o, n) for a, i, o, n in zip(AXES, me, offset, sizes)}

    def across(bits):
        return {a: (i + 1 - 2 * lax.rem(i, 2)) if f else i for a, i, f in zip(AXES, me, bits)}

    def line(axis, o):
        return tuple(o if a == axis else 0 for a in range(3))

    halo_sends = []
    for a in (2, 1, 0):
        halo_sends.append((2 * a, line(a, sizes[a] - 1)))
        if sizes[a] > 2:
            halo_sends.append((2 * a + 1, line(a, 1)))
    near_sends = [bits for bits in itertools.product((0, 1), repeat=3) if any(bits)]
    far_sends = [
        tuple(2 * o for o in offs)
        for offs in itertools.product(*(range(n // 2) for n in sizes))
        if any(offs)
    ]
    inv_sends = [line(2, o) for o in range(1, sizes[2])]

    barrier = pltpu.get_barrier_semaphore()
    offsets = sorted({o for _, o in halo_sends} | set(far_sends) | set(inv_sends))
    diagonals = [bits for bits in near_sends if sum(bits) > 1]
    for device in [at(o) for o in offsets] + [across(f) for f in diagonals]:
        pl.semaphore_signal(barrier, inc=1, device_id=device, device_id_type=MESH)

    mine = inv.at[pl.ds(me[2] * per, per)]
    loads = [
        pltpu.make_async_copy(src, dst, in_sem.at[i])
        for i, (src, dst) in enumerate(
            ((b_in, b_ref), (agg_in, agg_ref), (res_in, res_ref), (inv_in, mine))
        )
    ]
    copies = [
        pltpu.make_async_copy(sten_in.at[x], sten.at[x], sten_sem.at[x]) for x in range(xs)
    ]
    for c in loads + copies:
        c.start()

    pl.semaphore_wait(barrier, len(offsets) + len(diagonals))

    def remote(src, dst, send, recv, device):
        return pltpu.make_async_remote_copy(
            src_ref=src, dst_ref=dst, send_sem=send, recv_sem=recv,
            device_id=device, device_id_type=MESH,
        )

    def start_halo(src, halo, send, recv):
        out = [remote(src, halo.at[s], send.at[s], recv.at[s], at(o)) for s, o in halo_sends]
        for c in out:
            c.start()
        return out

    first = start_halo(b_in, halo1, h1s, h1r)

    for c in loads:
        c.wait()
    lab[0] = jnp.full(lab.shape[1:], agg_ref[0].astype(F32), F32)
    for x in range(xs):
        high, low = split(jnp.concatenate([res_ref[x]] * packs, axis=0))
        rp[pl.ds(0, comps), pl.ds(x * comps, comps)] = high
        rp[pl.ds(comps, comps), pl.ds(x * comps, comps)] = low
    early = [
        remote(lab.at[0], lab.at[i + 1], lbs.at[i], lbr.at[i], at(o))
        for i, o in enumerate(far_sends)
    ]
    for c in early:
        c.start()
    gather = [
        remote(mine, mine, ivs.at[i], ivr.at[i], at(o)) for i, o in enumerate(inv_sends)
    ]

    inside = ((0,), (7, 8)) if xs == 2 else ((0,), (7,), (8,))
    sides, slots = [(), ()], [(), ()]
    for a in range(3):
        pair = ((1 + 2 * a,), (2 + 2 * a,))
        sides[a // 2] += pair if sizes[a] > 2 else (pair[0] + pair[1],)
        slots[a // 2] += (2 * a, 2 * a + 1) if sizes[a] > 2 else (2 * a,)

    for x in range(xs):
        copies[x].wait()
        for i, ks in enumerate(inside + sides[0] + sides[1]):
            high, low = split(sum(sten[x, k] for k in ks))
            cols = pl.ds(i * comps, comps)
            sw[x, pl.ds(0, comps), cols] = high
            sw[x, pl.ds(comps, comps), cols] = low

    def multiply(x, fields, begin):
        lhs = stack_split(jnp.concatenate(fields, axis=1))
        return dot_nt(lhs, sw[x, :, pl.ds(begin * comps, len(fields) * comps)])

    def local_part(field):
        out = []
        for x in range(xs):
            fields = [field[x], field[(x + 1) % xs]]
            if xs > 2:
                fields.append(field[(x + xs - 1) % xs])
            out.append(multiply(x, fields, 0))
        return out

    def halo_part(halo, base, sends, then=()):
        for group in range(2):
            for (slot, _), c in zip(halo_sends, sends):
                if slot in slots[group]:
                    c.wait_recv()
            if group:
                for c in then:
                    c.start()
            begin = len(inside) + (len(sides[0]) if group else 0)
            base = [
                base[x] + multiply(x, [halo[i, x] for i in slots[group]], begin)
                for x in range(xs)
            ]
        return [fold(o) for o in base]

    lane = lax.broadcasted_iota(jnp.int32, (part, comps), 1)
    slot = lane // k3
    place = lax.rem(lane, k3)

    def pack(full):
        out = full[:part]
        for q in range(1, packs):
            out = jnp.where(slot == q, full[q * part : (q + 1) * part], out)
        return out

    def restricted(field):
        return pack(fold(dot_nt(stack_split(jnp.concatenate(field, axis=1)), rp[...])))

    def product(u, v, i):
        total = sum(u[x] * v[x] for x in range(xs))
        total = jnp.sum(total, axis=1, keepdims=True)
        return jnp.where(place == i, pack(jnp.broadcast_to(total, (nrhs, comps))), 0.0)

    def to_near(near, send, recv):
        out = [
            remote(near.at[0], near.at[i + 1], send.at[i], recv.at[i], across(f))
            for i, f in enumerate(near_sends)
        ]
        for c in out:
            c.start()
        return out

    def to_far(near, far, send, recv):
        total = near[0]
        for i in range(len(near_sends)):
            total = total + near[i + 1]
        far[0] = total
        out = [
            remote(far.at[0], far.at[i + 1], send.at[i], recv.at[i], at(o))
            for i, o in enumerate(far_sends)
        ]
        for c in out:
            c.start()
        return out

    bs = [b_ref[x] for x in range(xs)]
    base = local_part(bs)
    near_e[0, pl.ds(0, part)] = restricted(bs)
    w1s = halo_part(halo1, base, first, gather)
    for x in range(xs):
        w1[x] = w1s[x]
    second = start_halo(w1, halo2, h2s, h2r)

    near_e[0, pl.ds(part, part)] = restricted(w1s)
    near_e[0, pl.ds(2 * part, part)] = product(w1s, w1s, 0) + product(w1s, bs, 1)
    third_e = to_near(near_e, nes, ner)
    base = local_part(w1s)
    w2s = halo_part(halo2, base, second)
    near_l[0, pl.ds(0, part)] = restricted(w2s)
    near_l[0, pl.ds(part, part)] = (
        product(w1s, w2s, 2) + product(w2s, w2s, 3) + product(w2s, bs, 4)
    )
    third_l = to_near(near_l, nls, nlr)
    for x in range(xs):
        w2[x] = w2s[x]
    for c in third_e:
        c.wait_recv()
    fourth_e = to_far(near_e, far_e, fes, fer)
    for c in third_l:
        c.wait_recv()
    fourth_l = to_far(near_l, far_l, fls, flr)
    for c in early + gather:
        c.wait_recv()

    own = inv[agg_ref[0]]
    own_high, own_low = split(own)
    rows = lax.broadcasted_iota(jnp.int32, (comps, nc3), 0)
    cols = lax.broadcasted_iota(jnp.int32, (comps, nc3), 1)
    same = lax.rem(rows, k3) == lax.rem(cols, k3)
    block = (cols // k3).astype(F32)
    vec_high, vec_low = split(jnp.concatenate([res_ref[x] for x in range(xs)], axis=1))

    def prepare(g, carry):
        label = lab[g][0:1, 0:1]
        pick = jnp.where(same & (block == label), 1.0, 0.0).astype(BF16)
        weights = dot_nt(pick, own_high) + dot_nt(pick, own_low)
        high, low = split(weights)
        lift = dot_nn(high, vec_high) + (dot_nn(high, vec_low) + dot_nn(low, vec_high))
        high, low = split(lift)
        first_row = g * comps if isinstance(g, int) else pl.multiple_of(g * comps, comps)
        wr[pl.ds(first_row, comps), pl.ds(0, width)] = high
        wr[pl.ds(first_row, comps), pl.ds(width, width)] = low
        return carry

    loop(groups, prepare, 0)

    for c in first + early + gather + second + third_e + third_l:
        c.wait_send()
    for c in fourth_e + fourth_l:
        c.wait_recv()

    def add(g, acc):
        return acc + (far_e[g, pl.ds(2 * part, part)] + far_l[g, pl.ds(part, part)])

    square = loop(groups, add, jnp.zeros((part, comps), F32))
    cross, corr, square2, cross2 = (pltpu.roll(square, comps - i, 1) for i in range(1, 5))
    step = cross / square
    ratio = corr / square
    turn = (step * corr - cross2) / (square2 - ratio * corr)
    push = step + turn * ratio

    def spread(coef):
        return jnp.concatenate(
            [
                jnp.broadcast_to(coef[:, q * k3 : q * k3 + 1], (part, comps))
                for q in range(packs)
            ],
            axis=0,
        )

    push, turn = spread(push), spread(turn)
    push_packed, turn_packed = pack(push), pack(turn)

    def coarse(g):
        mixed = (
            far_e[g, pl.ds(0, part)]
            - push_packed * far_e[g, pl.ds(part, part)]
            + turn_packed * far_l[g, pl.ds(0, part)]
        )
        return jnp.concatenate([jnp.where(slot == q, mixed, 0.0) for q in range(packs)], axis=0)

    pair = 2 if groups % 2 == 0 else 1

    def lift_step(h, acc):
        lhs = jnp.concatenate([coarse(h * pair + j) for j in range(pair)], axis=1)
        rows = pair * comps
        first_row = h * rows if isinstance(h, int) else pl.multiple_of(h * rows, rows)
        return acc + dot_nn(stack_split(lhs), wr[pl.ds(first_row, rows), :])

    lifted = fold(loop(groups // pair, lift_step, jnp.zeros((2 * nrhs, 2 * width), F32)))
    for x in range(xs):
        bx, ux, vx = b_ref[x], w1[x], w2[x]
        resid_ref[x] = bx - push * ux + turn * vx
        sol_ref[x] = (push * bx - turn * ux) + lifted[:, x * comps : (x + 1) * comps]
    for c in fourth_e + fourth_l:
        c.wait_send()


def finish(sol_ref, resid_ref, sol_out, resid_out, sem):
    out = [
        pltpu.make_async_copy(src, dst, sem.at[i])
        for i, (src, dst) in enumerate(((sol_ref, sol_out), (resid_ref, resid_out)))
    ]
    for c in out:
        c.start()
    for c in out:
        c.wait()


def body(sizes, right_side, stencil, restrict, aggregate, coarsest_inverse):
    shape = right_side.shape
    xs, nrhs, comps = shape[3:]
    k3 = restrict.shape[4]
    nc3 = coarsest_inverse.shape[1]
    na = nc3 // k3
    groups = (sizes[0] // 2) * (sizes[1] // 2) * (sizes[2] // 2)
    per = coarsest_inverse.shape[0] // k3
    part = nrhs * k3 // comps
    blocks = 9 - (xs == 2) - sum(n == 2 for n in sizes)
    vmem = pl.BlockSpec(memory_space=pltpu.VMEM)
    dma = pltpu.SemaphoreType.DMA
    field = jax.ShapeDtypeStruct((xs, nrhs, comps), F32)
    sol, resid = pl.pallas_call(
        functools.partial(kernel, sizes),
        out_shape=(field, field),
        in_specs=[pl.BlockSpec(memory_space=pltpu.HBM)] * 5,
        out_specs=(vmem, vmem),
        scratch_shapes=[
            pltpu.SMEM((xs,), jnp.int32),
            pltpu.VMEM((xs, nrhs, comps), F32),
            pltpu.VMEM((xs, k3, comps), F32),
            dma((4,)),
            pltpu.VMEM((xs, 9, comps, comps), F32),
            pltpu.VMEM((xs, 2 * comps, blocks * comps), BF16),
            pltpu.VMEM((2 * comps, xs * comps), BF16),
            pltpu.VMEM((6, xs, nrhs, comps), F32),
            pltpu.VMEM((6, xs, nrhs, comps), F32),
            pltpu.VMEM((xs, nrhs, comps), F32),
            pltpu.VMEM((xs, nrhs, comps), F32),
            pltpu.VMEM((na, k3, nc3), F32),
            pltpu.VMEM((groups, 8, comps), F32),
            pltpu.VMEM((groups * comps, 2 * xs * comps), BF16),
            pltpu.VMEM((8, 3 * part, comps), F32),
            pltpu.VMEM((groups, 3 * part, comps), F32),
            pltpu.VMEM((8, 2 * part, comps), F32),
            pltpu.VMEM((groups, 2 * part, comps), F32),
            dma((xs,)),
            dma((6,)), dma((6,)), dma((6,)), dma((6,)),
            dma((sizes[2],)), dma((sizes[2],)),
            dma((groups,)), dma((groups,)),
            dma((7,)), dma((7,)), dma((groups,)), dma((groups,)),
            dma((7,)), dma((7,)), dma((groups,)), dma((groups,)),
        ],
        compiler_params=pltpu.CompilerParams(
            collective_id=0,
            has_side_effects=True,
            vmem_limit_bytes=(16 if groups <= 8 else 48) * 2**20,
        ),
    )(
        *(
            pltpu.with_memory_space_constraint(a, pltpu.HBM)
            for a in (
                aggregate.reshape(xs),
                right_side.reshape(xs, nrhs, comps),
                stencil.reshape(xs, 9, comps, comps),
                restrict.reshape(xs, k3, comps),
                coarsest_inverse.reshape(per, k3, nc3),
            )
        )
    )
    sol, resid = pl.pallas_call(
        finish,
        out_shape=(field, field),
        in_specs=[vmem, vmem],
        out_specs=[pl.BlockSpec(memory_space=pl.ANY)] * 2,
        scratch_shapes=[dma((2,))],
        compiler_params=pltpu.CompilerParams(vmem_limit_bytes=2**20),
    )(sol, resid)
    return sol.reshape(shape), resid.reshape(shape)


def solution(mesh):
    sizes = tuple(mesh.shape[a] for a in AXES)
    return jax.shard_map(
        functools.partial(body, sizes),
        mesh=mesh,
        in_specs=(
            P("ta", "gz", "xy", None, None, None),
            P("ta", "gz", "xy", None, None, None, None),
            P("ta", "gz", "xy", None, None, None),
            P("ta", "gz", "xy", None),
            P("xy", None),
        ),
        out_specs=(P("ta", "gz", "xy", None, None, None), P("ta", "gz", "xy", None, None, None)),
        check_vma=False,
    )
```

```python
import functools
import itertools

import jax
import jax.numpy as jnp
from jax import lax
from jax.experimental import pallas as pl
from jax.experimental.pallas import tpu as pltpu
from jax.sharding import PartitionSpec as P

AXES = ("ta", "gz", "xy")
F32 = jnp.float32
BF16 = jnp.bfloat16
MESH = pl.DeviceIdType.MESH


def split(x):
    high = x.astype(BF16)
    return high, (x - high.astype(F32)).astype(BF16)


def dot_nt(a, b):
    return lax.dot_general(a, b, (((1,), (1,)), ((), ())), preferred_element_type=F32)


def dot_nn(a, b):
    return lax.dot_general(a, b, (((1,), (0,)), ((), ())), preferred_element_type=F32)


def stack_split(x):
    return jnp.concatenate(split(x), axis=0)


def fold(o):
    r, n = o.shape[0] // 2, o.shape[1] // 2
    return o[:r, :n] + (o[:r, n:] + o[r:, :n])


def loop(n, step, init, most=8):
    if n <= most:
        for i in range(n):
            init = step(i, init)
        return init
    return lax.fori_loop(0, n, step, init)


def kernel(
    sizes, agg_in, b_in, sten_in, res_in, inv_in, sol_ref, resid_ref,
    agg_ref, b_ref, res_ref, in_sem, sten, sw, rp, halo1, halo2, w1, w2, inv, lab, wr, near, far,
    sten_sem, h1s, h1r, h2s, h2r, ivs, ivr, lbs, lbr, nrs, nrr, frs, frr,
):
    xs, nrhs, comps = b_ref.shape
    k3 = res_ref.shape[1]
    na, _, nc3 = inv.shape
    per = inv_in.shape[0]
    groups = far.shape[1]
    packs = comps // k3
    part = nrhs // packs
    width = xs * comps
    me = tuple(lax.axis_index(a) for a in AXES)

    def at(offset):
        return {a: lax.rem(i + o, n) for a, i, o, n in zip(AXES, me, offset, sizes)}

    def across(bits):
        return {a: (i + 1 - 2 * lax.rem(i, 2)) if f else i for a, i, f in zip(AXES, me, bits)}

    def line(axis, o):
        return tuple(o if a == axis else 0 for a in range(3))

    halo_sends = []
    for a in (2, 1, 0):
        halo_sends.append((2 * a, line(a, sizes[a] - 1)))
        if sizes[a] > 2:
            halo_sends.append((2 * a + 1, line(a, 1)))
    near_sends = [bits for bits in itertools.product((0, 1), repeat=3) if any(bits)]
    near_sends.sort(key=lambda f: -(f[0] + f[2]))
    far_sends = [
        tuple(2 * o for o in offs)
        for offs in itertools.product(*(range(n // 2) for n in sizes))
        if any(offs)
    ]
    inv_sends = [line(2, o) for o in range(1, sizes[2])]

    barrier = pltpu.get_barrier_semaphore()
    offsets = sorted({o for _, o in halo_sends} | set(far_sends) | set(inv_sends))
    diagonals = [bits for bits in near_sends if sum(bits) > 1]
    for device in [at(o) for o in offsets] + [across(f) for f in diagonals]:
        pl.semaphore_signal(barrier, inc=1, device_id=device, device_id_type=MESH)

    mine = inv.at[pl.ds(me[2] * per, per)]
    loads = [
        pltpu.make_async_copy(src, dst, in_sem.at[i])
        for i, (src, dst) in enumerate(
            ((b_in, b_ref), (agg_in, agg_ref), (res_in, res_ref), (inv_in, mine))
        )
    ]
    copies = [
        pltpu.make_async_copy(sten_in.at[x], sten.at[x], sten_sem.at[x]) for x in range(xs)
    ]
    for c in loads + copies:
        c.start()

    pl.semaphore_wait(barrier, len(offsets) + len(diagonals))

    def remote(src, dst, send, recv, device):
        return pltpu.make_async_remote_copy(
            src_ref=src, dst_ref=dst, send_sem=send, recv_sem=recv,
            device_id=device, device_id_type=MESH,
        )

    def start_halo(src, halo, send, recv):
        out = [remote(src, halo.at[s], send.at[s], recv.at[s], at(o)) for s, o in halo_sends]
        for c in out:
            c.start()
        return out

    first = start_halo(b_in, halo1, h1s, h1r)

    for c in loads:
        c.wait()
    lab[0] = jnp.full(lab.shape[1:], agg_ref[0].astype(F32), F32)
    for x in range(xs):
        high, low = split(jnp.concatenate([res_ref[x]] * packs, axis=0))
        rp[pl.ds(0, comps), pl.ds(x * comps, comps)] = high
        rp[pl.ds(comps, comps), pl.ds(x * comps, comps)] = low
    early = [
        remote(mine, mine, ivs.at[i], ivr.at[i], at(o))
        for i, o in enumerate(inv_sends)
    ] + [
        remote(lab.at[0], lab.at[i + 1], lbs.at[i], lbr.at[i], at(o))
        for i, o in enumerate(far_sends)
    ]
    for c in early:
        c.start()

    inside = ((0,), (7, 8)) if xs == 2 else ((0,), (7,), (8,))
    sides, slots = [(), ()], [(), ()]
    for a in range(3):
        pair = ((1 + 2 * a,), (2 + 2 * a,))
        sides[a // 2] += pair if sizes[a] > 2 else (pair[0] + pair[1],)
        slots[a // 2] += (2 * a, 2 * a + 1) if sizes[a] > 2 else (2 * a,)

    for x in range(xs):
        copies[x].wait()
        for i, ks in enumerate(inside + sides[0] + sides[1]):
            high, low = split(sum(sten[x, k] for k in ks))
            cols = pl.ds(i * comps, comps)
            sw[x, pl.ds(0, comps), cols] = high
            sw[x, pl.ds(comps, comps), cols] = low

    def multiply(x, fields, begin):
        lhs = stack_split(jnp.concatenate(fields, axis=1))
        return dot_nt(lhs, sw[x, :, pl.ds(begin * comps, len(fields) * comps)])

    def local_part(field):
        out = []
        for x in range(xs):
            fields = [field[x], field[(x + 1) % xs]]
            if xs > 2:
                fields.append(field[(x + xs - 1) % xs])
            out.append(multiply(x, fields, 0))
        return out

    def halo_part(halo, base, sends):
        for group in range(2):
            for (slot, _), c in zip(halo_sends, sends):
                if slot in slots[group]:
                    c.wait_recv()
            begin = len(inside) + (len(sides[0]) if group else 0)
            base = [
                base[x] + multiply(x, [halo[i, x] for i in slots[group]], begin)
                for x in range(xs)
            ]
        return [fold(o) for o in base]

    lane = lax.broadcasted_iota(jnp.int32, (part, comps), 1)
    slot = lane // k3

    def pack(full):
        out = full[:part]
        for q in range(1, packs):
            out = jnp.where(slot == q, full[q * part : (q + 1) * part], out)
        return out

    def restricted(field):
        return pack(fold(dot_nt(stack_split(jnp.concatenate(field, axis=1)), rp[...])))

    ones = jnp.ones((16, comps), BF16)

    def products(*pairs):
        rows = [sum(u[x] * v[x] for x in range(xs)) for u, v in pairs]
        if len(rows) < packs:
            rows.append(jnp.zeros(((packs - len(rows)) * nrhs, comps), F32))
        high, low = split(jnp.concatenate(rows, axis=0))
        return (dot_nt(ones, high) + dot_nt(ones, low))[:1]

    def to_near(i, count):
        here = pl.ds(0, count)
        out = [
            remote(
                near.at[i, 0, here], near.at[i, j + 1, here], nrs.at[i, j], nrr.at[i, j], across(f)
            )
            for j, f in enumerate(near_sends)
        ]
        for c in out:
            c.start()
        return out

    def to_far(i, count, arriving):
        here = pl.ds(0, count)
        for c in arriving:
            c.wait_recv()
        total = near[i, 0, here]
        for j in range(len(near_sends)):
            total = total + near[i, j + 1, here]
        far[i, 0, here] = total
        out = [
            remote(far.at[i, 0, here], far.at[i, j + 1, here], frs.at[i, j], frr.at[i, j], at(o))
            for j, o in enumerate(far_sends)
        ]
        for c in out:
            c.start()
        return out

    bs = [b_ref[x] for x in range(xs)]
    base = local_part(bs)
    near[0, 0, pl.ds(0, part)] = restricted(bs)
    near_b = to_near(0, part)
    w1s = halo_part(halo1, base, first)
    for x in range(xs):
        w1[x] = w1s[x]
    second = start_halo(w1, halo2, h2s, h2r)

    near[1, 0, pl.ds(0, part)] = restricted(w1s)
    near[1, 0, pl.ds(part, 1)] = products((w1s, w1s), (w1s, bs))
    near_1 = to_near(1, part + 1)
    far_b = to_far(0, part, near_b)
    base = local_part(w1s)
    for c in early:
        c.wait_recv()

    own = inv[agg_ref[0]]
    own_high, own_low = split(own)
    rows = lax.broadcasted_iota(jnp.int32, (comps, nc3), 0)
    cols = lax.broadcasted_iota(jnp.int32, (comps, nc3), 1)
    same = lax.rem(rows, k3) == lax.rem(cols, k3)
    block = (cols // k3).astype(F32)
    vec_high, vec_low = split(jnp.concatenate([res_ref[x] for x in range(xs)], axis=1))

    def prepare(g, carry):
        label = lab[g][0:1, 0:1]
        pick = jnp.where(same & (block == label), 1.0, 0.0).astype(BF16)
        weights = dot_nt(pick, own_high) + dot_nt(pick, own_low)
        high, low = split(weights)
        lift = dot_nn(high, vec_high) + (dot_nn(high, vec_low) + dot_nn(low, vec_high))
        high, low = split(lift)
        first_row = g * comps if isinstance(g, int) else pl.multiple_of(g * comps, comps)
        wr[pl.ds(first_row, comps), pl.ds(0, width)] = high
        wr[pl.ds(first_row, comps), pl.ds(width, width)] = low
        return carry

    loop(groups, prepare, 0)

    w2s = halo_part(halo2, base, second)
    near[2, 0, pl.ds(0, part)] = restricted(w2s)
    near[2, 0, pl.ds(part, 1)] = products((w1s, w2s), (w2s, w2s), (w2s, bs))
    near_2 = to_near(2, part + 1)
    for x in range(xs):
        w2[x] = w2s[x]
    far_1 = to_far(1, part + 1, near_1)
    far_2 = to_far(2, part + 1, near_2)
    for c in first + early + second + near_b + near_1 + near_2:
        c.wait_send()
    for c in far_b + far_1 + far_2:
        c.wait_recv()

    def add(g, acc):
        return acc[0] + far[1, g, pl.ds(part, 1)], acc[1] + far[2, g, pl.ds(part, 1)]

    blank = jnp.zeros((1, comps), F32)
    square, corr = loop(groups, add, (blank, blank))
    cross = pltpu.roll(square, comps - nrhs, 1)
    square2 = pltpu.roll(corr, comps - nrhs, 1)
    cross2 = pltpu.roll(corr, comps - 2 * nrhs, 1)
    step = cross / square
    ratio = corr / square
    turn = (step * corr - cross2) / (square2 - ratio * corr)
    push = step + turn * ratio

    own_lane = lax.broadcasted_iota(jnp.int32, (nrhs, comps), 0) == lax.broadcasted_iota(
        jnp.int32, (nrhs, comps), 1
    )

    def spread(coef):
        column = jnp.where(own_lane, jnp.broadcast_to(coef, (nrhs, comps)), 0.0)
        return jnp.broadcast_to(jnp.sum(column, axis=1, keepdims=True), (nrhs, comps))

    push, turn = spread(push), spread(turn)
    push_packed, turn_packed = pack(push), pack(turn)

    def coarse(g):
        mixed = (
            far[0, g, pl.ds(0, part)]
            - push_packed * far[1, g, pl.ds(0, part)]
            + turn_packed * far[2, g, pl.ds(0, part)]
        )
        return jnp.concatenate([jnp.where(slot == q, mixed, 0.0) for q in range(packs)], axis=0)

    pair = 2 if groups % 2 == 0 else 1

    def lift_step(h, acc):
        lhs = jnp.concatenate([coarse(h * pair + j) for j in range(pair)], axis=1)
        rows = pair * comps
        first_row = h * rows if isinstance(h, int) else pl.multiple_of(h * rows, rows)
        return acc + dot_nn(stack_split(lhs), wr[pl.ds(first_row, rows), :])

    lifted = fold(loop(groups // pair, lift_step, jnp.zeros((2 * nrhs, 2 * width), F32)))
    for x in range(xs):
        bx, ux, vx = b_ref[x], w1[x], w2[x]
        resid_ref[x] = bx - push * ux + turn * vx
        sol_ref[x] = (push * bx - turn * ux) + lifted[:, x * comps : (x + 1) * comps]
    for c in far_b + far_1 + far_2:
        c.wait_send()


def finish(sol_ref, resid_ref, sol_out, resid_out, sem):
    out = [
        pltpu.make_async_copy(src, dst, sem.at[i])
        for i, (src, dst) in enumerate(((sol_ref, sol_out), (resid_ref, resid_out)))
    ]
    for c in out:
        c.start()
    for c in out:
        c.wait()


def body(sizes, right_side, stencil, restrict, aggregate, coarsest_inverse):
    shape = right_side.shape
    xs, nrhs, comps = shape[3:]
    k3 = restrict.shape[4]
    nc3 = coarsest_inverse.shape[1]
    na = nc3 // k3
    groups = (sizes[0] // 2) * (sizes[1] // 2) * (sizes[2] // 2)
    per = coarsest_inverse.shape[0] // k3
    part = nrhs * k3 // comps
    blocks = 9 - (xs == 2) - sum(n == 2 for n in sizes)
    vmem = pl.BlockSpec(memory_space=pltpu.VMEM)
    dma = pltpu.SemaphoreType.DMA
    field = jax.ShapeDtypeStruct((xs, nrhs, comps), F32)
    sol, resid = pl.pallas_call(
        functools.partial(kernel, sizes),
        out_shape=(field, field),
        in_specs=[pl.BlockSpec(memory_space=pltpu.HBM)] * 5,
        out_specs=(vmem, vmem),
        scratch_shapes=[
            pltpu.SMEM((xs,), jnp.int32),
            pltpu.VMEM((xs, nrhs, comps), F32),
            pltpu.VMEM((xs, k3, comps), F32),
            dma((4,)),
            pltpu.VMEM((xs, 9, comps, comps), F32),
            pltpu.VMEM((xs, 2 * comps, blocks * comps), BF16),
            pltpu.VMEM((2 * comps, xs * comps), BF16),
            pltpu.VMEM((6, xs, nrhs, comps), F32),
            pltpu.VMEM((6, xs, nrhs, comps), F32),
            pltpu.VMEM((xs, nrhs, comps), F32),
            pltpu.VMEM((xs, nrhs, comps), F32),
            pltpu.VMEM((na, k3, nc3), F32),
            pltpu.VMEM((groups, 8, comps), F32),
            pltpu.VMEM((groups * comps, 2 * xs * comps), BF16),
            pltpu.VMEM((3, 8, 2 * part, comps), F32),
            pltpu.VMEM((3, groups, 2 * part, comps), F32),
            dma((xs,)),
            dma((6,)), dma((6,)), dma((6,)), dma((6,)),
            dma((sizes[2],)), dma((sizes[2],)),
            dma((groups,)), dma((groups,)),
            dma((3, 7)), dma((3, 7)), dma((3, groups)), dma((3, groups)),
        ],
        compiler_params=pltpu.CompilerParams(
            collective_id=0,
            has_side_effects=True,
            vmem_limit_bytes=(16 if groups <= 8 else 48) * 2**20,
        ),
    )(
        *(
            pltpu.with_memory_space_constraint(a, pltpu.HBM)
            for a in (
                aggregate.reshape(xs),
                right_side.reshape(xs, nrhs, comps),
                stencil.reshape(xs, 9, comps, comps),
                restrict.reshape(xs, k3, comps),
                coarsest_inverse.reshape(per, k3, nc3),
            )
        )
    )
    sol, resid = pl.pallas_call(
        finish,
        out_shape=(field, field),
        in_specs=[vmem, vmem],
        out_specs=[pl.BlockSpec(memory_space=pl.ANY)] * 2,
        scratch_shapes=[dma((2,))],
        compiler_params=pltpu.CompilerParams(vmem_limit_bytes=2**20),
    )(sol, resid)
    return sol.reshape(shape), resid.reshape(shape)


def solution(mesh):
    sizes = tuple(mesh.shape[a] for a in AXES)
    return jax.shard_map(
        functools.partial(body, sizes),
        mesh=mesh,
        in_specs=(
            P("ta", "gz", "xy", None, None, None),
            P("ta", "gz", "xy", None, None, None, None),
            P("ta", "gz", "xy", None, None, None),
            P("ta", "gz", "xy", None),
            P("xy", None),
        ),
        out_specs=(P("ta", "gz", "xy", None, None, None), P("ta", "gz", "xy", None, None, None)),
        check_vma=False,
    )
```

```python
import functools
import itertools

import jax
import jax.numpy as jnp
from jax import lax
from jax.experimental import pallas as pl
from jax.experimental.pallas import tpu as pltpu
from jax.sharding import PartitionSpec as P

AXES = ("ta", "gz", "xy")
F32 = jnp.float32
BF16 = jnp.bfloat16
MESH = pl.DeviceIdType.MESH


def split(x):
    high = x.astype(BF16)
    return high, (x - high.astype(F32)).astype(BF16)


def dot_nt(a, b):
    return lax.dot_general(a, b, (((1,), (1,)), ((), ())), preferred_element_type=F32)


def dot_nn(a, b):
    return lax.dot_general(a, b, (((1,), (0,)), ((), ())), preferred_element_type=F32)


def stack_split(x):
    return jnp.concatenate(split(x), axis=0)


def fold(o):
    r, n = o.shape[0] // 2, o.shape[1] // 2
    return o[:r, :n] + (o[:r, n:] + o[r:, :n])


def loop(n, step, init, most=8):
    if n <= most:
        for i in range(n):
            init = step(i, init)
        return init
    return lax.fori_loop(0, n, step, init)


def kernel(
    sizes, agg_in, b_in, sten_in, res_in, inv_in, sol_ref, resid_ref,
    agg_ref, b_ref, res_ref, in_sem, sten, sw, rp, halo1, halo2, w1, w2, inv, lab, wr, near, far,
    sten_sem, h1s, h1r, h2s, h2r, ivs, ivr, lbs, lbr, nrs, nrr, frs, frr,
):
    xs, nrhs, comps = b_ref.shape
    k3 = res_ref.shape[1]
    na, _, nc3 = inv.shape
    per = inv_in.shape[0]
    groups = far.shape[1]
    packs = comps // k3
    part = nrhs // packs
    width = xs * comps
    me = tuple(lax.axis_index(a) for a in AXES)

    def at(offset):
        return {a: lax.rem(i + o, n) for a, i, o, n in zip(AXES, me, offset, sizes)}

    def across(bits):
        return {a: (i + 1 - 2 * lax.rem(i, 2)) if f else i for a, i, f in zip(AXES, me, bits)}

    def line(axis, o):
        return tuple(o if a == axis else 0 for a in range(3))

    halo_sends = []
    for a in (2, 1, 0):
        halo_sends.append((2 * a, line(a, sizes[a] - 1)))
        if sizes[a] > 2:
            halo_sends.append((2 * a + 1, line(a, 1)))
    near_sends = [bits for bits in itertools.product((0, 1), repeat=3) if any(bits)]
    near_sends.sort(key=lambda f: -(f[0] + f[2]))
    far_sends = [
        tuple(2 * o for o in offs)
        for offs in itertools.product(*(range(n // 2) for n in sizes))
        if any(offs)
    ]
    inv_sends = [line(2, o) for o in range(1, sizes[2])]

    barrier = pltpu.get_barrier_semaphore()
    offsets = sorted({o for _, o in halo_sends} | set(far_sends) | set(inv_sends))
    diagonals = [bits for bits in near_sends if sum(bits) > 1]
    offsets.sort(key=lambda o: o not in [h for _, h in halo_sends])
    for device in [at(o) for o in offsets] + [across(f) for f in diagonals]:
        pl.semaphore_signal(barrier, inc=1, device_id=device, device_id_type=MESH)

    mine = inv.at[pl.ds(me[2] * per, per)]
    loads = [
        pltpu.make_async_copy(src, dst, in_sem.at[i])
        for i, (src, dst) in enumerate(
            ((b_in, b_ref), (agg_in, agg_ref), (res_in, res_ref), (inv_in, mine))
        )
    ]
    copies = [
        pltpu.make_async_copy(sten_in.at[x], sten.at[x], sten_sem.at[x]) for x in range(xs)
    ]
    for c in loads + copies:
        c.start()

    pl.semaphore_wait(barrier, len(offsets) + len(diagonals))

    def remote(src, dst, send, recv, device):
        return pltpu.make_async_remote_copy(
            src_ref=src, dst_ref=dst, send_sem=send, recv_sem=recv,
            device_id=device, device_id_type=MESH,
        )

    def start_halo(src, halo, send, recv):
        out = [remote(src, halo.at[s], send.at[s], recv.at[s], at(o)) for s, o in halo_sends]
        for c in out:
            c.start()
        return out

    first = start_halo(b_in, halo1, h1s, h1r)

    for c in loads:
        c.wait()
    lab[0] = jnp.full(lab.shape[1:], agg_ref[0].astype(F32), F32)
    for x in range(xs):
        high, low = split(jnp.concatenate([res_ref[x]] * packs, axis=0))
        rp[pl.ds(0, comps), pl.ds(x * comps, comps)] = high
        rp[pl.ds(comps, comps), pl.ds(x * comps, comps)] = low
    early = [
        remote(mine, mine, ivs.at[i], ivr.at[i], at(o))
        for i, o in enumerate(inv_sends)
    ] + [
        remote(lab.at[0], lab.at[i + 1], lbs.at[i], lbr.at[i], at(o))
        for i, o in enumerate(far_sends)
    ]
    for c in early:
        c.start()

    inside = ((0,), (7, 8)) if xs == 2 else ((0,), (7,), (8,))
    sides, slots = [(), ()], [(), ()]
    for a in range(3):
        pair = ((1 + 2 * a,), (2 + 2 * a,))
        sides[a // 2] += pair if sizes[a] > 2 else (pair[0] + pair[1],)
        slots[a // 2] += (2 * a, 2 * a + 1) if sizes[a] > 2 else (2 * a,)

    for x in range(xs):
        copies[x].wait()
        for i, ks in enumerate(inside + sides[0] + sides[1]):
            high, low = split(sum(sten[x, k] for k in ks))
            cols = pl.ds(i * comps, comps)
            sw[x, pl.ds(0, comps), cols] = high
            sw[x, pl.ds(comps, comps), cols] = low

    def multiply(x, fields, begin):
        lhs = stack_split(jnp.concatenate(fields, axis=1))
        return dot_nt(lhs, sw[x, :, pl.ds(begin * comps, len(fields) * comps)])

    def local_part(field):
        out = []
        for x in range(xs):
            fields = [field[x], field[(x + 1) % xs]]
            if xs > 2:
                fields.append(field[(x + xs - 1) % xs])
            out.append(multiply(x, fields, 0))
        return out

    def halo_part(halo, base, sends):
        for group in range(2):
            for (slot, _), c in zip(halo_sends, sends):
                if slot in slots[group]:
                    c.wait_recv()
            begin = len(inside) + (len(sides[0]) if group else 0)
            base = [
                base[x] + multiply(x, [halo[i, x] for i in slots[group]], begin)
                for x in range(xs)
            ]
        return [fold(o) for o in base]

    lane = lax.broadcasted_iota(jnp.int32, (part, comps), 1)
    slot = lane // k3

    def pack(full):
        out = full[:part]
        for q in range(1, packs):
            out = jnp.where(slot == q, full[q * part : (q + 1) * part], out)
        return out

    def restricted(field):
        return pack(fold(dot_nt(stack_split(jnp.concatenate(field, axis=1)), rp[...])))

    ones = jnp.ones((16, comps), BF16)

    def products(*pairs):
        rows = [sum(u[x] * v[x] for x in range(xs)) for u, v in pairs]
        if len(rows) < packs:
            rows.append(jnp.zeros(((packs - len(rows)) * nrhs, comps), F32))
        high, low = split(jnp.concatenate(rows, axis=0))
        return (dot_nt(ones, high) + dot_nt(ones, low))[:1]

    def to_near(i, count):
        here = pl.ds(0, count)
        out = [
            remote(
                near.at[i, 0, here], near.at[i, j + 1, here], nrs.at[i, j], nrr.at[i, j], across(f)
            )
            for j, f in enumerate(near_sends)
        ]
        for c in out:
            c.start()
        return out

    def to_far(i, count, arriving):
        here = pl.ds(0, count)
        for c in arriving:
            c.wait_recv()
        total = near[i, 0, here]
        for j in range(len(near_sends)):
            total = total + near[i, j + 1, here]
        far[i, 0, here] = total
        out = [
            remote(far.at[i, 0, here], far.at[i, j + 1, here], frs.at[i, j], frr.at[i, j], at(o))
            for j, o in enumerate(far_sends)
        ]
        for c in out:
            c.start()
        return out

    bs = [b_ref[x] for x in range(xs)]
    base = local_part(bs)
    near[0, 0, pl.ds(0, part)] = restricted(bs)
    w1s = halo_part(halo1, base, first)
    for x in range(xs):
        w1[x] = w1s[x]
    second = start_halo(w1, halo2, h2s, h2r)

    base = local_part(w1s)
    near[0, 0, pl.ds(part, part)] = restricted(w1s)
    near[0, 0, pl.ds(2 * part, 1)] = products((w1s, w1s), (w1s, bs))
    near_e = to_near(0, 2 * part + 1)
    w2s = halo_part(halo2, base, second)
    near[1, 0, pl.ds(0, part)] = restricted(w2s)
    near[1, 0, pl.ds(part, 1)] = products((w1s, w2s), (w2s, w2s), (w2s, bs))
    near_l = to_near(1, part + 1)
    for x in range(xs):
        w2[x] = w2s[x]
    far_e = to_far(0, 2 * part + 1, near_e)

    for c in early:
        c.wait_recv()

    own = inv[agg_ref[0]]
    own_high, own_low = split(own)
    rows = lax.broadcasted_iota(jnp.int32, (comps, nc3), 0)
    cols = lax.broadcasted_iota(jnp.int32, (comps, nc3), 1)
    same = lax.rem(rows, k3) == lax.rem(cols, k3)
    block = (cols // k3).astype(F32)
    vec_high, vec_low = split(jnp.concatenate([res_ref[x] for x in range(xs)], axis=1))

    def prepare(g, carry):
        label = lab[g][0:1, 0:1]
        pick = jnp.where(same & (block == label), 1.0, 0.0).astype(BF16)
        weights = dot_nt(pick, own_high) + dot_nt(pick, own_low)
        high, low = split(weights)
        lift = dot_nn(high, vec_high) + (dot_nn(high, vec_low) + dot_nn(low, vec_high))
        high, low = split(lift)
        first_row = g * comps if isinstance(g, int) else pl.multiple_of(g * comps, comps)
        wr[pl.ds(first_row, comps), pl.ds(0, width)] = high
        wr[pl.ds(first_row, comps), pl.ds(width, width)] = low
        return carry

    loop(groups, prepare, 0)

    pair = 2 if groups % 2 == 0 else 1

    def unpack(packed):
        return jnp.concatenate([jnp.where(slot == q, packed, 0.0) for q in range(packs)], axis=0)

    def lift(i, count):
        def lift_step(h, acc):
            lhs = jnp.concatenate(
                [
                    jnp.concatenate(
                        [
                            unpack(far[i, h * pair + j, pl.ds(f * part, part)])
                            for f in range(count)
                        ],
                        axis=0,
                    )
                    for j in range(pair)
                ],
                axis=1,
            )
            rows = pair * comps
            first_row = h * rows if isinstance(h, int) else pl.multiple_of(h * rows, rows)
            return acc + dot_nn(stack_split(lhs), wr[pl.ds(first_row, rows), :])

        zero = jnp.zeros((2 * count * nrhs, 2 * width), F32)
        return fold(loop(groups // pair, lift_step, zero))

    far_l = to_far(1, part + 1, near_l)
    for c in first + early + second + near_e + near_l:
        c.wait_send()
    for c in far_e:
        c.wait_recv()
    lift_early = lift(0, 2)
    for c in far_l:
        c.wait_recv()
    lift_late = lift(1, 1)

    def add(g, acc):
        return acc[0] + far[0, g, pl.ds(2 * part, 1)], acc[1] + far[1, g, pl.ds(part, 1)]

    blank = jnp.zeros((1, comps), F32)
    square, corr = loop(groups, add, (blank, blank))
    cross = pltpu.roll(square, comps - nrhs, 1)
    square2 = pltpu.roll(corr, comps - nrhs, 1)
    cross2 = pltpu.roll(corr, comps - 2 * nrhs, 1)
    step = cross / square
    ratio = corr / square
    turn = (step * corr - cross2) / (square2 - ratio * corr)
    push = step + turn * ratio

    own_lane = lax.broadcasted_iota(jnp.int32, (nrhs, comps), 0) == lax.broadcasted_iota(
        jnp.int32, (nrhs, comps), 1
    )

    def spread(coef):
        column = jnp.where(own_lane, jnp.broadcast_to(coef, (nrhs, comps)), 0.0)
        return jnp.broadcast_to(jnp.sum(column, axis=1, keepdims=True), (nrhs, comps))

    push, turn = spread(push), spread(turn)
    for x in range(xs):
        cols = slice(x * comps, (x + 1) * comps)
        bx, ux, vx = b_ref[x], w1[x], w2[x]
        resid_ref[x] = bx - push * ux + turn * vx
        sol_ref[x] = (
            (push * bx - turn * ux)
            + lift_early[:nrhs, cols]
            - push * lift_early[nrhs:, cols]
            + turn * lift_late[:, cols]
        )
    for c in far_e + far_l:
        c.wait_send()


def finish(sol_ref, resid_ref, sol_out, resid_out, sem):
    out = [
        pltpu.make_async_copy(src, dst, sem.at[i])
        for i, (src, dst) in enumerate(((sol_ref, sol_out), (resid_ref, resid_out)))
    ]
    for c in out:
        c.start()
    for c in out:
        c.wait()


def body(sizes, right_side, stencil, restrict, aggregate, coarsest_inverse):
    shape = right_side.shape
    xs, nrhs, comps = shape[3:]
    k3 = restrict.shape[4]
    nc3 = coarsest_inverse.shape[1]
    na = nc3 // k3
    groups = (sizes[0] // 2) * (sizes[1] // 2) * (sizes[2] // 2)
    per = coarsest_inverse.shape[0] // k3
    part = nrhs * k3 // comps
    blocks = 9 - (xs == 2) - sum(n == 2 for n in sizes)
    vmem = pl.BlockSpec(memory_space=pltpu.VMEM)
    dma = pltpu.SemaphoreType.DMA
    field = jax.ShapeDtypeStruct((xs, nrhs, comps), F32)
    sol, resid = pl.pallas_call(
        functools.partial(kernel, sizes),
        out_shape=(field, field),
        in_specs=[pl.BlockSpec(memory_space=pltpu.HBM)] * 5,
        out_specs=(vmem, vmem),
        scratch_shapes=[
            pltpu.SMEM((xs,), jnp.int32),
            pltpu.VMEM((xs, nrhs, comps), F32),
            pltpu.VMEM((xs, k3, comps), F32),
            dma((4,)),
            pltpu.VMEM((xs, 9, comps, comps), F32),
            pltpu.VMEM((xs, 2 * comps, blocks * comps), BF16),
            pltpu.VMEM((2 * comps, xs * comps), BF16),
            pltpu.VMEM((6, xs, nrhs, comps), F32),
            pltpu.VMEM((6, xs, nrhs, comps), F32),
            pltpu.VMEM((xs, nrhs, comps), F32),
            pltpu.VMEM((xs, nrhs, comps), F32),
            pltpu.VMEM((na, k3, nc3), F32),
            pltpu.VMEM((groups, 8, comps), F32),
            pltpu.VMEM((groups * comps, 2 * xs * comps), BF16),
            pltpu.VMEM((2, 8, 3 * part, comps), F32),
            pltpu.VMEM((2, groups, 3 * part, comps), F32),
            dma((xs,)),
            dma((6,)), dma((6,)), dma((6,)), dma((6,)),
            dma((sizes[2],)), dma((sizes[2],)),
            dma((groups,)), dma((groups,)),
            dma((2, 7)), dma((2, 7)), dma((2, groups)), dma((2, groups)),
        ],
        compiler_params=pltpu.CompilerParams(
            collective_id=0,
            has_side_effects=True,
            vmem_limit_bytes=(16 if groups <= 8 else 48) * 2**20,
        ),
    )(
        *(
            pltpu.with_memory_space_constraint(a, pltpu.HBM)
            for a in (
                aggregate.reshape(xs),
                right_side.reshape(xs, nrhs, comps),
                stencil.reshape(xs, 9, comps, comps),
                restrict.reshape(xs, k3, comps),
                coarsest_inverse.reshape(per, k3, nc3),
            )
        )
    )
    sol, resid = pl.pallas_call(
        finish,
        out_shape=(field, field),
        in_specs=[vmem, vmem],
        out_specs=[pl.BlockSpec(memory_space=pl.ANY)] * 2,
        scratch_shapes=[dma((2,))],
        compiler_params=pltpu.CompilerParams(vmem_limit_bytes=2**20),
    )(sol, resid)
    return sol.reshape(shape), resid.reshape(shape)


def solution(mesh):
    sizes = tuple(mesh.shape[a] for a in AXES)
    return jax.shard_map(
        functools.partial(body, sizes),
        mesh=mesh,
        in_specs=(
            P("ta", "gz", "xy", None, None, None),
            P("ta", "gz", "xy", None, None, None, None),
            P("ta", "gz", "xy", None, None, None),
            P("ta", "gz", "xy", None),
            P("xy", None),
        ),
        out_specs=(P("ta", "gz", "xy", None, None, None), P("ta", "gz", "xy", None, None, None)),
        check_vma=False,
    )
```

```python
import functools
import itertools

import jax
import jax.numpy as jnp
from jax import lax
from jax.experimental import pallas as pl
from jax.experimental.pallas import tpu as pltpu
from jax.sharding import PartitionSpec as P

AXES = ("ta", "gz", "xy")
F32 = jnp.float32
BF16 = jnp.bfloat16
MESH = pl.DeviceIdType.MESH


def split(x):
    high = x.astype(BF16)
    return high, (x - high.astype(F32)).astype(BF16)


def dot_nt(a, b):
    return lax.dot_general(a, b, (((1,), (1,)), ((), ())), preferred_element_type=F32)


def dot_nn(a, b):
    return lax.dot_general(a, b, (((1,), (0,)), ((), ())), preferred_element_type=F32)


def stack_split(x):
    return jnp.concatenate(split(x), axis=0)


def fold(o):
    r, n = o.shape[0] // 2, o.shape[1] // 2
    return o[:r, :n] + (o[:r, n:] + o[r:, :n])


def loop(n, step, init, most=8):
    if n <= most:
        for i in range(n):
            init = step(i, init)
        return init
    return lax.fori_loop(0, n, step, init)


def kernel(
    sizes, agg_in, b_in, sten_in, res_in, inv_in, sol_ref, resid_ref,
    agg_ref, b_ref, res_ref, in_sem, sten, sw, rp, halo1, halo2, w1, w2, inv, lab, wr, near, far,
    sten_sem, h1s, h1r, h2s, h2r, ivs, ivr, lbs, lbr, nrs, nrr, frs, frr,
):
    xs, nrhs, comps = b_ref.shape
    k3 = res_ref.shape[1]
    na, _, nc3 = inv.shape
    per = inv_in.shape[0]
    groups = far.shape[1]
    packs = comps // k3
    part = nrhs // packs
    width = xs * comps
    me = tuple(lax.axis_index(a) for a in AXES)

    def at(offset):
        return {a: lax.rem(i + o, n) for a, i, o, n in zip(AXES, me, offset, sizes)}

    def across(bits):
        return {a: (i + 1 - 2 * lax.rem(i, 2)) if f else i for a, i, f in zip(AXES, me, bits)}

    def line(axis, o):
        return tuple(o if a == axis else 0 for a in range(3))

    halo_sends = []
    for a in (2, 1, 0):
        halo_sends.append((2 * a, line(a, sizes[a] - 1)))
        if sizes[a] > 2:
            halo_sends.append((2 * a + 1, line(a, 1)))
    near_sends = [bits for bits in itertools.product((0, 1), repeat=3) if any(bits)]
    near_sends.sort(key=lambda f: -(f[0] + f[2]))
    far_sends = [
        tuple(2 * o for o in offs)
        for offs in itertools.product(*(range(n // 2) for n in sizes))
        if any(offs)
    ]
    inv_sends = [line(2, o) for o in range(1, sizes[2])]

    barrier = pltpu.get_barrier_semaphore()
    offsets = sorted({o for _, o in halo_sends} | set(far_sends) | set(inv_sends))
    diagonals = [bits for bits in near_sends if sum(bits) > 1]
    offsets.sort(key=lambda o: o not in [h for _, h in halo_sends])
    for device in [at(o) for o in offsets] + [across(f) for f in diagonals]:
        pl.semaphore_signal(barrier, inc=1, device_id=device, device_id_type=MESH)

    mine = inv.at[pl.ds(me[2] * per, per)]
    loads = [
        pltpu.make_async_copy(src, dst, in_sem.at[i])
        for i, (src, dst) in enumerate(
            ((b_in, b_ref), (agg_in, agg_ref), (res_in, res_ref), (inv_in, mine))
        )
    ]
    copies = [
        pltpu.make_async_copy(sten_in.at[x], sten.at[x], sten_sem.at[x]) for x in range(xs)
    ]
    for c in loads + copies:
        c.start()

    pl.semaphore_wait(barrier, len(offsets) + len(diagonals))

    def remote(src, dst, send, recv, device):
        return pltpu.make_async_remote_copy(
            src_ref=src, dst_ref=dst, send_sem=send, recv_sem=recv,
            device_id=device, device_id_type=MESH,
        )

    def start_halo(src, halo, send, recv):
        out = [remote(src, halo.at[s], send.at[s], recv.at[s], at(o)) for s, o in halo_sends]
        for c in out:
            c.start()
        return out

    first = start_halo(b_in, halo1, h1s, h1r)

    for c in loads:
        c.wait()
    lab[0] = jnp.full(lab.shape[1:], agg_ref[0].astype(F32), F32)
    for x in range(xs):
        high, low = split(jnp.transpose(jnp.concatenate([res_ref[x]] * packs, axis=0)))
        rp[pl.ds(x * comps, comps), pl.ds(0, comps)] = high
        rp[pl.ds(x * comps, comps), pl.ds(comps, comps)] = low
    early = [
        remote(mine, mine, ivs.at[i], ivr.at[i], at(o))
        for i, o in enumerate(inv_sends)
    ] + [
        remote(lab.at[0], lab.at[i + 1], lbs.at[i], lbr.at[i], at(o))
        for i, o in enumerate(far_sends)
    ]
    for c in early:
        c.start()

    inside = ((0,), (7, 8)) if xs == 2 else ((0,), (7,), (8,))
    sides, slots = [(), ()], [(), ()]
    for a in range(3):
        pair = ((1 + 2 * a,), (2 + 2 * a,))
        sides[a // 2] += pair if sizes[a] > 2 else (pair[0] + pair[1],)
        slots[a // 2] += (2 * a, 2 * a + 1) if sizes[a] > 2 else (2 * a,)

    for x in range(xs):
        copies[x].wait()
        for i, ks in enumerate(inside + sides[0] + sides[1]):
            high, low = split(jnp.transpose(sum(sten[x, k] for k in ks)))
            rows = pl.ds(i * comps, comps)
            sw[x, rows, pl.ds(0, comps)] = high
            sw[x, rows, pl.ds(comps, comps)] = low

    def multiply(x, fields, begin):
        lhs = stack_split(jnp.concatenate(fields, axis=1))
        return dot_nn(lhs, sw[x, pl.ds(begin * comps, len(fields) * comps), :])

    def local_part(field):
        out = []
        for x in range(xs):
            fields = [field[x], field[(x + 1) % xs]]
            if xs > 2:
                fields.append(field[(x + xs - 1) % xs])
            out.append(multiply(x, fields, 0))
        return out

    def halo_part(halo, base, sends):
        for group in range(2):
            for (slot, _), c in zip(halo_sends, sends):
                if slot in slots[group]:
                    c.wait_recv()
            begin = len(inside) + (len(sides[0]) if group else 0)
            base = [
                base[x] + multiply(x, [halo[i, x] for i in slots[group]], begin)
                for x in range(xs)
            ]
        return [fold(o) for o in base]

    lane = lax.broadcasted_iota(jnp.int32, (part, comps), 1)
    slot = lane // k3

    def pack(full):
        out = full[:part]
        for q in range(1, packs):
            out = jnp.where(slot == q, full[q * part : (q + 1) * part], out)
        return out

    def restricted(field):
        return pack(fold(dot_nn(stack_split(jnp.concatenate(field, axis=1)), rp[...])))

    def products(*pairs):
        rows = [sum(u[x] * v[x] for x in range(xs)) for u, v in pairs]
        if len(rows) < packs:
            rows.append(jnp.zeros(((packs - len(rows)) * nrhs, comps), F32))
        return jnp.sum(jnp.transpose(jnp.concatenate(rows, axis=0)), axis=0, keepdims=True)

    def to_near(i, count):
        here = pl.ds(0, count)
        out = [
            remote(
                near.at[i, 0, here], near.at[i, j + 1, here], nrs.at[i, j], nrr.at[i, j], across(f)
            )
            for j, f in enumerate(near_sends)
        ]
        for c in out:
            c.start()
        return out

    def to_far(i, count, arriving):
        here = pl.ds(0, count)
        for c in arriving:
            c.wait_recv()
        total = near[i, 0, here]
        for j in range(len(near_sends)):
            total = total + near[i, j + 1, here]
        far[i, 0, here] = total
        out = [
            remote(far.at[i, 0, here], far.at[i, j + 1, here], frs.at[i, j], frr.at[i, j], at(o))
            for j, o in enumerate(far_sends)
        ]
        for c in out:
            c.start()
        return out

    bs = [b_ref[x] for x in range(xs)]
    base = local_part(bs)
    near[0, 0, pl.ds(0, part)] = restricted(bs)
    w1s = halo_part(halo1, base, first)
    for x in range(xs):
        w1[x] = w1s[x]
    second = start_halo(w1, halo2, h2s, h2r)

    base = local_part(w1s)
    near[0, 0, pl.ds(part, part)] = restricted(w1s)
    near[0, 0, pl.ds(2 * part, 1)] = products((w1s, w1s), (w1s, bs))
    near_e = to_near(0, 2 * part + 1)
    w2s = halo_part(halo2, base, second)
    near[1, 0, pl.ds(0, part)] = restricted(w2s)
    near[1, 0, pl.ds(part, 1)] = products((w1s, w2s), (w2s, w2s), (w2s, bs))
    near_l = to_near(1, part + 1)
    for x in range(xs):
        w2[x] = w2s[x]
    far_e = to_far(0, 2 * part + 1, near_e)

    for c in early:
        c.wait_recv()

    own = inv[agg_ref[0]]
    own_high, own_low = split(own)
    rows = lax.broadcasted_iota(jnp.int32, (comps, nc3), 0)
    cols = lax.broadcasted_iota(jnp.int32, (comps, nc3), 1)
    same = lax.rem(rows, k3) == lax.rem(cols, k3)
    block = (cols // k3).astype(F32)
    vec_high, vec_low = split(jnp.concatenate([res_ref[x] for x in range(xs)], axis=1))

    def prepare(g, carry):
        label = lab[g][0:1, 0:1]
        pick = jnp.where(same & (block == label), 1.0, 0.0).astype(BF16)
        weights = dot_nt(pick, own_high) + dot_nt(pick, own_low)
        high, low = split(weights)
        lift = dot_nn(high, vec_high) + (dot_nn(high, vec_low) + dot_nn(low, vec_high))
        high, low = split(lift)
        first_row = g * comps if isinstance(g, int) else pl.multiple_of(g * comps, comps)
        wr[pl.ds(first_row, comps), pl.ds(0, width)] = high
        wr[pl.ds(first_row, comps), pl.ds(width, width)] = low
        return carry

    loop(groups, prepare, 0)

    pair = 2 if groups % 2 == 0 else 1

    def unpack(packed):
        return jnp.concatenate([jnp.where(slot == q, packed, 0.0) for q in range(packs)], axis=0)

    def lift(i, count):
        def lift_step(h, acc):
            lhs = jnp.concatenate(
                [
                    jnp.concatenate(
                        [
                            unpack(far[i, h * pair + j, pl.ds(f * part, part)])
                            for f in range(count)
                        ],
                        axis=0,
                    )
                    for j in range(pair)
                ],
                axis=1,
            )
            rows = pair * comps
            first_row = h * rows if isinstance(h, int) else pl.multiple_of(h * rows, rows)
            return acc + dot_nn(stack_split(lhs), wr[pl.ds(first_row, rows), :])

        zero = jnp.zeros((2 * count * nrhs, 2 * width), F32)
        return fold(loop(groups // pair, lift_step, zero))

    far_l = to_far(1, part + 1, near_l)
    for c in first + early + second + near_e + near_l:
        c.wait_send()
    for c in far_e:
        c.wait_recv()
    lift_early = lift(0, 2)
    for c in far_l:
        c.wait_recv()
    lift_late = lift(1, 1)

    def add(g, acc):
        return acc[0] + far[0, g, pl.ds(2 * part, 1)], acc[1] + far[1, g, pl.ds(part, 1)]

    blank = jnp.zeros((1, comps), F32)
    square, corr = loop(groups, add, (blank, blank))
    cross = pltpu.roll(square, comps - nrhs, 1)
    square2 = pltpu.roll(corr, comps - nrhs, 1)
    cross2 = pltpu.roll(corr, comps - 2 * nrhs, 1)
    step = cross / square
    ratio = corr / square
    turn = (step * corr - cross2) / (square2 - ratio * corr)
    push = step + turn * ratio

    own_lane = lax.broadcasted_iota(jnp.int32, (nrhs, comps), 0) == lax.broadcasted_iota(
        jnp.int32, (nrhs, comps), 1
    )

    def spread(coef):
        column = jnp.where(own_lane, jnp.broadcast_to(coef, (nrhs, comps)), 0.0)
        return jnp.broadcast_to(jnp.sum(column, axis=1, keepdims=True), (nrhs, comps))

    push, turn = spread(push), spread(turn)
    for x in range(xs):
        cols = slice(x * comps, (x + 1) * comps)
        bx, ux, vx = b_ref[x], w1[x], w2[x]
        resid_ref[x] = bx - push * ux + turn * vx
        sol_ref[x] = (
            (push * bx - turn * ux)
            + lift_early[:nrhs, cols]
            - push * lift_early[nrhs:, cols]
            + turn * lift_late[:, cols]
        )
    for c in far_e + far_l:
        c.wait_send()


def finish(sol_ref, resid_ref, sol_out, resid_out, sem):
    out = [
        pltpu.make_async_copy(src, dst, sem.at[i])
        for i, (src, dst) in enumerate(((sol_ref, sol_out), (resid_ref, resid_out)))
    ]
    for c in out:
        c.start()
    for c in out:
        c.wait()


def body(sizes, right_side, stencil, restrict, aggregate, coarsest_inverse):
    shape = right_side.shape
    xs, nrhs, comps = shape[3:]
    k3 = restrict.shape[4]
    nc3 = coarsest_inverse.shape[1]
    na = nc3 // k3
    groups = (sizes[0] // 2) * (sizes[1] // 2) * (sizes[2] // 2)
    per = coarsest_inverse.shape[0] // k3
    part = nrhs * k3 // comps
    blocks = 9 - (xs == 2) - sum(n == 2 for n in sizes)
    vmem = pl.BlockSpec(memory_space=pltpu.VMEM)
    dma = pltpu.SemaphoreType.DMA
    field = jax.ShapeDtypeStruct((xs, nrhs, comps), F32)
    sol, resid = pl.pallas_call(
        functools.partial(kernel, sizes),
        out_shape=(field, field),
        in_specs=[pl.BlockSpec(memory_space=pltpu.HBM)] * 5,
        out_specs=(vmem, vmem),
        scratch_shapes=[
            pltpu.SMEM((xs,), jnp.int32),
            pltpu.VMEM((xs, nrhs, comps), F32),
            pltpu.VMEM((xs, k3, comps), F32),
            dma((4,)),
            pltpu.VMEM((xs, 9, comps, comps), F32),
            pltpu.VMEM((xs, blocks * comps, 2 * comps), BF16),
            pltpu.VMEM((xs * comps, 2 * comps), BF16),
            pltpu.VMEM((6, xs, nrhs, comps), F32),
            pltpu.VMEM((6, xs, nrhs, comps), F32),
            pltpu.VMEM((xs, nrhs, comps), F32),
            pltpu.VMEM((xs, nrhs, comps), F32),
            pltpu.VMEM((na, k3, nc3), F32),
            pltpu.VMEM((groups, 8, comps), F32),
            pltpu.VMEM((groups * comps, 2 * xs * comps), BF16),
            pltpu.VMEM((2, 8, 3 * part, comps), F32),
            pltpu.VMEM((2, groups, 3 * part, comps), F32),
            dma((xs,)),
            dma((6,)), dma((6,)), dma((6,)), dma((6,)),
            dma((sizes[2],)), dma((sizes[2],)),
            dma((groups,)), dma((groups,)),
            dma((2, 7)), dma((2, 7)), dma((2, groups)), dma((2, groups)),
        ],
        compiler_params=pltpu.CompilerParams(
            collective_id=0,
            has_side_effects=True,
            vmem_limit_bytes=(16 if groups <= 8 else 48) * 2**20,
        ),
    )(
        *(
            pltpu.with_memory_space_constraint(a, pltpu.HBM)
            for a in (
                aggregate.reshape(xs),
                right_side.reshape(xs, nrhs, comps),
                stencil.reshape(xs, 9, comps, comps),
                restrict.reshape(xs, k3, comps),
                coarsest_inverse.reshape(per, k3, nc3),
            )
        )
    )
    sol, resid = pl.pallas_call(
        finish,
        out_shape=(field, field),
        in_specs=[vmem, vmem],
        out_specs=[pl.BlockSpec(memory_space=pl.ANY)] * 2,
        scratch_shapes=[dma((2,))],
        compiler_params=pltpu.CompilerParams(vmem_limit_bytes=2**20),
    )(sol, resid)
    return sol.reshape(shape), resid.reshape(shape)


def solution(mesh):
    sizes = tuple(mesh.shape[a] for a in AXES)
    return jax.shard_map(
        functools.partial(body, sizes),
        mesh=mesh,
        in_specs=(
            P("ta", "gz", "xy", None, None, None),
            P("ta", "gz", "xy", None, None, None, None),
            P("ta", "gz", "xy", None, None, None),
            P("ta", "gz", "xy", None),
            P("xy", None),
        ),
        out_specs=(P("ta", "gz", "xy", None, None, None), P("ta", "gz", "xy", None, None, None)),
        check_vma=False,
    )
```

```python
import functools
import itertools

import jax
import jax.numpy as jnp
from jax import lax
from jax.experimental import pallas as pl
from jax.experimental.pallas import tpu as pltpu
from jax.sharding import PartitionSpec as P

AXES = ("ta", "gz", "xy")
F32 = jnp.float32
BF16 = jnp.bfloat16
MESH = pl.DeviceIdType.MESH


def split(x):
    high = x.astype(BF16)
    return high, (x - high.astype(F32)).astype(BF16)


def dot_nt(a, b):
    return lax.dot_general(a, b, (((1,), (1,)), ((), ())), preferred_element_type=F32)


def dot_nn(a, b):
    return lax.dot_general(a, b, (((1,), (0,)), ((), ())), preferred_element_type=F32)


def stack_split(x):
    return jnp.concatenate(split(x), axis=0)


def fold(o):
    r, n = o.shape[0] // 2, o.shape[1] // 2
    return o[:r, :n] + (o[:r, n:] + o[r:, :n])


def loop(n, step, init, most=8):
    if n <= most:
        for i in range(n):
            init = step(i, init)
        return init
    return lax.fori_loop(0, n, step, init)


def kernel(
    sizes, agg_in, b_in, sten_in, res_in, inv_in, sol_ref, resid_ref,
    agg_ref, b_ref, res_ref, in_sem, sten, sw, rp, halo1, halo2, w1, w2, inv, lab, wr, near, far,
    sten_sem, h1s, h1r, h2s, h2r, ivs, ivr, lbs, lbr, nrs, nrr, frs, frr,
):
    xs, nrhs, comps = b_ref.shape
    k3 = res_ref.shape[1]
    na, _, nc3 = inv.shape
    per = inv_in.shape[0]
    groups = far.shape[1]
    packs = comps // k3
    part = nrhs // packs
    width = xs * comps
    me = tuple(lax.axis_index(a) for a in AXES)

    def at(offset):
        return {a: lax.rem(i + o, n) for a, i, o, n in zip(AXES, me, offset, sizes)}

    def across(bits):
        return {a: (i + 1 - 2 * lax.rem(i, 2)) if f else i for a, i, f in zip(AXES, me, bits)}

    def line(axis, o):
        return tuple(o if a == axis else 0 for a in range(3))

    halo_sends = []
    for a in (2, 1, 0):
        halo_sends.append((2 * a, line(a, sizes[a] - 1)))
        if sizes[a] > 2:
            halo_sends.append((2 * a + 1, line(a, 1)))
    near_sends = [bits for bits in itertools.product((0, 1), repeat=3) if any(bits)]
    near_sends.sort(key=lambda f: -(f[0] + f[2]))
    far_sends = [
        tuple(2 * o for o in offs)
        for offs in itertools.product(*(range(n // 2) for n in sizes))
        if any(offs)
    ]
    inv_sends = [line(2, o) for o in range(1, sizes[2])]

    barrier = pltpu.get_barrier_semaphore()
    offsets = sorted({o for _, o in halo_sends} | set(far_sends) | set(inv_sends))
    diagonals = [bits for bits in near_sends if sum(bits) > 1]
    offsets.sort(key=lambda o: o not in [h for _, h in halo_sends])
    for device in [at(o) for o in offsets] + [across(f) for f in diagonals]:
        pl.semaphore_signal(barrier, inc=1, device_id=device, device_id_type=MESH)

    mine = inv.at[pl.ds(me[2] * per, per)]
    loads = [
        pltpu.make_async_copy(src, dst, in_sem.at[i])
        for i, (src, dst) in enumerate(
            ((b_in, b_ref), (agg_in, agg_ref), (res_in, res_ref), (inv_in, mine))
        )
    ]
    copies = [
        pltpu.make_async_copy(sten_in.at[x], sten.at[x], sten_sem.at[x]) for x in range(xs)
    ]
    for c in loads + copies:
        c.start()

    pl.semaphore_wait(barrier, len(offsets) + len(diagonals))

    def remote(src, dst, send, recv, device):
        return pltpu.make_async_remote_copy(
            src_ref=src, dst_ref=dst, send_sem=send, recv_sem=recv,
            device_id=device, device_id_type=MESH,
        )

    def start_halo(src, halo, send, recv):
        out = [remote(src, halo.at[s], send.at[s], recv.at[s], at(o)) for s, o in halo_sends]
        for c in out:
            c.start()
        return out

    first = start_halo(b_in, halo1, h1s, h1r)

    for c in loads:
        c.wait()
    lab[0] = jnp.full(lab.shape[1:], agg_ref[0].astype(F32), F32)
    for x in range(xs):
        high, low = split(jnp.transpose(jnp.concatenate([res_ref[x]] * packs, axis=0)))
        rp[pl.ds(x * comps, comps), pl.ds(0, comps)] = high
        rp[pl.ds(x * comps, comps), pl.ds(comps, comps)] = low
    early = [
        remote(lab.at[0], lab.at[i + 1], lbs.at[i], lbr.at[i], at(o))
        for i, o in enumerate(far_sends)
    ]
    for c in early:
        c.start()

    inside = ((0,), (7, 8)) if xs == 2 else ((0,), (7,), (8,))
    sides, slots = [(), ()], [(), ()]
    for a in range(3):
        pair = ((1 + 2 * a,), (2 + 2 * a,))
        sides[a // 2] += pair if sizes[a] > 2 else (pair[0] + pair[1],)
        slots[a // 2] += (2 * a, 2 * a + 1) if sizes[a] > 2 else (2 * a,)

    for x in range(xs):
        copies[x].wait()
        for i, ks in enumerate(inside + sides[0] + sides[1]):
            high, low = split(jnp.transpose(sum(sten[x, k] for k in ks)))
            rows = pl.ds(i * comps, comps)
            sw[x, rows, pl.ds(0, comps)] = high
            sw[x, rows, pl.ds(comps, comps)] = low

    def multiply(x, fields, begin):
        lhs = stack_split(jnp.concatenate(fields, axis=1))
        return dot_nn(lhs, sw[x, pl.ds(begin * comps, len(fields) * comps), :])

    def local_part(field):
        out = []
        for x in range(xs):
            fields = [field[x], field[(x + 1) % xs]]
            if xs > 2:
                fields.append(field[(x + xs - 1) % xs])
            out.append(multiply(x, fields, 0))
        return out

    def halo_part(halo, base, sends):
        for group in range(2):
            for (slot, _), c in zip(halo_sends, sends):
                if slot in slots[group]:
                    c.wait_recv()
            begin = len(inside) + (len(sides[0]) if group else 0)
            base = [
                base[x] + multiply(x, [halo[i, x] for i in slots[group]], begin)
                for x in range(xs)
            ]
        return [fold(o) for o in base]

    lane = lax.broadcasted_iota(jnp.int32, (part, comps), 1)
    slot = lane // k3

    def pack(full):
        out = full[:part]
        for q in range(1, packs):
            out = jnp.where(slot == q, full[q * part : (q + 1) * part], out)
        return out

    def restricted(field):
        return pack(fold(dot_nn(stack_split(jnp.concatenate(field, axis=1)), rp[...])))

    def products(*pairs):
        rows = [sum(u[x] * v[x] for x in range(xs)) for u, v in pairs]
        if len(rows) < packs:
            rows.append(jnp.zeros(((packs - len(rows)) * nrhs, comps), F32))
        return jnp.sum(jnp.transpose(jnp.concatenate(rows, axis=0)), axis=0, keepdims=True)

    def to_near(i, count):
        here = pl.ds(0, count)
        out = [
            remote(
                near.at[i, 0, here], near.at[i, j + 1, here], nrs.at[i, j], nrr.at[i, j], across(f)
            )
            for j, f in enumerate(near_sends)
        ]
        for c in out:
            c.start()
        return out

    def to_far(i, count, arriving):
        here = pl.ds(0, count)
        for c in arriving:
            c.wait_recv()
        total = near[i, 0, here]
        for j in range(len(near_sends)):
            total = total + near[i, j + 1, here]
        far[i, 0, here] = total
        out = [
            remote(far.at[i, 0, here], far.at[i, j + 1, here], frs.at[i, j], frr.at[i, j], at(o))
            for j, o in enumerate(far_sends)
        ]
        for c in out:
            c.start()
        return out

    bs = [b_ref[x] for x in range(xs)]
    base = local_part(bs)
    near[0, 0, pl.ds(0, part)] = restricted(bs)
    w1s = halo_part(halo1, base, first)
    for x in range(xs):
        w1[x] = w1s[x]
    second = start_halo(w1, halo2, h2s, h2r)

    base = local_part(w1s)
    near[0, 0, pl.ds(part, part)] = restricted(w1s)
    near[0, 0, pl.ds(2 * part, 1)] = products((w1s, w1s), (w1s, bs))
    near_e = to_near(0, 2 * part + 1)
    w2s = halo_part(halo2, base, second)
    near[1, 0, pl.ds(0, part)] = restricted(w2s)
    near[1, 0, pl.ds(part, 1)] = products((w1s, w2s), (w2s, w2s), (w2s, bs))
    near_l = to_near(1, part + 1)
    gather = [
        remote(mine, mine, ivs.at[i], ivr.at[i], at(o)) for i, o in enumerate(inv_sends)
    ]
    for c in gather:
        c.start()
    for x in range(xs):
        w2[x] = w2s[x]
    far_e = to_far(0, 2 * part + 1, near_e)

    pair = 2 if groups % 2 == 0 else 1

    def unpack(packed):
        return jnp.concatenate([jnp.where(slot == q, packed, 0.0) for q in range(packs)], axis=0)

    def lift(i, count):
        def lift_step(h, acc):
            lhs = jnp.concatenate(
                [
                    jnp.concatenate(
                        [
                            unpack(far[i, h * pair + j, pl.ds(f * part, part)])
                            for f in range(count)
                        ],
                        axis=0,
                    )
                    for j in range(pair)
                ],
                axis=1,
            )
            rows = pair * comps
            first_row = h * rows if isinstance(h, int) else pl.multiple_of(h * rows, rows)
            return acc + dot_nn(stack_split(lhs), wr[pl.ds(first_row, rows), :])

        zero = jnp.zeros((2 * count * nrhs, 2 * width), F32)
        return fold(loop(groups // pair, lift_step, zero))

    far_l = to_far(1, part + 1, near_l)
    for c in early + gather:
        c.wait_recv()

    own = inv[agg_ref[0]]
    own_high, own_low = split(own)
    rows = lax.broadcasted_iota(jnp.int32, (comps, nc3), 0)
    cols = lax.broadcasted_iota(jnp.int32, (comps, nc3), 1)
    same = lax.rem(rows, k3) == lax.rem(cols, k3)
    block = (cols // k3).astype(F32)
    vec_high, vec_low = split(jnp.concatenate([res_ref[x] for x in range(xs)], axis=1))

    def prepare(g, carry):
        label = lab[g][0:1, 0:1]
        pick = jnp.where(same & (block == label), 1.0, 0.0).astype(BF16)
        weights = dot_nt(pick, own_high) + dot_nt(pick, own_low)
        high, low = split(weights)
        lift = dot_nn(high, vec_high) + (dot_nn(high, vec_low) + dot_nn(low, vec_high))
        high, low = split(lift)
        first_row = g * comps if isinstance(g, int) else pl.multiple_of(g * comps, comps)
        wr[pl.ds(first_row, comps), pl.ds(0, width)] = high
        wr[pl.ds(first_row, comps), pl.ds(width, width)] = low
        return carry

    loop(groups, prepare, 0)

    for c in first + early + gather + second + near_e + near_l:
        c.wait_send()
    for c in far_e:
        c.wait_recv()
    lift_early = lift(0, 2)
    for c in far_l:
        c.wait_recv()
    lift_late = lift(1, 1)

    def add(g, acc):
        return acc[0] + far[0, g, pl.ds(2 * part, 1)], acc[1] + far[1, g, pl.ds(part, 1)]

    blank = jnp.zeros((1, comps), F32)
    square, corr = loop(groups, add, (blank, blank))
    cross = pltpu.roll(square, comps - nrhs, 1)
    square2 = pltpu.roll(corr, comps - nrhs, 1)
    cross2 = pltpu.roll(corr, comps - 2 * nrhs, 1)
    step = cross / square
    ratio = corr / square
    turn = (step * corr - cross2) / (square2 - ratio * corr)
    push = step + turn * ratio

    own_lane = lax.broadcasted_iota(jnp.int32, (nrhs, comps), 0) == lax.broadcasted_iota(
        jnp.int32, (nrhs, comps), 1
    )

    def spread(coef):
        column = jnp.where(own_lane, jnp.broadcast_to(coef, (nrhs, comps)), 0.0)
        return jnp.broadcast_to(jnp.sum(column, axis=1, keepdims=True), (nrhs, comps))

    push, turn = spread(push), spread(turn)
    for x in range(xs):
        cols = slice(x * comps, (x + 1) * comps)
        bx, ux, vx = b_ref[x], w1[x], w2[x]
        resid_ref[x] = bx - push * ux + turn * vx
        sol_ref[x] = (
            (push * bx - turn * ux)
            + lift_early[:nrhs, cols]
            - push * lift_early[nrhs:, cols]
            + turn * lift_late[:, cols]
        )
    for c in far_e + far_l:
        c.wait_send()


def finish(sol_ref, resid_ref, sol_out, resid_out, sem):
    out = [
        pltpu.make_async_copy(src, dst, sem.at[i])
        for i, (src, dst) in enumerate(((sol_ref, sol_out), (resid_ref, resid_out)))
    ]
    for c in out:
        c.start()
    for c in out:
        c.wait()


def body(sizes, right_side, stencil, restrict, aggregate, coarsest_inverse):
    shape = right_side.shape
    xs, nrhs, comps = shape[3:]
    k3 = restrict.shape[4]
    nc3 = coarsest_inverse.shape[1]
    na = nc3 // k3
    groups = (sizes[0] // 2) * (sizes[1] // 2) * (sizes[2] // 2)
    per = coarsest_inverse.shape[0] // k3
    part = nrhs * k3 // comps
    blocks = 9 - (xs == 2) - sum(n == 2 for n in sizes)
    vmem = pl.BlockSpec(memory_space=pltpu.VMEM)
    dma = pltpu.SemaphoreType.DMA
    field = jax.ShapeDtypeStruct((xs, nrhs, comps), F32)
    sol, resid = pl.pallas_call(
        functools.partial(kernel, sizes),
        out_shape=(field, field),
        in_specs=[pl.BlockSpec(memory_space=pltpu.HBM)] * 5,
        out_specs=(vmem, vmem),
        scratch_shapes=[
            pltpu.SMEM((xs,), jnp.int32),
            pltpu.VMEM((xs, nrhs, comps), F32),
            pltpu.VMEM((xs, k3, comps), F32),
            dma((4,)),
            pltpu.VMEM((xs, 9, comps, comps), F32),
            pltpu.VMEM((xs, blocks * comps, 2 * comps), BF16),
            pltpu.VMEM((xs * comps, 2 * comps), BF16),
            pltpu.VMEM((6, xs, nrhs, comps), F32),
            pltpu.VMEM((6, xs, nrhs, comps), F32),
            pltpu.VMEM((xs, nrhs, comps), F32),
            pltpu.VMEM((xs, nrhs, comps), F32),
            pltpu.VMEM((na, k3, nc3), F32),
            pltpu.VMEM((groups, 8, comps), F32),
            pltpu.VMEM((groups * comps, 2 * xs * comps), BF16),
            pltpu.VMEM((2, 8, 3 * part, comps), F32),
            pltpu.VMEM((2, groups, 3 * part, comps), F32),
            dma((xs,)),
            dma((6,)), dma((6,)), dma((6,)), dma((6,)),
            dma((sizes[2],)), dma((sizes[2],)),
            dma((groups,)), dma((groups,)),
            dma((2, 7)), dma((2, 7)), dma((2, groups)), dma((2, groups)),
        ],
        compiler_params=pltpu.CompilerParams(
            collective_id=0,
            has_side_effects=True,
            vmem_limit_bytes=(16 if groups <= 8 else 48) * 2**20,
        ),
    )(
        *(
            pltpu.with_memory_space_constraint(a, pltpu.HBM)
            for a in (
                aggregate.reshape(xs),
                right_side.reshape(xs, nrhs, comps),
                stencil.reshape(xs, 9, comps, comps),
                restrict.reshape(xs, k3, comps),
                coarsest_inverse.reshape(per, k3, nc3),
            )
        )
    )
    sol, resid = pl.pallas_call(
        finish,
        out_shape=(field, field),
        in_specs=[vmem, vmem],
        out_specs=[pl.BlockSpec(memory_space=pl.ANY)] * 2,
        scratch_shapes=[dma((2,))],
        compiler_params=pltpu.CompilerParams(vmem_limit_bytes=2**20),
    )(sol, resid)
    return sol.reshape(shape), resid.reshape(shape)


def solution(mesh):
    sizes = tuple(mesh.shape[a] for a in AXES)
    return jax.shard_map(
        functools.partial(body, sizes),
        mesh=mesh,
        in_specs=(
            P("ta", "gz", "xy", None, None, None),
            P("ta", "gz", "xy", None, None, None, None),
            P("ta", "gz", "xy", None, None, None),
            P("ta", "gz", "xy", None),
            P("xy", None),
        ),
        out_specs=(P("ta", "gz", "xy", None, None, None), P("ta", "gz", "xy", None, None, None)),
        check_vma=False,
    )
```

```python
import functools
import itertools

import jax
import jax.numpy as jnp
from jax import lax
from jax.experimental import pallas as pl
from jax.experimental.pallas import tpu as pltpu
from jax.sharding import PartitionSpec as P

AXES = ("ta", "gz", "xy")
F32 = jnp.float32
BF16 = jnp.bfloat16
MESH = pl.DeviceIdType.MESH


def split(x):
    high = x.astype(BF16)
    return high, (x - high.astype(F32)).astype(BF16)


def dot_nt(a, b):
    return lax.dot_general(a, b, (((1,), (1,)), ((), ())), preferred_element_type=F32)


def dot_nn(a, b):
    return lax.dot_general(a, b, (((1,), (0,)), ((), ())), preferred_element_type=F32)


def stack_split(x):
    return jnp.concatenate(split(x), axis=0)


def fold(o):
    r, n = o.shape[0] // 2, o.shape[1] // 2
    return o[:r, :n] + (o[:r, n:] + o[r:, :n])


def loop(n, step, init, most=8):
    if n <= most:
        for i in range(n):
            init = step(i, init)
        return init
    return lax.fori_loop(0, n, step, init)


def kernel(
    sizes, agg_in, b_in, sten_in, res_in, inv_in, sol_ref, resid_ref,
    agg_ref, b_ref, res_ref, in_sem, sten, sw, rp, halo1, halo2, w1, w2, inv, lab, wr, near, far,
    sten_sem, h1s, h1r, h2s, h2r, ivs, ivr, lbs, lbr, nrs, nrr, frs, frr,
):
    xs, nrhs, comps = b_ref.shape
    k3 = res_ref.shape[1]
    na, _, nc3 = inv.shape
    per = inv_in.shape[0]
    groups = far.shape[1]
    packs = comps // k3
    part = nrhs // packs
    width = xs * comps
    me = tuple(lax.axis_index(a) for a in AXES)

    def at(offset):
        return {a: lax.rem(i + o, n) for a, i, o, n in zip(AXES, me, offset, sizes)}

    def across(bits):
        return {a: (i + 1 - 2 * lax.rem(i, 2)) if f else i for a, i, f in zip(AXES, me, bits)}

    def line(axis, o):
        return tuple(o if a == axis else 0 for a in range(3))

    halo_sends, slots = [], [(), ()]
    for a in range(3):
        for o in (sizes[a] - 1, 1)[: 2 if sizes[a] > 2 else 1]:
            slots[a // 2] += (len(halo_sends),)
            halo_sends.append((len(halo_sends), line(a, o)))
    halo_sends.reverse()
    near_sends = [bits for bits in itertools.product((0, 1), repeat=3) if any(bits)]
    near_sends.sort(key=lambda f: -(f[0] + f[2]))
    far_sends = [
        tuple(2 * o for o in offs)
        for offs in itertools.product(*(range(n // 2) for n in sizes))
        if any(offs)
    ]
    inv_sends = [line(2, o) for o in range(1, sizes[2])]

    barrier = pltpu.get_barrier_semaphore()
    offsets = sorted({o for _, o in halo_sends} | set(far_sends) | set(inv_sends))
    diagonals = [bits for bits in near_sends if sum(bits) > 1]
    offsets.sort(key=lambda o: o not in [h for _, h in halo_sends])
    for device in [at(o) for o in offsets] + [across(f) for f in diagonals]:
        pl.semaphore_signal(barrier, inc=1, device_id=device, device_id_type=MESH)

    mine = inv.at[pl.ds(me[2] * per, per)]
    loads = [
        pltpu.make_async_copy(src, dst, in_sem.at[i])
        for i, (src, dst) in enumerate(
            ((b_in, b_ref), (agg_in, agg_ref), (res_in, res_ref), (inv_in, mine))
        )
    ]
    copies = [
        pltpu.make_async_copy(sten_in.at[x], sten.at[x], sten_sem.at[x]) for x in range(xs)
    ]
    for c in loads + copies:
        c.start()

    pl.semaphore_wait(barrier, len(offsets) + len(diagonals))

    def remote(src, dst, send, recv, device):
        return pltpu.make_async_remote_copy(
            src_ref=src, dst_ref=dst, send_sem=send, recv_sem=recv,
            device_id=device, device_id_type=MESH,
        )

    def arrived(ref, sem):
        pltpu.make_async_copy(ref, ref, sem).wait()

    def start_halo(src, halo, send, recv):
        for s, o in halo_sends:
            side = 1 if s in slots[1] else 0
            remote(src, halo.at[s], send.at[0], recv.at[side], at(o)).start()

    start_halo(b_in, halo1, h1s, h1r)

    for c in loads:
        c.wait()
    lab[0] = jnp.full(lab.shape[1:], agg_ref[0].astype(F32), F32)
    for x in range(xs):
        high, low = split(jnp.transpose(jnp.concatenate([res_ref[x]] * packs, axis=0)))
        rp[pl.ds(x * comps, comps), pl.ds(0, comps)] = high
        rp[pl.ds(x * comps, comps), pl.ds(comps, comps)] = low
    early = [
        remote(lab.at[0], lab.at[i + 1], lbs.at[i], lbr.at[i], at(o))
        for i, o in enumerate(far_sends)
    ]
    for c in early:
        c.start()

    inside = ((0,), (7, 8)) if xs == 2 else ((0,), (7,), (8,))
    sides = [(), ()]
    for a in range(3):
        pair = ((1 + 2 * a,), (2 + 2 * a,))
        sides[a // 2] += pair if sizes[a] > 2 else (pair[0] + pair[1],)

    for x in range(xs):
        copies[x].wait()
        for i, ks in enumerate(inside + sides[0] + sides[1]):
            high, low = split(jnp.transpose(sum(sten[x, k] for k in ks)))
            rows = pl.ds(i * comps, comps)
            sw[x, rows, pl.ds(0, comps)] = high
            sw[x, rows, pl.ds(comps, comps)] = low

    def multiply(x, fields, begin):
        lhs = stack_split(jnp.concatenate(fields, axis=1))
        return dot_nn(lhs, sw[x, pl.ds(begin * comps, len(fields) * comps), :])

    def local_part(field):
        out = []
        for x in range(xs):
            fields = [field[x], field[(x + 1) % xs]]
            if xs > 2:
                fields.append(field[(x + xs - 1) % xs])
            out.append(multiply(x, fields, 0))
        return out

    def halo_part(halo, base, recv):
        for group in range(2):
            arrived(halo.at[pl.ds(slots[group][0], len(slots[group]))], recv.at[group])
            begin = len(inside) + (len(sides[0]) if group else 0)
            base = [
                base[x] + multiply(x, [halo[i, x] for i in slots[group]], begin)
                for x in range(xs)
            ]
        return [fold(o) for o in base]

    lane = lax.broadcasted_iota(jnp.int32, (part, comps), 1)
    slot = lane // k3

    def pack(full):
        out = full[:part]
        for q in range(1, packs):
            out = jnp.where(slot == q, full[q * part : (q + 1) * part], out)
        return out

    def restricted(field):
        return pack(fold(dot_nn(stack_split(jnp.concatenate(field, axis=1)), rp[...])))

    def products(*pairs):
        rows = [sum(u[x] * v[x] for x in range(xs)) for u, v in pairs]
        if len(rows) < packs:
            rows.append(jnp.zeros(((packs - len(rows)) * nrhs, comps), F32))
        return jnp.sum(jnp.transpose(jnp.concatenate(rows, axis=0)), axis=0, keepdims=True)

    def to_near(i, count):
        here = pl.ds(0, count)
        for j, f in enumerate(near_sends):
            remote(
                near.at[i, 0, here], near.at[i, j + 1, here], nrs.at[i], nrr.at[i], across(f)
            ).start()

    def near_slots(i, count):
        return near.at[i, pl.ds(1, len(near_sends)), pl.ds(0, count)]

    def far_slots(i, count):
        return far.at[i, pl.ds(1, len(far_sends)), pl.ds(0, count)]

    def to_far(i, count):
        here = pl.ds(0, count)
        arrived(near_slots(i, count), nrr.at[i])
        total = near[i, 0, here]
        for j in range(len(near_sends)):
            total = total + near[i, j + 1, here]
        far[i, 0, here] = total
        for j, o in enumerate(far_sends):
            remote(
                far.at[i, 0, here], far.at[i, j + 1, here], frs.at[i], frr.at[i], at(o)
            ).start()

    bs = [b_ref[x] for x in range(xs)]
    base = local_part(bs)
    near[0, 0, pl.ds(0, part)] = restricted(bs)
    w1s = halo_part(halo1, base, h1r)
    for x in range(xs):
        w1[x] = w1s[x]
    start_halo(w1, halo2, h2s, h2r)

    base = local_part(w1s)
    near[0, 0, pl.ds(part, part)] = restricted(w1s)
    near[0, 0, pl.ds(2 * part, 1)] = products((w1s, w1s), (w1s, bs))
    to_near(0, 2 * part + 1)
    w2s = halo_part(halo2, base, h2r)
    near[1, 0, pl.ds(0, part)] = restricted(w2s)
    near[1, 0, pl.ds(part, 1)] = products((w1s, w2s), (w2s, w2s), (w2s, bs))
    to_near(1, part + 1)
    gather = [
        remote(mine, mine, ivs.at[i], ivr.at[i], at(o)) for i, o in enumerate(inv_sends)
    ]
    for c in gather:
        c.start()
    for x in range(xs):
        w2[x] = w2s[x]
    to_far(0, 2 * part + 1)

    pair = 2 if groups % 2 == 0 else 1

    def unpack(packed):
        return jnp.concatenate([jnp.where(slot == q, packed, 0.0) for q in range(packs)], axis=0)

    def lift(i, count):
        def lift_step(h, acc):
            lhs = jnp.concatenate(
                [
                    jnp.concatenate(
                        [
                            unpack(far[i, h * pair + j, pl.ds(f * part, part)])
                            for f in range(count)
                        ],
                        axis=0,
                    )
                    for j in range(pair)
                ],
                axis=1,
            )
            rows = pair * comps
            first_row = h * rows if isinstance(h, int) else pl.multiple_of(h * rows, rows)
            return acc + dot_nn(stack_split(lhs), wr[pl.ds(first_row, rows), :])

        zero = jnp.zeros((2 * count * nrhs, 2 * width), F32)
        return fold(loop(groups // pair, lift_step, zero))

    to_far(1, part + 1)
    for c in early + gather:
        c.wait_recv()

    own = inv[agg_ref[0]]
    own_high, own_low = split(own)
    rows = lax.broadcasted_iota(jnp.int32, (comps, nc3), 0)
    cols = lax.broadcasted_iota(jnp.int32, (comps, nc3), 1)
    same = lax.rem(rows, k3) == lax.rem(cols, k3)
    block = (cols // k3).astype(F32)
    vec_high, vec_low = split(jnp.concatenate([res_ref[x] for x in range(xs)], axis=1))

    def prepare(g, carry):
        label = lab[g][0:1, 0:1]
        pick = jnp.where(same & (block == label), 1.0, 0.0).astype(BF16)
        weights = dot_nt(pick, own_high) + dot_nt(pick, own_low)
        high, low = split(weights)
        lift = dot_nn(high, vec_high) + (dot_nn(high, vec_low) + dot_nn(low, vec_high))
        high, low = split(lift)
        first_row = g * comps if isinstance(g, int) else pl.multiple_of(g * comps, comps)
        wr[pl.ds(first_row, comps), pl.ds(0, width)] = high
        wr[pl.ds(first_row, comps), pl.ds(width, width)] = low
        return carry

    loop(groups, prepare, 0)

    for c in early + gather:
        c.wait_send()
    every = pl.ds(0, len(halo_sends))
    for halo, sem in ((halo1, h1s), (halo2, h2s)):
        arrived(halo.at[every], sem.at[0])
    rows_of = (2 * part + 1, part + 1)
    for i in range(2):
        arrived(near_slots(i, rows_of[i]), nrs.at[i])
    arrived(far_slots(0, rows_of[0]), frr.at[0])
    lift_early = lift(0, 2)
    for i in range(2):
        arrived(far_slots(i, rows_of[i]), frs.at[i])
    arrived(far_slots(1, rows_of[1]), frr.at[1])
    lift_late = lift(1, 1)

    def add(g, acc):
        return acc[0] + far[0, g, pl.ds(2 * part, 1)], acc[1] + far[1, g, pl.ds(part, 1)]

    blank = jnp.zeros((1, comps), F32)
    square, corr = loop(groups, add, (blank, blank))
    cross = pltpu.roll(square, comps - nrhs, 1)
    square2 = pltpu.roll(corr, comps - nrhs, 1)
    cross2 = pltpu.roll(corr, comps - 2 * nrhs, 1)
    step = cross / square
    ratio = corr / square
    turn = (step * corr - cross2) / (square2 - ratio * corr)
    push = step + turn * ratio

    own_lane = lax.broadcasted_iota(jnp.int32, (nrhs, comps), 0) == lax.broadcasted_iota(
        jnp.int32, (nrhs, comps), 1
    )

    def spread(coef):
        column = jnp.where(own_lane, jnp.broadcast_to(coef, (nrhs, comps)), 0.0)
        return jnp.broadcast_to(jnp.sum(column, axis=1, keepdims=True), (nrhs, comps))

    push, turn = spread(push), spread(turn)
    for x in range(xs):
        cols = slice(x * comps, (x + 1) * comps)
        bx, ux, vx = b_ref[x], w1[x], w2[x]
        resid_ref[x] = bx - push * ux + turn * vx
        sol_ref[x] = (
            (push * bx - turn * ux)
            + lift_early[:nrhs, cols]
            - push * lift_early[nrhs:, cols]
            + turn * lift_late[:, cols]
        )


def finish(sol_ref, resid_ref, sol_out, resid_out, sem):
    out = [
        pltpu.make_async_copy(src, dst, sem.at[i])
        for i, (src, dst) in enumerate(((sol_ref, sol_out), (resid_ref, resid_out)))
    ]
    for c in out:
        c.start()
    for c in out:
        c.wait()


def body(sizes, right_side, stencil, restrict, aggregate, coarsest_inverse):
    shape = right_side.shape
    xs, nrhs, comps = shape[3:]
    k3 = restrict.shape[4]
    nc3 = coarsest_inverse.shape[1]
    na = nc3 // k3
    groups = (sizes[0] // 2) * (sizes[1] // 2) * (sizes[2] // 2)
    per = coarsest_inverse.shape[0] // k3
    part = nrhs * k3 // comps
    blocks = 9 - (xs == 2) - sum(n == 2 for n in sizes)
    vmem = pl.BlockSpec(memory_space=pltpu.VMEM)
    dma = pltpu.SemaphoreType.DMA
    field = jax.ShapeDtypeStruct((xs, nrhs, comps), F32)
    sol, resid = pl.pallas_call(
        functools.partial(kernel, sizes),
        out_shape=(field, field),
        in_specs=[pl.BlockSpec(memory_space=pltpu.HBM)] * 5,
        out_specs=(vmem, vmem),
        scratch_shapes=[
            pltpu.SMEM((xs,), jnp.int32),
            pltpu.VMEM((xs, nrhs, comps), F32),
            pltpu.VMEM((xs, k3, comps), F32),
            dma((4,)),
            pltpu.VMEM((xs, 9, comps, comps), F32),
            pltpu.VMEM((xs, blocks * comps, 2 * comps), BF16),
            pltpu.VMEM((xs * comps, 2 * comps), BF16),
            pltpu.VMEM((6, xs, nrhs, comps), F32),
            pltpu.VMEM((6, xs, nrhs, comps), F32),
            pltpu.VMEM((xs, nrhs, comps), F32),
            pltpu.VMEM((xs, nrhs, comps), F32),
            pltpu.VMEM((na, k3, nc3), F32),
            pltpu.VMEM((groups, 8, comps), F32),
            pltpu.VMEM((groups * comps, 2 * xs * comps), BF16),
            pltpu.VMEM((2, 8, 3 * part, comps), F32),
            pltpu.VMEM((2, groups, 3 * part, comps), F32),
            dma((xs,)),
            dma((1,)), dma((2,)), dma((1,)), dma((2,)),
            dma((sizes[2],)), dma((sizes[2],)),
            dma((groups,)), dma((groups,)),
            dma((2,)), dma((2,)), dma((2,)), dma((2,)),
        ],
        compiler_params=pltpu.CompilerParams(
            collective_id=0,
            has_side_effects=True,
            vmem_limit_bytes=(16 if groups <= 8 else 48) * 2**20,
        ),
    )(
        *(
            pltpu.with_memory_space_constraint(a, pltpu.HBM)
            for a in (
                aggregate.reshape(xs),
                right_side.reshape(xs, nrhs, comps),
                stencil.reshape(xs, 9, comps, comps),
                restrict.reshape(xs, k3, comps),
                coarsest_inverse.reshape(per, k3, nc3),
            )
        )
    )
    sol, resid = pl.pallas_call(
        finish,
        out_shape=(field, field),
        in_specs=[vmem, vmem],
        out_specs=[pl.BlockSpec(memory_space=pl.ANY)] * 2,
        scratch_shapes=[dma((2,))],
        compiler_params=pltpu.CompilerParams(vmem_limit_bytes=2**20),
    )(sol, resid)
    return sol.reshape(shape), resid.reshape(shape)


def solution(mesh):
    sizes = tuple(mesh.shape[a] for a in AXES)
    return jax.shard_map(
        functools.partial(body, sizes),
        mesh=mesh,
        in_specs=(
            P("ta", "gz", "xy", None, None, None),
            P("ta", "gz", "xy", None, None, None, None),
            P("ta", "gz", "xy", None, None, None),
            P("ta", "gz", "xy", None),
            P("xy", None),
        ),
        out_specs=(P("ta", "gz", "xy", None, None, None), P("ta", "gz", "xy", None, None, None)),
        check_vma=False,
    )
```

```python
import functools
import itertools

import jax
import jax.numpy as jnp
from jax import lax
from jax.experimental import pallas as pl
from jax.experimental.pallas import tpu as pltpu
from jax.sharding import PartitionSpec as P

AXES = ("ta", "gz", "xy")
F32 = jnp.float32
BF16 = jnp.bfloat16
MESH = pl.DeviceIdType.MESH


def split(x):
    high = x.astype(BF16)
    return high, (x - high.astype(F32)).astype(BF16)


def dot_nt(a, b):
    return lax.dot_general(a, b, (((1,), (1,)), ((), ())), preferred_element_type=F32)


def dot_nn(a, b):
    return lax.dot_general(a, b, (((1,), (0,)), ((), ())), preferred_element_type=F32)


def stack_split(x):
    return jnp.concatenate(split(x), axis=0)


def fold(o):
    r, n = o.shape[0] // 2, o.shape[1] // 2
    return o[:r, :n] + (o[:r, n:] + o[r:, :n])


def loop(n, step, init, most=8):
    if n <= most:
        for i in range(n):
            init = step(i, init)
        return init
    return lax.fori_loop(0, n, step, init)


def kernel(
    sizes, agg_in, b_in, sten_in, res_in, inv_in, sol_ref, resid_ref,
    agg_ref, b_ref, res_ref, in_sem, sten, sw, rp, halo1, halo2, w1, w2, inv, lab, wr, near, far,
    sten_sem, h1s, h1r, h2s, h2r, ivs, ivr, lbs, lbr, nrs, nrr, frs, frr,
):
    xs, nrhs, comps = b_ref.shape
    k3 = res_ref.shape[1]
    na, _, nc3 = inv.shape
    per = inv_in.shape[0]
    groups = far.shape[1]
    packs = comps // k3
    part = nrhs // packs
    width = xs * comps
    me = tuple(lax.axis_index(a) for a in AXES)

    def at(offset):
        return {a: lax.rem(i + o, n) for a, i, o, n in zip(AXES, me, offset, sizes)}

    def across(bits):
        return {a: (i + 1 - 2 * lax.rem(i, 2)) if f else i for a, i, f in zip(AXES, me, bits)}

    def line(axis, o):
        return tuple(o if a == axis else 0 for a in range(3))

    halo_sends, slots = [], [(), ()]
    for a in range(3):
        for o in (sizes[a] - 1, 1)[: 2 if sizes[a] > 2 else 1]:
            slots[a // 2] += (len(halo_sends),)
            halo_sends.append((len(halo_sends), line(a, o)))
    halo_sends.reverse()
    near_sends = [bits for bits in itertools.product((0, 1), repeat=3) if any(bits)]
    near_sends.sort(key=lambda f: -(f[0] + f[2]))
    far_sends = [
        tuple(2 * o for o in offs)
        for offs in itertools.product(*(range(n // 2) for n in sizes))
        if any(offs)
    ]
    inv_sends = [line(2, o) for o in range(1, sizes[2])]

    barrier = pltpu.get_barrier_semaphore()
    offsets = sorted({o for _, o in halo_sends} | set(far_sends) | set(inv_sends))
    diagonals = [bits for bits in near_sends if sum(bits) > 1]
    offsets.sort(key=lambda o: o not in [h for _, h in halo_sends])
    for device in [at(o) for o in offsets] + [across(f) for f in diagonals]:
        pl.semaphore_signal(barrier, inc=1, device_id=device, device_id_type=MESH)

    mine = inv.at[pl.ds(me[2] * per, per)]
    loads = [
        pltpu.make_async_copy(src, dst, in_sem.at[i])
        for i, (src, dst) in enumerate(
            ((b_in, b_ref), (agg_in, agg_ref), (res_in, res_ref), (inv_in, mine))
        )
    ]
    copies = [
        pltpu.make_async_copy(sten_in.at[x], sten.at[x], sten_sem.at[x]) for x in range(xs)
    ]
    for c in loads + copies:
        c.start()

    pl.semaphore_wait(barrier, len(offsets) + len(diagonals))

    def remote(src, dst, send, recv, device):
        return pltpu.make_async_remote_copy(
            src_ref=src, dst_ref=dst, send_sem=send, recv_sem=recv,
            device_id=device, device_id_type=MESH,
        )

    def arrived(ref, sem):
        pltpu.make_async_copy(ref, ref, sem).wait()

    def start_halo(src, halo, send, recv):
        for s, o in halo_sends:
            side = 1 if s in slots[1] else 0
            remote(src, halo.at[s], send.at[0], recv.at[side], at(o)).start()

    start_halo(b_in, halo1, h1s, h1r)

    for c in loads:
        c.wait()
    lab[0] = jnp.full(lab.shape[1:], agg_ref[0].astype(F32), F32)
    for x in range(xs):
        high, low = split(jnp.transpose(jnp.concatenate([res_ref[x]] * packs, axis=0)))
        rp[pl.ds(x * comps, comps), pl.ds(0, comps)] = high
        rp[pl.ds(x * comps, comps), pl.ds(comps, comps)] = low
    early = [
        remote(lab.at[0], lab.at[i + 1], lbs.at[i], lbr.at[i], at(o))
        for i, o in enumerate(far_sends)
    ]
    for c in early:
        c.start()

    inside = ((0,), (7, 8)) if xs == 2 else ((0,), (7,), (8,))
    sides = [(), ()]
    for a in range(3):
        pair = ((1 + 2 * a,), (2 + 2 * a,))
        sides[a // 2] += pair if sizes[a] > 2 else (pair[0] + pair[1],)

    for x in range(xs):
        copies[x].wait()
        for i, ks in enumerate(inside + sides[0] + sides[1]):
            high, low = split(jnp.transpose(sum(sten[x, k] for k in ks)))
            rows = pl.ds(i * comps, comps)
            sw[x, rows, pl.ds(0, comps)] = high
            sw[x, rows, pl.ds(comps, comps)] = low

    def multiply(x, fields, begin):
        lhs = stack_split(jnp.concatenate(fields, axis=1))
        return dot_nn(lhs, sw[x, pl.ds(begin * comps, len(fields) * comps), :])

    def local_part(field):
        out = []
        for x in range(xs):
            fields = [field[x], field[(x + 1) % xs]]
            if xs > 2:
                fields.append(field[(x + xs - 1) % xs])
            out.append(multiply(x, fields, 0))
        return out

    def halo_part(halo, base, recv, emit):
        out = []
        for group in range(2):
            arrived(halo.at[pl.ds(slots[group][0], len(slots[group]))], recv.at[group])
            begin = len(inside) + (len(sides[0]) if group else 0)
            for x in range(xs):
                base[x] = base[x] + multiply(x, [halo[i, x] for i in slots[group]], begin)
                if group:
                    out.append(fold(base[x]))
                    emit(x, out[x])
        return out

    lane = lax.broadcasted_iota(jnp.int32, (part, comps), 1)
    slot = lane // k3

    def pack(full):
        out = full[:part]
        for q in range(1, packs):
            out = jnp.where(slot == q, full[q * part : (q + 1) * part], out)
        return out

    def restricted(field):
        return pack(fold(dot_nn(stack_split(jnp.concatenate(field, axis=1)), rp[...])))

    def products(*pairs):
        rows = [sum(u[x] * v[x] for x in range(xs)) for u, v in pairs]
        if len(rows) < packs:
            rows.append(jnp.zeros(((packs - len(rows)) * nrhs, comps), F32))
        return jnp.sum(jnp.transpose(jnp.concatenate(rows, axis=0)), axis=0, keepdims=True)

    def to_near(i, count):
        here = pl.ds(0, count)
        for j, f in enumerate(near_sends):
            remote(
                near.at[i, 0, here], near.at[i, j + 1, here], nrs.at[i], nrr.at[i], across(f)
            ).start()

    def near_slots(i, count):
        return near.at[i, pl.ds(1, len(near_sends)), pl.ds(0, count)]

    def far_slots(i, count):
        return far.at[i, pl.ds(1, len(far_sends)), pl.ds(0, count)]

    def to_far(i, count):
        here = pl.ds(0, count)
        arrived(near_slots(i, count), nrr.at[i])
        total = near[i, 0, here]
        for j in range(len(near_sends)):
            total = total + near[i, j + 1, here]
        far[i, 0, here] = total
        for j, o in enumerate(far_sends):
            remote(
                far.at[i, 0, here], far.at[i, j + 1, here], frs.at[i], frr.at[i], at(o)
            ).start()

    bs = [b_ref[x] for x in range(xs)]
    base = local_part(bs)
    near[0, 0, pl.ds(0, part)] = restricted(bs)
    def emit_first(x, image):
        w1[x] = image
        start_halo(w1.at[x], halo2.at[:, x], h2s, h2r)

    def emit_second(x, image):
        w2[x] = image

    w1s = halo_part(halo1, base, h1r, emit_first)
    base = local_part(w1s)
    near[0, 0, pl.ds(part, part)] = restricted(w1s)
    near[0, 0, pl.ds(2 * part, 1)] = products((w1s, w1s), (w1s, bs))
    to_near(0, 2 * part + 1)
    w2s = halo_part(halo2, base, h2r, emit_second)
    near[1, 0, pl.ds(0, part)] = restricted(w2s)
    near[1, 0, pl.ds(part, 1)] = products((w1s, w2s), (w2s, w2s), (w2s, bs))
    to_near(1, part + 1)
    gather = [
        remote(mine, mine, ivs.at[i], ivr.at[i], at(o)) for i, o in enumerate(inv_sends)
    ]
    for c in gather:
        c.start()
    to_far(0, 2 * part + 1)

    pair = 2 if groups % 2 == 0 else 1

    def unpack(packed):
        return jnp.concatenate([jnp.where(slot == q, packed, 0.0) for q in range(packs)], axis=0)

    def lift(i, count):
        def lift_step(h, acc):
            lhs = jnp.concatenate(
                [
                    jnp.concatenate(
                        [
                            unpack(far[i, h * pair + j, pl.ds(f * part, part)])
                            for f in range(count)
                        ],
                        axis=0,
                    )
                    for j in range(pair)
                ],
                axis=1,
            )
            rows = pair * comps
            first_row = h * rows if isinstance(h, int) else pl.multiple_of(h * rows, rows)
            return acc + dot_nn(stack_split(lhs), wr[pl.ds(first_row, rows), :])

        zero = jnp.zeros((2 * count * nrhs, 2 * width), F32)
        return fold(loop(groups // pair, lift_step, zero))

    to_far(1, part + 1)
    for c in early + gather:
        c.wait_recv()

    own = inv[agg_ref[0]]
    own_high, own_low = split(own)
    rows = lax.broadcasted_iota(jnp.int32, (comps, nc3), 0)
    cols = lax.broadcasted_iota(jnp.int32, (comps, nc3), 1)
    same = lax.rem(rows, k3) == lax.rem(cols, k3)
    block = (cols // k3).astype(F32)
    vec_high, vec_low = split(jnp.concatenate([res_ref[x] for x in range(xs)], axis=1))

    def prepare(g, carry):
        label = lab[g][0:1, 0:1]
        pick = jnp.where(same & (block == label), 1.0, 0.0).astype(BF16)
        weights = dot_nt(pick, own_high) + dot_nt(pick, own_low)
        high, low = split(weights)
        lift = dot_nn(high, vec_high) + (dot_nn(high, vec_low) + dot_nn(low, vec_high))
        high, low = split(lift)
        first_row = g * comps if isinstance(g, int) else pl.multiple_of(g * comps, comps)
        wr[pl.ds(first_row, comps), pl.ds(0, width)] = high
        wr[pl.ds(first_row, comps), pl.ds(width, width)] = low
        return carry

    loop(groups, prepare, 0)

    for c in early + gather:
        c.wait_send()
    every = pl.ds(0, len(halo_sends))
    for halo, sem in ((halo1, h1s), (halo2, h2s)):
        arrived(halo.at[every], sem.at[0])
    rows_of = (2 * part + 1, part + 1)
    for i in range(2):
        arrived(near_slots(i, rows_of[i]), nrs.at[i])
    arrived(far_slots(0, rows_of[0]), frr.at[0])
    lift_early = lift(0, 2)
    for i in range(2):
        arrived(far_slots(i, rows_of[i]), frs.at[i])
    arrived(far_slots(1, rows_of[1]), frr.at[1])
    lift_late = lift(1, 1)

    def add(g, acc):
        return acc[0] + far[0, g, pl.ds(2 * part, 1)], acc[1] + far[1, g, pl.ds(part, 1)]

    blank = jnp.zeros((1, comps), F32)
    square, corr = loop(groups, add, (blank, blank))
    cross = pltpu.roll(square, comps - nrhs, 1)
    square2 = pltpu.roll(corr, comps - nrhs, 1)
    cross2 = pltpu.roll(corr, comps - 2 * nrhs, 1)
    step = cross / square
    ratio = corr / square
    turn = (step * corr - cross2) / (square2 - ratio * corr)
    push = step + turn * ratio

    own_lane = lax.broadcasted_iota(jnp.int32, (nrhs, comps), 0) == lax.broadcasted_iota(
        jnp.int32, (nrhs, comps), 1
    )

    def spread(coef):
        column = jnp.where(own_lane, jnp.broadcast_to(coef, (nrhs, comps)), 0.0)
        return jnp.broadcast_to(jnp.sum(column, axis=1, keepdims=True), (nrhs, comps))

    push, turn = spread(push), spread(turn)
    for x in range(xs):
        cols = slice(x * comps, (x + 1) * comps)
        bx, ux, vx = b_ref[x], w1[x], w2[x]
        resid_ref[x] = bx - push * ux + turn * vx
        sol_ref[x] = (
            (push * bx - turn * ux)
            + lift_early[:nrhs, cols]
            - push * lift_early[nrhs:, cols]
            + turn * lift_late[:, cols]
        )


def finish(sol_ref, resid_ref, sol_out, resid_out, sem):
    out = [
        pltpu.make_async_copy(src, dst, sem.at[i])
        for i, (src, dst) in enumerate(((sol_ref, sol_out), (resid_ref, resid_out)))
    ]
    for c in out:
        c.start()
    for c in out:
        c.wait()


def body(sizes, right_side, stencil, restrict, aggregate, coarsest_inverse):
    shape = right_side.shape
    xs, nrhs, comps = shape[3:]
    k3 = restrict.shape[4]
    nc3 = coarsest_inverse.shape[1]
    na = nc3 // k3
    groups = (sizes[0] // 2) * (sizes[1] // 2) * (sizes[2] // 2)
    per = coarsest_inverse.shape[0] // k3
    part = nrhs * k3 // comps
    blocks = 9 - (xs == 2) - sum(n == 2 for n in sizes)
    vmem = pl.BlockSpec(memory_space=pltpu.VMEM)
    dma = pltpu.SemaphoreType.DMA
    field = jax.ShapeDtypeStruct((xs, nrhs, comps), F32)
    sol, resid = pl.pallas_call(
        functools.partial(kernel, sizes),
        out_shape=(field, field),
        in_specs=[pl.BlockSpec(memory_space=pltpu.HBM)] * 5,
        out_specs=(vmem, vmem),
        scratch_shapes=[
            pltpu.SMEM((xs,), jnp.int32),
            pltpu.VMEM((xs, nrhs, comps), F32),
            pltpu.VMEM((xs, k3, comps), F32),
            dma((4,)),
            pltpu.VMEM((xs, 9, comps, comps), F32),
            pltpu.VMEM((xs, blocks * comps, 2 * comps), BF16),
            pltpu.VMEM((xs * comps, 2 * comps), BF16),
            pltpu.VMEM((6, xs, nrhs, comps), F32),
            pltpu.VMEM((6, xs, nrhs, comps), F32),
            pltpu.VMEM((xs, nrhs, comps), F32),
            pltpu.VMEM((xs, nrhs, comps), F32),
            pltpu.VMEM((na, k3, nc3), F32),
            pltpu.VMEM((groups, 8, comps), F32),
            pltpu.VMEM((groups * comps, 2 * xs * comps), BF16),
            pltpu.VMEM((2, 8, 3 * part, comps), F32),
            pltpu.VMEM((2, groups, 3 * part, comps), F32),
            dma((xs,)),
            dma((1,)), dma((2,)), dma((1,)), dma((2,)),
            dma((sizes[2],)), dma((sizes[2],)),
            dma((groups,)), dma((groups,)),
            dma((2,)), dma((2,)), dma((2,)), dma((2,)),
        ],
        compiler_params=pltpu.CompilerParams(
            collective_id=0,
            has_side_effects=True,
            vmem_limit_bytes=(16 if groups <= 8 else 48) * 2**20,
        ),
    )(
        *(
            pltpu.with_memory_space_constraint(a, pltpu.HBM)
            for a in (
                aggregate.reshape(xs),
                right_side.reshape(xs, nrhs, comps),
                stencil.reshape(xs, 9, comps, comps),
                restrict.reshape(xs, k3, comps),
                coarsest_inverse.reshape(per, k3, nc3),
            )
        )
    )
    sol, resid = pl.pallas_call(
        finish,
        out_shape=(field, field),
        in_specs=[vmem, vmem],
        out_specs=[pl.BlockSpec(memory_space=pl.ANY)] * 2,
        scratch_shapes=[dma((2,))],
        compiler_params=pltpu.CompilerParams(vmem_limit_bytes=2**20),
    )(sol, resid)
    return sol.reshape(shape), resid.reshape(shape)


def solution(mesh):
    sizes = tuple(mesh.shape[a] for a in AXES)
    return jax.shard_map(
        functools.partial(body, sizes),
        mesh=mesh,
        in_specs=(
            P("ta", "gz", "xy", None, None, None),
            P("ta", "gz", "xy", None, None, None, None),
            P("ta", "gz", "xy", None, None, None),
            P("ta", "gz", "xy", None),
            P("xy", None),
        ),
        out_specs=(P("ta", "gz", "xy", None, None, None), P("ta", "gz", "xy", None, None, None)),
        check_vma=False,
    )
```

```python
import functools
import itertools

import jax
import jax.numpy as jnp
from jax import lax
from jax.experimental import pallas as pl
from jax.experimental.pallas import tpu as pltpu
from jax.sharding import PartitionSpec as P

AXES = ("ta", "gz", "xy")
F32 = jnp.float32
BF16 = jnp.bfloat16
MESH = pl.DeviceIdType.MESH


def split(x):
    high = x.astype(BF16)
    return high, (x - high.astype(F32)).astype(BF16)


def dot_nt(a, b):
    return lax.dot_general(a, b, (((1,), (1,)), ((), ())), preferred_element_type=F32)


def dot_nn(a, b):
    return lax.dot_general(a, b, (((1,), (0,)), ((), ())), preferred_element_type=F32)


def stack_split(x):
    return jnp.concatenate(split(x), axis=0)


def fold(o):
    r, n = o.shape[0] // 2, o.shape[1] // 2
    return o[:r, :n] + (o[:r, n:] + o[r:, :n])


def loop(n, step, init, most=8):
    if n <= most:
        for i in range(n):
            init = step(i, init)
        return init
    return lax.fori_loop(0, n, step, init)


def kernel(
    sizes, agg_in, b_in, sten_in, res_in, inv_in, sol_ref, resid_ref,
    agg_ref, b_ref, res_ref, in_sem, sten, sw, rp, halo1, halo2, w1, w2, inv, lab, wr, near, far,
    sten_sem, h1s, h1r, h2s, h2r, ivs, ivr, lbs, lbr, nrs, nrr, frs, frr,
):
    xs, nrhs, comps = b_ref.shape
    k3 = res_ref.shape[1]
    na, _, nc3 = inv.shape
    per = inv_in.shape[0]
    groups = far.shape[1]
    packs = comps // k3
    part = nrhs // packs
    width = xs * comps
    me = tuple(lax.axis_index(a) for a in AXES)

    def at(offset):
        return {a: lax.rem(i + o, n) for a, i, o, n in zip(AXES, me, offset, sizes)}

    def across(bits):
        return {a: (i + 1 - 2 * lax.rem(i, 2)) if f else i for a, i, f in zip(AXES, me, bits)}

    def line(axis, o):
        return tuple(o if a == axis else 0 for a in range(3))

    halo_sends, slots = [], [(), ()]
    for a in range(3):
        for o in (sizes[a] - 1, 1)[: 2 if sizes[a] > 2 else 1]:
            slots[a // 2] += (len(halo_sends),)
            halo_sends.append((len(halo_sends), line(a, o)))
    halo_sends.reverse()
    near_sends = [bits for bits in itertools.product((0, 1), repeat=3) if any(bits)]
    near_sends.sort(key=lambda f: -(f[0] + f[2]))
    far_sends = [
        tuple(2 * o for o in offs)
        for offs in itertools.product(*(range(n // 2) for n in sizes))
        if any(offs)
    ]
    inv_sends = [line(2, o) for o in range(1, sizes[2])]

    barrier = pltpu.get_barrier_semaphore()
    offsets = sorted({o for _, o in halo_sends} | set(far_sends) | set(inv_sends))
    diagonals = [bits for bits in near_sends if sum(bits) > 1]
    offsets.sort(key=lambda o: o not in [h for _, h in halo_sends])
    for device in [at(o) for o in offsets] + [across(f) for f in diagonals]:
        pl.semaphore_signal(barrier, inc=1, device_id=device, device_id_type=MESH)

    mine = inv.at[pl.ds(me[2] * per, per)]
    loads = [
        pltpu.make_async_copy(src, dst, in_sem.at[i])
        for i, (src, dst) in enumerate(
            ((b_in, b_ref), (agg_in, agg_ref), (res_in, res_ref), (inv_in, mine))
        )
    ]
    copies = [
        pltpu.make_async_copy(sten_in.at[x], sten.at[x], sten_sem.at[x]) for x in range(xs)
    ]
    for c in loads + copies:
        c.start()

    pl.semaphore_wait(barrier, len(offsets) + len(diagonals))

    def remote(src, dst, send, recv, device):
        return pltpu.make_async_remote_copy(
            src_ref=src, dst_ref=dst, send_sem=send, recv_sem=recv,
            device_id=device, device_id_type=MESH,
        )

    def arrived(ref, sem):
        pltpu.make_async_copy(ref, ref, sem).wait()

    def start_halo(src, halo, send, recv):
        for s, o in halo_sends:
            side = 1 if s in slots[1] else 0
            remote(src, halo.at[s], send.at[0], recv.at[side], at(o)).start()

    start_halo(b_in, halo1, h1s, h1r)

    for c in loads:
        c.wait()
    lab[0] = jnp.full(lab.shape[1:], agg_ref[0].astype(F32), F32)
    for x in range(xs):
        high, low = split(jnp.transpose(jnp.concatenate([res_ref[x]] * packs, axis=0)))
        rp[pl.ds(x * comps, comps), pl.ds(0, comps)] = high
        rp[pl.ds(x * comps, comps), pl.ds(comps, comps)] = low
    early = [
        remote(lab.at[0], lab.at[i + 1], lbs.at[i], lbr.at[i], at(o))
        for i, o in enumerate(far_sends)
    ]
    for c in early:
        c.start()

    inside = ((0,), (7, 8)) if xs == 2 else ((0,), (7,), (8,))
    sides = [(), ()]
    for a in range(3):
        pair = ((1 + 2 * a,), (2 + 2 * a,))
        sides[a // 2] += pair if sizes[a] > 2 else (pair[0] + pair[1],)

    for x in range(xs):
        copies[x].wait()
        for i, ks in enumerate(inside + sides[0] + sides[1]):
            high, low = split(jnp.transpose(sum(sten[x, k] for k in ks)))
            rows = pl.ds(i * comps, comps)
            sw[x, rows, pl.ds(0, comps)] = high
            sw[x, rows, pl.ds(comps, comps)] = low

    def multiply(x, fields, begin):
        lhs = stack_split(jnp.concatenate(fields, axis=1))
        return dot_nn(lhs, sw[x, pl.ds(begin * comps, len(fields) * comps), :])

    def local_part(field):
        out = []
        for x in range(xs):
            fields = [field[x], field[(x + 1) % xs]]
            if xs > 2:
                fields.append(field[(x + xs - 1) % xs])
            out.append(multiply(x, fields, 0))
        return out

    def halo_part(halo, base, recv, between=lambda: None):
        for group in range(2):
            if group:
                between()
            arrived(halo.at[pl.ds(slots[group][0], len(slots[group]))], recv.at[group])
            begin = len(inside) + (len(sides[0]) if group else 0)
            base = [
                base[x] + multiply(x, [halo[i, x] for i in slots[group]], begin)
                for x in range(xs)
            ]
        return [fold(o) for o in base]

    lane = lax.broadcasted_iota(jnp.int32, (part, comps), 1)
    slot = lane // k3

    def pack(full):
        out = full[:part]
        for q in range(1, packs):
            out = jnp.where(slot == q, full[q * part : (q + 1) * part], out)
        return out

    def restricted(field):
        return pack(fold(dot_nn(stack_split(jnp.concatenate(field, axis=1)), rp[...])))

    def products(*pairs):
        rows = [sum(u[x] * v[x] for x in range(xs)) for u, v in pairs]
        if len(rows) < packs:
            rows.append(jnp.zeros(((packs - len(rows)) * nrhs, comps), F32))
        return jnp.sum(jnp.transpose(jnp.concatenate(rows, axis=0)), axis=0, keepdims=True)

    def to_near(i, count):
        here = pl.ds(0, count)
        for j, f in enumerate(near_sends):
            remote(
                near.at[i, 0, here], near.at[i, j + 1, here], nrs.at[i], nrr.at[i], across(f)
            ).start()

    def near_slots(i, count):
        return near.at[i, pl.ds(1, len(near_sends)), pl.ds(0, count)]

    def far_slots(i, count):
        return far.at[i, pl.ds(1, len(far_sends)), pl.ds(0, count)]

    def to_far(i, count):
        here = pl.ds(0, count)
        arrived(near_slots(i, count), nrr.at[i])
        total = near[i, 0, here]
        for j in range(len(near_sends)):
            total = total + near[i, j + 1, here]
        far[i, 0, here] = total
        for j, o in enumerate(far_sends):
            remote(
                far.at[i, 0, here], far.at[i, j + 1, here], frs.at[i], frr.at[i], at(o)
            ).start()

    bs = [b_ref[x] for x in range(xs)]
    base = local_part(bs)
    near[0, 0, pl.ds(0, part)] = restricted(bs)
    w1s = halo_part(halo1, base, h1r)
    for x in range(xs):
        w1[x] = w1s[x]
    start_halo(w1, halo2, h2s, h2r)

    base = local_part(w1s)
    near[0, 0, pl.ds(part, part)] = restricted(w1s)
    near[0, 0, pl.ds(2 * part, 1)] = products((w1s, w1s), (w1s, bs))
    w2s = halo_part(halo2, base, h2r, lambda: to_near(0, 2 * part + 1))
    near[1, 0, pl.ds(0, part)] = restricted(w2s)
    near[1, 0, pl.ds(part, 1)] = products((w1s, w2s), (w2s, w2s), (w2s, bs))
    to_near(1, part + 1)
    gather = [
        remote(mine, mine, ivs.at[i], ivr.at[i], at(o)) for i, o in enumerate(inv_sends)
    ]
    for c in gather:
        c.start()
    for x in range(xs):
        w2[x] = w2s[x]
    to_far(0, 2 * part + 1)

    pair = 2 if groups % 2 == 0 else 1

    def unpack(packed):
        return jnp.concatenate([jnp.where(slot == q, packed, 0.0) for q in range(packs)], axis=0)

    def lift(i, count):
        def lift_step(h, acc):
            lhs = jnp.concatenate(
                [
                    jnp.concatenate(
                        [
                            unpack(far[i, h * pair + j, pl.ds(f * part, part)])
                            for f in range(count)
                        ],
                        axis=0,
                    )
                    for j in range(pair)
                ],
                axis=1,
            )
            rows = pair * comps
            first_row = h * rows if isinstance(h, int) else pl.multiple_of(h * rows, rows)
            return acc + dot_nn(stack_split(lhs), wr[pl.ds(first_row, rows), :])

        zero = jnp.zeros((2 * count * nrhs, 2 * width), F32)
        return fold(loop(groups // pair, lift_step, zero))

    to_far(1, part + 1)
    for c in early + gather:
        c.wait_recv()

    own = inv[agg_ref[0]]
    own_high, own_low = split(own)
    rows = lax.broadcasted_iota(jnp.int32, (comps, nc3), 0)
    cols = lax.broadcasted_iota(jnp.int32, (comps, nc3), 1)
    same = lax.rem(rows, k3) == lax.rem(cols, k3)
    block = (cols // k3).astype(F32)
    vec_high, vec_low = split(jnp.concatenate([res_ref[x] for x in range(xs)], axis=1))

    def prepare(g, carry):
        label = lab[g][0:1, 0:1]
        pick = jnp.where(same & (block == label), 1.0, 0.0).astype(BF16)
        weights = dot_nt(pick, own_high) + dot_nt(pick, own_low)
        high, low = split(weights)
        lift = dot_nn(high, vec_high) + (dot_nn(high, vec_low) + dot_nn(low, vec_high))
        high, low = split(lift)
        first_row = g * comps if isinstance(g, int) else pl.multiple_of(g * comps, comps)
        wr[pl.ds(first_row, comps), pl.ds(0, width)] = high
        wr[pl.ds(first_row, comps), pl.ds(width, width)] = low
        return carry

    loop(groups, prepare, 0)

    for c in early + gather:
        c.wait_send()
    every = pl.ds(0, len(halo_sends))
    for halo, sem in ((halo1, h1s), (halo2, h2s)):
        arrived(halo.at[every], sem.at[0])
    rows_of = (2 * part + 1, part + 1)
    for i in range(2):
        arrived(near_slots(i, rows_of[i]), nrs.at[i])
    arrived(far_slots(0, rows_of[0]), frr.at[0])
    lift_early = lift(0, 2)
    for i in range(2):
        arrived(far_slots(i, rows_of[i]), frs.at[i])
    arrived(far_slots(1, rows_of[1]), frr.at[1])
    lift_late = lift(1, 1)

    def add(g, acc):
        return acc[0] + far[0, g, pl.ds(2 * part, 1)], acc[1] + far[1, g, pl.ds(part, 1)]

    blank = jnp.zeros((1, comps), F32)
    square, corr = loop(groups, add, (blank, blank))
    cross = pltpu.roll(square, comps - nrhs, 1)
    square2 = pltpu.roll(corr, comps - nrhs, 1)
    cross2 = pltpu.roll(corr, comps - 2 * nrhs, 1)
    step = cross / square
    ratio = corr / square
    turn = (step * corr - cross2) / (square2 - ratio * corr)
    push = step + turn * ratio

    own_lane = lax.broadcasted_iota(jnp.int32, (nrhs, comps), 0) == lax.broadcasted_iota(
        jnp.int32, (nrhs, comps), 1
    )

    def spread(coef):
        column = jnp.where(own_lane, jnp.broadcast_to(coef, (nrhs, comps)), 0.0)
        return jnp.broadcast_to(jnp.sum(column, axis=1, keepdims=True), (nrhs, comps))

    push, turn = spread(push), spread(turn)
    for x in range(xs):
        cols = slice(x * comps, (x + 1) * comps)
        bx, ux, vx = b_ref[x], w1[x], w2[x]
        resid_ref[x] = bx - push * ux + turn * vx
        sol_ref[x] = (
            (push * bx - turn * ux)
            + lift_early[:nrhs, cols]
            - push * lift_early[nrhs:, cols]
            + turn * lift_late[:, cols]
        )


def finish(sol_ref, resid_ref, sol_out, resid_out, sem):
    out = [
        pltpu.make_async_copy(src, dst, sem.at[i])
        for i, (src, dst) in enumerate(((sol_ref, sol_out), (resid_ref, resid_out)))
    ]
    for c in out:
        c.start()
    for c in out:
        c.wait()


def body(sizes, right_side, stencil, restrict, aggregate, coarsest_inverse):
    shape = right_side.shape
    xs, nrhs, comps = shape[3:]
    k3 = restrict.shape[4]
    nc3 = coarsest_inverse.shape[1]
    na = nc3 // k3
    groups = (sizes[0] // 2) * (sizes[1] // 2) * (sizes[2] // 2)
    per = coarsest_inverse.shape[0] // k3
    part = nrhs * k3 // comps
    blocks = 9 - (xs == 2) - sum(n == 2 for n in sizes)
    vmem = pl.BlockSpec(memory_space=pltpu.VMEM)
    dma = pltpu.SemaphoreType.DMA
    field = jax.ShapeDtypeStruct((xs, nrhs, comps), F32)
    sol, resid = pl.pallas_call(
        functools.partial(kernel, sizes),
        out_shape=(field, field),
        in_specs=[pl.BlockSpec(memory_space=pltpu.HBM)] * 5,
        out_specs=(vmem, vmem),
        scratch_shapes=[
            pltpu.SMEM((xs,), jnp.int32),
            pltpu.VMEM((xs, nrhs, comps), F32),
            pltpu.VMEM((xs, k3, comps), F32),
            dma((4,)),
            pltpu.VMEM((xs, 9, comps, comps), F32),
            pltpu.VMEM((xs, blocks * comps, 2 * comps), BF16),
            pltpu.VMEM((xs * comps, 2 * comps), BF16),
            pltpu.VMEM((6, xs, nrhs, comps), F32),
            pltpu.VMEM((6, xs, nrhs, comps), F32),
            pltpu.VMEM((xs, nrhs, comps), F32),
            pltpu.VMEM((xs, nrhs, comps), F32),
            pltpu.VMEM((na, k3, nc3), F32),
            pltpu.VMEM((groups, 8, comps), F32),
            pltpu.VMEM((groups * comps, 2 * xs * comps), BF16),
            pltpu.VMEM((2, 8, 3 * part, comps), F32),
            pltpu.VMEM((2, groups, 3 * part, comps), F32),
            dma((xs,)),
            dma((1,)), dma((2,)), dma((1,)), dma((2,)),
            dma((sizes[2],)), dma((sizes[2],)),
            dma((groups,)), dma((groups,)),
            dma((2,)), dma((2,)), dma((2,)), dma((2,)),
        ],
        compiler_params=pltpu.CompilerParams(
            collective_id=0,
            has_side_effects=True,
            vmem_limit_bytes=(16 if groups <= 8 else 48) * 2**20,
        ),
    )(
        *(
            pltpu.with_memory_space_constraint(a, pltpu.HBM)
            for a in (
                aggregate.reshape(xs),
                right_side.reshape(xs, nrhs, comps),
                stencil.reshape(xs, 9, comps, comps),
                restrict.reshape(xs, k3, comps),
                coarsest_inverse.reshape(per, k3, nc3),
            )
        )
    )
    sol, resid = pl.pallas_call(
        finish,
        out_shape=(field, field),
        in_specs=[vmem, vmem],
        out_specs=[pl.BlockSpec(memory_space=pl.ANY)] * 2,
        scratch_shapes=[dma((2,))],
        compiler_params=pltpu.CompilerParams(vmem_limit_bytes=2**20),
    )(sol, resid)
    return sol.reshape(shape), resid.reshape(shape)


def solution(mesh):
    sizes = tuple(mesh.shape[a] for a in AXES)
    return jax.shard_map(
        functools.partial(body, sizes),
        mesh=mesh,
        in_specs=(
            P("ta", "gz", "xy", None, None, None),
            P("ta", "gz", "xy", None, None, None, None),
            P("ta", "gz", "xy", None, None, None),
            P("ta", "gz", "xy", None),
            P("xy", None),
        ),
        out_specs=(P("ta", "gz", "xy", None, None, None), P("ta", "gz", "xy", None, None, None)),
        check_vma=False,
    )
```
